128 devices in a mesh: grp: 8 (over y_lo, x), tp: 16 (over z, y_hi, core).
Axes of the slice: x: 4, y: 4 (y_hi: 2, y_lo: 2; y = y_hi * 2 + y_lo), z: 4, core: 2. Of those that a mesh axis runs over, the one named last changes fastest.
Arguments:
- queries: bfloat16 [8, 2048, 8192], P('grp', None, 'tp'), may hold values from -400 to 400
- keys_values: bfloat16 [8, 2048, 2048], P('grp', 'tp'), may hold values from -6 to 6
- projector: bfloat16 [8192, 1024], P('tp'), may hold values from -1 to 1
- ownership: int32 [8], replicated, may hold values from 0 to 7, each once
- token_ids: int32 [16384], P(('grp', 'tp')), may hold values from 150143 to 152142
- student_input: bfloat16 [16384, 3584], P(('grp', 'tp')), may hold values from -24 to 24
- student_weight: bfloat16 [3584, 1024], P(('grp', 'tp')), may hold values from -0.09375 to 0.09375
- student_bias: bfloat16 [1024], P(('grp', 'tp')), may hold values from -3 to 3
Outputs:
- loss_value: float32 [], replicated
- weight_grad: float32 [3584, 1024], P(('grp', 'tp'))
- bias_grad: float32 [1024], P(('grp', 'tp'))
- input_grad: bfloat16 [16384, 3584], P(('grp', 'tp'))
The draws below stay inside these ranges and needn't reach their ends.
Inputs may be any that keep to these rules, and one draw needn't show every extreme that they name: `ownership`: each number once.
All inputs are finite; a program needn't handle non-finite values.
Results may differ from the reference program's by a relative error of at most 0.019.
Values may be sent and summed in bfloat16 or wider, within the bound.
A program may use at most 128 MiB of HBM per device.

```python
import math
import jax
import jax.numpy as jnp
from jax import lax

HEADS = 64
KV_HEADS = 8
HEAD_DIM = 128
STUDENT_WIDTH = 3584
TEXT_IDS = 151643
SEQUENCES = 8
SEQ_LEN = 2048
PIECE = 16
TEACHER_WIDTH = 8192
STUDENT_KV = 1024
STUDENT_ROWS = 16384
N_TP = 16


def shared_keys(key):
    return jnp.clip(jax.random.normal(key, (SEQUENCES, SEQ_LEN, KV_HEADS * HEAD_DIM), jnp.float32), -6.0, 6.0)


def draw_queries(key, part):
    key = jax.random.fold_in(key, 7)
    first_key = jax.random.fold_in(key, 0)
    base_values = jnp.clip(jax.random.normal(first_key, (SEQUENCES, SEQ_LEN, HEADS, HEAD_DIM), jnp.float32), -6.0, 6.0)
    return base_values.reshape(SEQUENCES, SEQ_LEN, HEADS * HEAD_DIM).astype(jnp.bfloat16)


def draw_keys_values(key, part):
    keys_part = shared_keys(key)
    key = jax.random.fold_in(key, 11)
    values_part = jnp.clip(jax.random.normal(key, keys_part.shape, jnp.float32), -6.0, 6.0)
    return jnp.concatenate([keys_part, values_part], axis=2).astype(jnp.bfloat16)


def draw_student_input(key, part):
    key = jax.random.fold_in(key, 5)
    first_key, second_key = jax.random.split(key)
    row_share = jnp.arange(STUDENT_ROWS, dtype=jnp.float32) / STUDENT_ROWS
    spread = jnp.exp(jax.random.uniform(second_key, (STUDENT_ROWS, 1), jnp.float32, 0.0, math.log(10.0)))
    base_values = jnp.clip(jax.random.normal(first_key, (STUDENT_ROWS, STUDENT_WIDTH), jnp.float32), -6.0, 6.0)
    rise_factor = 3.0 ** row_share
    return (base_values * spread * rise_factor[:, None] / 8.0).astype(jnp.bfloat16)


def set_ends(result, own_key, smallest, largest):
    place = [jax.random.randint(jax.random.fold_in(own_key, axis), (), 0, length) for axis, length in enumerate(result.shape)]
    widest = result.shape.index(max(result.shape))
    next_to = place[:widest] + [(place[widest] + 1) % result.shape[widest]] + place[widest + 1:]
    return result.at[tuple(place)].set(smallest).at[tuple(next_to)].set(largest)


def level_of(key, shape, shards, least, largest):
    factor_of = 1.0
    for dim, shards_of in shards:
        steps = jax.random.uniform(jax.random.fold_in(jax.random.fold_in(key, 6), dim), (shards_of,), jnp.float32, least / len(shards), largest / len(shards))
        factor_of = factor_of * jnp.repeat(jnp.exp(steps), shape[dim] // shards_of).reshape((-1,) + (1,) * (len(shape) - 1 - dim))
    return factor_of


def normal_values(key, dims, scale, reach, pieces=(), kind=jnp.bfloat16):
    gain = level_of(key, dims, pieces, -0.22, 0.18) if pieces else 1.0
    result = jax.random.normal(key, dims, jnp.float32) * scale * gain
    return jnp.minimum(jnp.maximum(result, -reach), reach).astype(kind)


def setup_inputs(seed: int = 0) -> dict:
    streams_of = jax.random.split(jax.random.key(seed), 9)
    return {
        "queries": draw_queries(jax.random.fold_in(streams_of[8], 71), 0),
        "keys_values": draw_keys_values(jax.random.fold_in(streams_of[8], 71), 0),
        "projector": normal_values(streams_of[2], (TEACHER_WIDTH, STUDENT_KV), (TEACHER_WIDTH // 256) ** -0.5, 1.0, ((0, 16),)),
        "ownership": jax.random.permutation(streams_of[3], SEQUENCES).astype(jnp.int32),
        "token_ids": set_ends(jax.random.randint(streams_of[4], (STUDENT_ROWS,), TEXT_IDS - 1500, TEXT_IDS + 500), jax.random.fold_in(streams_of[4], 1), TEXT_IDS - 1500, (TEXT_IDS + 500) - 1).astype(jnp.int32),
        "student_input": draw_student_input(jax.random.fold_in(streams_of[8], 71), 0),
        "student_weight": normal_values(streams_of[6], (STUDENT_WIDTH, STUDENT_KV), STUDENT_WIDTH ** -0.5, 0.09375, ((0, 128),)),
        "student_bias": normal_values(streams_of[7], (STUDENT_KV,), 0.5, 3.0, ((0, 128),)),
    }


def attend_sequence(inputs):
    query_part, stacked_part = inputs
    key_rows = stacked_part[:, :KV_HEADS * HEAD_DIM].reshape(SEQ_LEN, KV_HEADS, HEAD_DIM)
    value_rows = stacked_part[:, KV_HEADS * HEAD_DIM:].reshape(SEQ_LEN, KV_HEADS, HEAD_DIM)
    query_rows = query_part.reshape(SEQ_LEN, HEADS, HEAD_DIM)
    per_group = HEADS // KV_HEADS
    position = jnp.arange(SEQ_LEN, dtype=jnp.int32)
    causal = position[:, None] >= position[None, :]

    def one_head(head_index):
        query_head = lax.dynamic_index_in_dim(query_rows, head_index, 1, keepdims=False)
        group_index = head_index // per_group
        key_head = lax.dynamic_index_in_dim(key_rows, group_index, 1, keepdims=False)
        value_head = lax.dynamic_index_in_dim(value_rows, group_index, 1, keepdims=False)
        scores = jnp.dot(query_head, key_head.T, preferred_element_type=jnp.float32) * (HEAD_DIM ** -0.5)
        scores = jnp.where(causal, scores, -1e30)
        row_peak = jnp.max(scores, axis=1, keepdims=True)
        weights = jnp.exp(scores - row_peak)
        prob_rows = (weights / jnp.sum(weights, axis=1, keepdims=True)).astype(jnp.bfloat16)
        return jnp.dot(prob_rows, value_head, preferred_element_type=jnp.float32).astype(jnp.bfloat16)

    outputs = lax.map(one_head, jnp.arange(HEADS, dtype=jnp.int32))
    return jnp.transpose(outputs, (1, 0, 2)).reshape(SEQ_LEN, HEADS * HEAD_DIM)


def reference(queries, keys_values, projector, ownership, token_ids, student_input, student_weight, student_bias):
    attention = lax.map(attend_sequence, (queries, keys_values))

    def project(sequence_rows):
        return jnp.dot(sequence_rows, projector, preferred_element_type=jnp.float32).astype(jnp.bfloat16)

    target = lax.map(project, attention)
    arranged = target.reshape(SEQUENCES, N_TP, SEQUENCES, PIECE, STUDENT_KV)
    chosen = jnp.take(arranged, ownership, axis=0)
    paired = jnp.transpose(chosen, (2, 1, 0, 3, 4)).reshape(STUDENT_ROWS, STUDENT_KV)
    keep_mask = (token_ids < TEXT_IDS).astype(jnp.float32)[:, None]
    output = jnp.dot(student_input, student_weight, preferred_element_type=jnp.float32) + student_bias.astype(jnp.float32)
    residual = keep_mask * (output - paired.astype(jnp.float32))
    loss_value = jnp.sum(residual * residual) / (2.0 * STUDENT_ROWS)
    error_rows = residual.astype(jnp.bfloat16)
    weight_grad = lax.dot_general(student_input, error_rows, (((0,), (0,)), ((), ())), preferred_element_type=jnp.float32)
    bias_grad = jnp.sum(error_rows.astype(jnp.float32), axis=0)
    input_grad = lax.dot_general(error_rows, student_weight, (((1,), (1,)), ((), ())), preferred_element_type=jnp.float32).astype(jnp.bfloat16)
    return (loss_value, weight_grad, bias_grad, input_grad)
```

```python
import functools

import jax
import jax.numpy as jnp
from jax import lax
from jax.experimental import pallas as pl
from jax.experimental.pallas import tpu as pltpu
from jax.sharding import PartitionSpec as P

MESH = pl.DeviceIdType.MESH
TEXT_IDS = 151643
SCALE = 128 ** -0.5 * 1.4426950408889634
BF = jnp.bfloat16
F32 = jnp.float32


def rcopy(src, dst, send_sem, recv_sem, grp, tp):
    return pltpu.make_async_remote_copy(
        src_ref=src, dst_ref=dst, send_sem=send_sem, recv_sem=recv_sem,
        device_id=(grp, tp), device_id_type=MESH)


def loop(first, last, body):
    lax.fori_loop(first, last, lambda i, carry: (body(i), carry)[1], 0)


def attend(core, c, qo, qs, keys, values, S, mx, acc, out):
    T = 256

    def score(j, masked):
        at = pl.ds(pl.multiple_of(j * T, T), T)
        kt = keys[at, :]
        if masked:
            row = lax.broadcasted_iota(jnp.int32, (128, T), 0) + core * 128
            keep = row >= lax.broadcasted_iota(jnp.int32, (128, T), 1)
        for h in range(8):
            hr = slice(h * 128, (h + 1) * 128)
            q = (qo if h < 4 else qs)[:, (h % 4) * 128:(h % 4) * 128 + 128]
            s = lax.dot_general(q, kt, (((1,), (1,)), ((), ())), preferred_element_type=F32)
            if masked:
                s = jnp.where(keep, s, -1e30)
            S[hr, at] = s
            m = jnp.maximum(mx[hr, :], jnp.maximum(s[:, :128], s[:, 128:]))
            if masked:
                m = jnp.broadcast_to(jnp.max(m, axis=1, keepdims=True) * SCALE, (128, 128))
            mx[hr, :] = m

    mx[...] = jnp.full_like(mx, -1e30)
    loop(0, c, lambda j: score(j, False))
    score(c, True)
    acc[...] = jnp.zeros_like(acc)

    def weigh(off, W):
        vt = values[pl.ds(off, W), :]
        vt = jnp.concatenate([vt, jnp.ones_like(vt)], axis=1)
        for h in range(8):
            hr = slice(h * 128, (h + 1) * 128)
            m = mx[hr, :]
            ps = []
            for w in range(W // 128):
                s = S[hr, pl.ds(pl.multiple_of(off + w * 128, 128), 128)]
                ps.append(jnp.exp2(s * SCALE - m).astype(BF))
            acc[hr, :] += jnp.dot(jnp.concatenate(ps, axis=1), vt, preferred_element_type=F32)

    n = c + 1
    loop(0, n // 2, lambda j: weigh(pl.multiple_of(j * 512, 512), 512))
    loop(0, n % 2, lambda j: weigh(pl.multiple_of((n - 1) * 256, 256), 256))
    for h in range(8):
        a = acc[h * 128:(h + 1) * 128, :]
        out[:, h * 128:(h + 1) * 128] = (a[:, :128] / a[:, 128:]).astype(BF)


def kernel(q_in, kv_in, proj_in, own_in, ids_in, x_in, w_in,
           wg_out, small_out, ig_out,
           qo, qs, keys, values, S, mx, acc, att, proj_o, proj_s, tsend, tland, tsum, pland,
           xland, xt, wland, wz, brow, osend, oland, eland, wg, wsend, wgland, igsend, igland,
           l_sem, qp_s, qp_r, k_s, k_r, v_s, v_r, rk_s, rv_s, w_s, w_r, x_s, x_r, o_s, o_r,
           t_s, t_r, p_s, p_r, e_s, e_r, re_s, g_s, g_r, i_s, i_r):
    g = lax.axis_index("grp")
    t = lax.axis_index("tp")
    x, yl = lax.rem(g, 4), g // 4
    core, chip = lax.rem(t, 2), t // 2
    sib = chip * 2 + 1 - core
    m = core * 4 + x
    src16 = chip * 2 + yl

    def member(i):
        return yl * 4 + lax.rem(i, 4), chip * 2 + i // 4

    def plane(i):
        return lax.rem(i, 2) * 4 + x, (i // 2) * 2 + yl

    own_kv = pl.ds(pl.multiple_of(t * 128, 128), 128)
    kcol = pl.ds(pl.multiple_of(chip * 128, 128), 128)
    vcol = pl.ds(pl.multiple_of(1024 + chip * 128, 128), 128)

    def window(i):
        return pl.ds(pl.multiple_of((i // 2) * 896 + lax.rem(i, 2) * 384, 128), 512)

    local = [
        pltpu.make_async_copy(kv_in.at[:, kcol], keys.at[own_kv, :], l_sem.at[0]),
        pltpu.make_async_copy(kv_in.at[:, vcol], values.at[own_kv, :], l_sem.at[1]),
        pltpu.make_async_copy(q_in.at[:, core], qo, l_sem.at[2]),
        pltpu.make_async_copy(proj_in, proj_o, l_sem.at[3]),
        pltpu.make_async_copy(x_in.at[:, window(m)], xland.at[m], l_sem.at[4]),
    ]
    for copy in local:
        copy.start()

    barrier = pltpu.get_barrier_semaphore()

    def greet(grp, tp):
        pl.semaphore_signal(barrier, inc=1, device_id=(grp, tp), device_id_type=MESH)

    def greet_plane(i):
        j = lax.rem(yl * 16 + t + i, 32)
        greet((j // 16) * 4 + x, lax.rem(j, 16))

    loop(1, 32, greet_plane)

    def greet_x(i):
        xx = lax.rem(x + i, 4)
        greet(yl * 4 + xx, t)
        greet(yl * 4 + xx, sib)
        greet((1 - yl) * 4 + xx, t)

    loop(1, 4, greet_x)
    pl.semaphore_wait(barrier, 31 + 9)

    def kv_cols(q):
        return (pl.ds(pl.multiple_of(q * 128, 128), 128),
                pl.ds(pl.multiple_of(1024 + q * 128, 128), 128))

    def kv_send(i, start):
        q = lax.rem(chip + i, 8)
        kc, vc = kv_cols(q)
        a = rcopy(kv_in.at[:, kc], keys.at[own_kv, :], k_s.at[q], k_r.at[t], g, q * 2 + core)
        b = rcopy(kv_in.at[:, vc], values.at[own_kv, :], v_s.at[q], v_r.at[t], g, q * 2 + core)
        if start:
            a.start()
            b.start()
        else:
            a.wait_send()
            b.wait_send()

    loop(1, 8, lambda i: kv_send(i, True))
    qcopy = rcopy(q_in.at[:, 1 - core], qs, qp_s.at[0], qp_r.at[0], g, sib)
    pcopy = rcopy(proj_in, proj_s, qp_s.at[1], qp_r.at[1], g, sib)
    qcopy.start()

    def kv_relay(src, start):
        rows = pl.ds(pl.multiple_of(src * 128, 128), 128)
        a = rcopy(keys.at[rows, :], keys.at[rows, :], rk_s.at[src // 2], k_r.at[src], g, sib)
        b = rcopy(values.at[rows, :], values.at[rows, :], rv_s.at[src // 2], v_r.at[src], g, sib)
        if start:
            a.start()
            b.start()
        else:
            a.wait_send()
            b.wait_send()

    def kv_wait(src):
        rows = pl.ds(pl.multiple_of(src * 128, 128), 128)
        rcopy(keys.at[rows, :], keys.at[rows, :], k_s.at[0], k_r.at[src], g, sib).wait_recv()
        rcopy(values.at[rows, :], values.at[rows, :], v_s.at[0], v_r.at[src], g, sib).wait_recv()

    local[0].wait()
    local[1].wait()
    kv_relay(t, True)

    def w_send(i, start):
        i = lax.rem(src16 + i, 16)
        dg, dt = plane(i)
        here = (i == src16) & (core == yl)

        if start:
            @pl.when(here)
            def _():
                pltpu.make_async_copy(w_in, wland.at[t], w_r.at[t]).start()

        @pl.when(jnp.logical_not(here))
        def _():
            copy = rcopy(w_in, wland.at[t], w_s.at[i], w_r.at[t], dg, dt)
            if start:
                copy.start()
            else:
                copy.wait_send()

    def x_send(i, start):
        j = lax.rem(m + i, 8)
        dg, dt = member(j)
        copy = rcopy(x_in.at[:, window(j)], xland.at[m], x_s.at[j], x_r.at[m], dg, dt)
        if start:
            copy.start()
        else:
            copy.wait_send()

    def kv_pass(i):
        src = lax.rem(chip + 8 - i, 8) * 2 + core
        kv_wait(src)
        kv_relay(src, True)

    loop(1, 8, kv_pass)
    pcopy.start()
    loop(0, 16, lambda i: w_send(i, True))
    loop(1, 8, lambda i: x_send(i, True))

    loop(0, 8, lambda i: kv_wait(i * 2 + 1 - core))
    local[2].wait()
    qcopy.wait_recv()

    def t_send(q, start):
        copy = rcopy(tsend.at[q], tland.at[chip], t_s.at[q], t_r.at[chip], g, q * 2 + core)
        if start:
            copy.start()
        else:
            copy.wait_send()

    def o_send(i, start):
        j = lax.rem(m + i, 8)
        dg, dt = member(j)
        copy = rcopy(osend.at[j], oland.at[m], o_s.at[j], o_r.at[m], dg, dt)
        if start:
            copy.start()
        else:
            copy.wait_send()

    off = pl.multiple_of(lax.rem(x, 2) * 64, 64)

    def student_forward():
        loop(0, 16, lambda i: pltpu.make_async_copy(w_in, wland.at[i], w_r.at[i]).wait())
        wz[...] = jnp.zeros_like(wz)
        bias = jnp.zeros((1, 1024), F32)
        for a in range(4):
            rows = [wland[4 * a + b].astype(F32) for b in range(4)]
            for r in rows:
                bias = bias + r[28:29]
            wz[pl.ds(off + a * 112, 112), :] = jnp.concatenate([r[:28] for r in rows], axis=0).astype(BF)
        brow[...] = bias
        local[4].wait()

        def one(i):
            j = lax.rem(m + i, 8)

            @pl.when(i > 0)
            def _():
                rcopy(xland.at[j], xland.at[j], x_s.at[0], x_r.at[j], g, sib).wait_recv()

            xw = xland[j]
            xt[j] = jnp.transpose(xw)
            for n in range(4):
                cols = slice(n * 256, (n + 1) * 256)
                o = jnp.dot(xw, wz[:, cols], preferred_element_type=F32) + brow[:, cols]
                osend[j, :, cols] = o.astype(BF)

            @pl.when(i > 0)
            def _():
                o_send(i, True)

        loop(0, 8, one)
        oland[m] = osend[m]

    local[3].wait()
    pcopy.wait_recv()

    def chunk(i):
        c = lax.rem(chip + 1 + i, 8)

        @pl.when(i == 3)
        def _():
            student_forward()

        attend(core, c, qo.at[c], qs.at[c], keys, values, S, mx, acc, att)
        for n in range(4):
            cols = slice(n * 256, (n + 1) * 256)
            p = jnp.dot(att[:, :512], proj_o[:, cols], preferred_element_type=F32)
            p = p + jnp.dot(att[:, 512:], proj_s[:, cols], preferred_element_type=F32)
            tsend[c, :, cols] = p.astype(BF)

        @pl.when(i < 7)
        def _():
            t_send(c, True)

    loop(0, 8, chunk)
    tland[chip] = tsend[chip]

    def t_wait(i):
        q = lax.rem(chip + i, 8)
        rcopy(tland.at[q], tland.at[q], t_s.at[0], t_r.at[q], g, sib).wait_recv()

    loop(1, 8, t_wait)
    for n in range(4):
        cols = slice(n * 256, (n + 1) * 256)
        total = tland[0, :, cols].astype(F32)
        for q in range(1, 8):
            total = total + tland[q, :, cols].astype(F32)
        tsum[:, :, cols] = total.astype(BF).reshape(8, 16, 256)

    def p_send(i, start):
        j = lax.rem(g + i, 8)
        copy = rcopy(tsum.at[j], pland.at[g], p_s.at[j], p_r.at[g], j, t)
        if start:
            copy.start()
        else:
            copy.wait_send()

    loop(1, 8, lambda i: p_send(i, True))
    pland[g] = tsum[g]

    def o_wait(i):
        j = lax.rem(m + i, 8)
        rcopy(oland.at[j], oland.at[j], o_s.at[0], o_r.at[j], g, sib).wait_recv()

    loop(1, 8, o_wait)

    def p_wait(i):
        j = lax.rem(g + i, 8)
        rcopy(pland.at[j], pland.at[j], p_s.at[0], p_r.at[j], g, sib).wait_recv()

    loop(1, 8, p_wait)
    keep = jnp.where(ids_in[...] < TEXT_IDS, 1.0, 0.0).astype(F32)
    keep = jnp.transpose(jnp.broadcast_to(keep, (128, 128)))
    for k in range(8):
        rows = slice(k * 16, (k + 1) * 16)
        o = oland[0, rows, :].astype(F32)
        for j in range(1, 8):
            o = o + oland[j, rows, :].astype(F32)
        paired = pland[own_in[k]].astype(F32)
        kk = jnp.concatenate([keep[rows]] * 8, axis=1)
        eland[m, rows, :] = (kk * (o - paired)).astype(BF)

    def e_send(i, start):
        xx = lax.rem(x + i, 4)
        copy = rcopy(eland.at[m], eland.at[m], e_s.at[i], e_r.at[m], yl * 4 + xx, t)
        if start:
            copy.start()
        else:
            copy.wait_send()

    def e_relay(i, start):
        j = core * 4 + lax.rem(x + i, 4)
        copy = rcopy(eland.at[j], eland.at[j], re_s.at[i], e_r.at[j], g, sib)
        if start:
            copy.start()
        else:
            copy.wait_send()

    def e_wait(j):
        rcopy(eland.at[j], eland.at[j], e_s.at[0], e_r.at[j], g, sib).wait_recv()

    loop(1, 4, lambda i: e_send(i, True))
    e_relay(0, True)

    def e_pass(i):
        e_wait(core * 4 + lax.rem(x + i, 4))
        e_relay(i, True)

    loop(1, 4, e_pass)
    loop(0, 4, lambda i: e_wait((1 - core) * 4 + i))

    def i_send(i, start):
        j = lax.rem(m + i, 8)
        dg, dt = member(j)
        copy = rcopy(igsend.at[j], igland.at[m], i_s.at[j], i_r.at[m], dg, dt)
        if start:
            copy.start()
        else:
            copy.wait_send()

    def input_grad(i):
        j = lax.rem(m + i, 8)
        igsend[j] = lax.dot_general(eland[j], wz[...], (((1,), (1,)), ((), ())),
                                    preferred_element_type=F32).astype(BF)

        @pl.when(i < 8)
        def _():
            i_send(i, True)

    esum = []
    lsum = []
    for n in range(4):
        cols = slice(n * 256, (n + 1) * 256)
        total = jnp.zeros((512, 256), F32)
        eb = jnp.zeros((8, 256), F32)
        lb = jnp.zeros((8, 256), F32)
        for j in range(8):
            e = eland[j, :, cols]
            total = total + jnp.dot(xt[j], e, preferred_element_type=F32)
            ef = e.astype(F32)
            for r in range(16):
                er = ef[r * 8:(r + 1) * 8]
                eb = eb + er
                lb = lb + er * er
        wg[:, cols] = total
        esum.append(jnp.sum(eb, axis=0, keepdims=True))
        lsum.append(jnp.sum(lb, axis=0, keepdims=True))
    esum = jnp.concatenate(esum, axis=1)
    lsum = jnp.concatenate(lsum, axis=1)
    ehi = esum.astype(BF).astype(F32)
    lhi = lsum.astype(BF).astype(F32)
    extra = [ehi, esum - ehi, lhi, lsum - lhi]

    def g_send(i, start):
        here = (c_is_yl) & (i == t)

        if start:
            @pl.when(here)
            def _():
                pltpu.make_async_copy(wsend.at[i], wgland.at[src16], g_r.at[src16]).start()

        @pl.when(jnp.logical_not(here))
        def _():
            copy = rcopy(wsend.at[i], wgland.at[src16], g_s.at[i], g_r.at[src16], core * 4 + x, i)
            if start:
                copy.start()
            else:
                copy.wait_send()

    c_is_yl = core == yl
    row = lax.broadcasted_iota(jnp.int32, (32, 1024), 0)
    for i in range(16):
        v = wg[pl.ds(off + (28 * i) // 8 * 8, 32), :]
        if (28 * i) % 8:
            v = pltpu.roll(v, 28, 0)
        for r in range(4):
            v = jnp.where(row == 28 + r, extra[r], v)
        wsend[i] = v.astype(BF)
    loop(0, 16, lambda i: g_send(lax.rem(t + i, 16), True))
    loop(1, 9, input_grad)
    igland[m] = igsend[m]

    loop(0, 16, lambda i: pltpu.make_async_copy(wsend.at[i], wgland.at[i], g_r.at[i]).wait())
    total = wgland[0].astype(F32)
    for i in range(1, 16):
        total = total + wgland[i].astype(F32)
    wg_out[...] = total[:28]
    small_out[...] = total[24:32]

    def i_wait(i):
        j = lax.rem(m + i, 8)
        rcopy(igland.at[j], igland.at[j], i_s.at[0], i_r.at[j], g, sib).wait_recv()

    loop(1, 8, i_wait)
    for b in range(4):
        ig_out[:, b * 896:b * 896 + 384] = igland[2 * b, :, :384]
        ig_out[:, b * 896 + 384:b * 896 + 512] = igland[2 * b, :, 384:] + igland[2 * b + 1, :, :128]
        ig_out[:, b * 896 + 512:(b + 1) * 896] = igland[2 * b + 1, :, 128:]

    loop(1, 8, lambda i: kv_send(i, False))
    qcopy.wait_send()
    pcopy.wait_send()
    loop(0, 8, lambda i: kv_relay(i * 2 + core, False))
    loop(0, 16, lambda i: w_send(i, False))
    loop(1, 8, lambda i: x_send(i, False))
    loop(1, 8, lambda i: o_send(i, False))
    loop(1, 8, lambda i: t_send(lax.rem(chip + i, 8), False))
    loop(1, 8, lambda i: p_send(i, False))
    loop(1, 4, lambda i: e_send(i, False))
    loop(0, 4, lambda i: e_relay(i, False))
    loop(0, 16, lambda i: g_send(i, False))
    loop(1, 8, lambda i: i_send(i, False))


def on_device(queries, keys_values, projector, ownership, token_ids, student_input, student_weight, student_bias):
    d = lax.axis_index("grp") * 16 + lax.axis_index("tp")
    bias_row = lax.dynamic_update_slice(jnp.zeros((4, 1024), BF), student_bias[None], (0, d * 8))
    w_pad = jnp.concatenate([student_weight, bias_row], axis=0)
    hbm = pl.BlockSpec(memory_space=pl.ANY)
    vmem = pl.BlockSpec(memory_space=pltpu.VMEM)
    smem = pl.BlockSpec(memory_space=pltpu.SMEM)
    dma = pltpu.SemaphoreType.DMA
    V = pltpu.VMEM
    wg, small, ig = pl.pallas_call(
        kernel,
        out_shape=(jax.ShapeDtypeStruct((28, 1024), F32), jax.ShapeDtypeStruct((8, 1024), F32),
                   jax.ShapeDtypeStruct((128, 3584), BF)),
        in_specs=[hbm, hbm, hbm, smem, vmem, hbm, hbm],
        out_specs=(vmem, vmem, vmem),
        scratch_shapes=[
            V((8, 128, 512), BF), V((8, 128, 512), BF), V((2048, 128), BF), V((2048, 128), BF),
            V((1024, 2048), F32), V((1024, 128), F32), V((1024, 256), F32), V((128, 1024), BF),
            V((512, 1024), BF), V((512, 1024), BF), V((8, 128, 1024), BF), V((8, 128, 1024), BF),
            V((8, 16, 1024), BF), V((8, 16, 1024), BF),
            V((8, 128, 512), BF), V((8, 512, 128), BF), V((16, 32, 1024), BF), V((512, 1024), BF), V((1, 1024), F32),
            V((8, 128, 1024), BF), V((8, 128, 1024), BF), V((8, 128, 1024), BF),
            V((512, 1024), F32), V((16, 32, 1024), BF), V((16, 32, 1024), BF),
            V((8, 128, 512), BF), V((8, 128, 512), BF),
            dma((5,)), dma((2,)), dma((2,)), dma((8,)), dma((16,)), dma((8,)), dma((16,)), dma((8,)), dma((8,)),
            dma((16,)), dma((16,)), dma((8,)), dma((8,)), dma((8,)), dma((8,)),
            dma((8,)), dma((8,)), dma((8,)), dma((8,)), dma((4,)), dma((8,)), dma((4,)), dma((16,)), dma((16,)),
            dma((8,)), dma((8,)),
        ],
        compiler_params=pltpu.CompilerParams(
            collective_id=0, has_side_effects=True, vmem_limit_bytes=60 * 2 ** 20),
        cost_estimate=pl.CostEstimate(flops=9 * 10 ** 9, bytes_accessed=8 * 10 ** 6, transcendentals=9 * 10 ** 6),
    )(queries.reshape(8, 2, 128, 512), keys_values[0], projector, ownership, token_ids.reshape(1, 128),
      student_input, w_pad)
    loss = (jnp.sum(small[6]) + jnp.sum(small[7])) / 32768.0
    bias = lax.dynamic_slice(small[4] + small[5], (d * 8,), (8,))
    return loss, wg, bias, ig


def solution(mesh):
    return jax.shard_map(
        on_device,
        mesh=mesh,
        in_specs=(
            P("grp", None, "tp"), P("grp", "tp", None), P("tp", None), P(), P(("grp", "tp")),
            P(("grp", "tp"), None), P(("grp", "tp"), None), P(("grp", "tp")),
        ),
        out_specs=(P(), P(("grp", "tp"), None), P(("grp", "tp")), P(("grp", "tp"), None)),
        check_vma=False,
    )
```

```python
import functools

import jax
import jax.numpy as jnp
from jax import lax
from jax.experimental import pallas as pl
from jax.experimental.pallas import tpu as pltpu
from jax.sharding import PartitionSpec as P

MESH = pl.DeviceIdType.MESH
TEXT_IDS = 151643
SCALE = 128 ** -0.5 * 1.4426950408889634
BF = jnp.bfloat16
F32 = jnp.float32


def rcopy(src, dst, send_sem, recv_sem, grp, tp):
    return pltpu.make_async_remote_copy(
        src_ref=src, dst_ref=dst, send_sem=send_sem, recv_sem=recv_sem,
        device_id=(grp, tp), device_id_type=MESH)


def loop(first, last, body):
    lax.fori_loop(first, last, lambda i, carry: (body(i), carry)[1], 0)


def attend(core, c, qo, qs, keys, values, S, mx, acc, out):
    T = 256

    def score(j, masked):
        at = pl.ds(pl.multiple_of(j * T, T), T)
        kt = keys[at, :]
        if masked:
            row = lax.broadcasted_iota(jnp.int32, (128, T), 0) + core * 128
            keep = row >= lax.broadcasted_iota(jnp.int32, (128, T), 1)
        for h in range(8):
            hr = slice(h * 128, (h + 1) * 128)
            q = (qo if h < 4 else qs)[:, (h % 4) * 128:(h % 4) * 128 + 128]
            s = lax.dot_general(q, kt, (((1,), (1,)), ((), ())), preferred_element_type=F32)
            if masked:
                s = jnp.where(keep, s, -1e30)
            S[hr, at] = s
            m = jnp.maximum(mx[hr, :], jnp.maximum(s[:, :128], s[:, 128:]))
            if masked:
                m = jnp.broadcast_to(jnp.max(m, axis=1, keepdims=True) * SCALE, (128, 128))
            mx[hr, :] = m

    mx[...] = jnp.full_like(mx, -1e30)
    loop(0, c, lambda j: score(j, False))
    score(c, True)
    acc[...] = jnp.zeros_like(acc)

    def weigh(off, W):
        vt = values[pl.ds(off, W), :]
        vt = jnp.concatenate([vt, jnp.ones_like(vt)], axis=1)
        for h in range(8):
            hr = slice(h * 128, (h + 1) * 128)
            m = mx[hr, :]
            ps = []
            for w in range(W // 128):
                s = S[hr, pl.ds(pl.multiple_of(off + w * 128, 128), 128)]
                ps.append(jnp.exp2(s * SCALE - m).astype(BF))
            acc[hr, :] += jnp.dot(jnp.concatenate(ps, axis=1), vt, preferred_element_type=F32)

    n = c + 1
    loop(0, n // 2, lambda j: weigh(pl.multiple_of(j * 512, 512), 512))
    loop(0, n % 2, lambda j: weigh(pl.multiple_of((n - 1) * 256, 256), 256))
    for h in range(8):
        a = acc[h * 128:(h + 1) * 128, :]
        out[:, h * 128:(h + 1) * 128] = (a[:, :128] / a[:, 128:]).astype(BF)


def kernel(q_in, kv_in, proj_in, own_in, ids_in, x_in, w_in, b_in,
           wgland, igland,
           qo, qs, keys, values, S, mx, acc, att, proj_o, proj_s, tsend, ta, ta2, tb, tbsum, tb2, tsum, pland,
           xland, xt, w_pad, wland, wz, brow, osib, oswap, osend, oland, eland, wg, wsend, igsend,
           l_sem, qp_s, qp_r, k_s, k_r, v_s, v_r, rk_s, rv_s, w_s, w_r, x_s, x_r, os_s, os_r, o_s, o_r,
           ta_s, ta_r, tb_s, tb_r, ta2_s, ta2_r, tb2_s, tb2_r, p_s, p_r, e_s, e_r, re_s, g_s, g_r, i_s, i_r):
    g = lax.axis_index("grp")
    t = lax.axis_index("tp")
    x, yl = lax.rem(g, 4), g // 4
    core, chip = lax.rem(t, 2), t // 2
    sib = chip * 2 + 1 - core
    m = core * 4 + x
    src16 = chip * 2 + yl

    def member(i):
        return yl * 4 + lax.rem(i, 4), chip * 2 + i // 4

    def plane(i):
        return lax.rem(i, 2) * 4 + x, (i // 2) * 2 + yl

    own_kv = pl.ds(pl.multiple_of(t * 128, 128), 128)
    kcol = pl.ds(pl.multiple_of(chip * 128, 128), 128)
    vcol = pl.ds(pl.multiple_of(1024 + chip * 128, 128), 128)

    def window(i):
        return pl.ds(pl.multiple_of((i // 2) * 896 + lax.rem(i, 2) * 384, 128), 512)

    local = [
        pltpu.make_async_copy(kv_in.at[:, kcol], keys.at[own_kv, :], l_sem.at[0]),
        pltpu.make_async_copy(kv_in.at[:, vcol], values.at[own_kv, :], l_sem.at[1]),
        pltpu.make_async_copy(q_in.at[:, core], qo, l_sem.at[2]),
        pltpu.make_async_copy(proj_in, proj_o, l_sem.at[3]),
        pltpu.make_async_copy(x_in.at[:, window(m)], xland.at[m], l_sem.at[4]),
    ]
    for copy in local:
        copy.start()

    lane = lax.broadcasted_iota(jnp.int32, (4, 1024), 1) - (g * 16 + t) * 8
    first = lax.broadcasted_iota(jnp.int32, (4, 1024), 0) == 0
    b_row = jnp.zeros((4, 1024), F32)
    for r in range(8):
        b_row = jnp.where(first & (lane == r), jnp.broadcast_to(b_in[:, r:r + 1].astype(F32), (4, 1024)), b_row)
    w_pad[...] = jnp.concatenate([w_in[...].astype(F32), b_row], axis=0).astype(BF)

    barrier = pltpu.get_barrier_semaphore()

    def greet(grp, tp):
        pl.semaphore_signal(barrier, inc=1, device_id=(grp, tp), device_id_type=MESH)

    def greet_plane(i):
        j = lax.rem(yl * 16 + t + i, 32)
        greet((j // 16) * 4 + x, lax.rem(j, 16))

    loop(1, 32, greet_plane)

    def greet_x(i):
        xx = lax.rem(x + i, 4)
        greet(yl * 4 + xx, t)
        greet(yl * 4 + xx, sib)
        greet((1 - yl) * 4 + xx, t)

    loop(1, 4, greet_x)
    pl.semaphore_wait(barrier, 31 + 9)

    def kv_cols(q):
        return (pl.ds(pl.multiple_of(q * 128, 128), 128),
                pl.ds(pl.multiple_of(1024 + q * 128, 128), 128))

    def kv_send(i, start):
        q = lax.rem(chip + i, 8)
        kc, vc = kv_cols(q)
        a = rcopy(kv_in.at[:, kc], keys.at[own_kv, :], k_s.at[q], k_r.at[t], g, q * 2 + core)
        b = rcopy(kv_in.at[:, vc], values.at[own_kv, :], v_s.at[q], v_r.at[t], g, q * 2 + core)
        if start:
            a.start()
            b.start()
        else:
            a.wait_send()
            b.wait_send()

    loop(1, 8, lambda i: kv_send(i, True))
    qcopy = rcopy(q_in.at[:, 1 - core], qs, qp_s.at[0], qp_r.at[0], g, sib)
    pcopy = rcopy(proj_in, proj_s, qp_s.at[1], qp_r.at[1], g, sib)
    qcopy.start()

    def kv_relay(src, start):
        rows = pl.ds(pl.multiple_of(src * 128, 128), 128)
        a = rcopy(keys.at[rows, :], keys.at[rows, :], rk_s.at[src // 2], k_r.at[src], g, sib)
        b = rcopy(values.at[rows, :], values.at[rows, :], rv_s.at[src // 2], v_r.at[src], g, sib)
        if start:
            a.start()
            b.start()
        else:
            a.wait_send()
            b.wait_send()

    def kv_wait(src):
        rows = pl.ds(pl.multiple_of(src * 128, 128), 128)
        rcopy(keys.at[rows, :], keys.at[rows, :], k_s.at[0], k_r.at[src], g, sib).wait_recv()
        rcopy(values.at[rows, :], values.at[rows, :], v_s.at[0], v_r.at[src], g, sib).wait_recv()

    local[0].wait()
    local[1].wait()
    kv_relay(t, True)

    def w_send(i, start):
        i = lax.rem(src16 + i, 16)
        dg, dt = plane(i)
        here = (i == src16) & (core == yl)

        if start:
            @pl.when(here)
            def _():
                pltpu.make_async_copy(w_pad, wland.at[t], w_r.at[t]).start()

        @pl.when(jnp.logical_not(here))
        def _():
            copy = rcopy(w_pad, wland.at[t], w_s.at[i], w_r.at[t], dg, dt)
            if start:
                copy.start()
            else:
                copy.wait_send()

    def x_send(i, start):
        j = lax.rem(m + i, 8)
        dg, dt = member(j)
        copy = rcopy(x_in.at[:, window(j)], xland.at[m], x_s.at[j], x_r.at[m], dg, dt)
        if start:
            copy.start()
        else:
            copy.wait_send()

    def kv_pass(i):
        src = lax.rem(chip + 8 - i, 8) * 2 + core
        kv_wait(src)
        kv_relay(src, True)

    loop(1, 8, kv_pass)
    pcopy.start()
    loop(0, 16, lambda i: w_send(i, True))
    loop(1, 8, lambda i: x_send(i, True))

    loop(0, 8, lambda i: kv_wait(i * 2 + 1 - core))
    local[2].wait()
    qcopy.wait_recv()

    cz, ch = chip // 2, lax.rem(chip, 2)
    A, B = pl.ds(0, 512), pl.ds(512, 512)

    def ta_send(c, start):
        copy = rcopy(tsend.at[c, :, A], ta.at[lax.rem(c, 2), cz], ta_s.at[c], ta_r.at[lax.rem(c, 2) * 4 + cz],
                     g, (c // 2 * 2 + ch) * 2 + core)
        if start:
            copy.start()
        else:
            copy.wait_send()

    def ta_wait(h, z):
        rcopy(ta.at[h, z], ta.at[h, z], ta_s.at[0], ta_r.at[h * 4 + z], g, sib).wait_recv()

    def ta2_send():
        return rcopy(ta2.at[0], ta2.at[1], ta2_s.at[0], ta2_r.at[0], g, (cz * 2 + 1 - ch) * 2 + core)

    def tb_send(z, start):
        copy = rcopy(tsend.at[z * 2 + 1 - ch, :, B], tb.at[z], tb_s.at[z], tb_r.at[z],
                     g, (cz * 2 + 1 - ch) * 2 + core)
        if start:
            copy.start()
        else:
            copy.wait_send()

    def tb2_send(z, start):
        copy = rcopy(tbsum.at[z], tb2.at[cz], tb2_s.at[z], tb2_r.at[cz], g, (z * 2 + ch) * 2 + core)
        if start:
            copy.start()
        else:
            copy.wait_send()

    def os_send(i, start):
        copy = rcopy(osib.at[i], oswap.at[i], os_s.at[i], os_r.at[i], g, sib)
        if start:
            copy.start()
        else:
            copy.wait_send()

    def o_send(i, start):
        xx = lax.rem(x + i, 4)
        copy = rcopy(osend.at[xx], oland.at[x], o_s.at[xx], o_r.at[x], yl * 4 + xx, t)
        if start:
            copy.start()
        else:
            copy.wait_send()

    off = pl.multiple_of(lax.rem(x, 2) * 64, 64)

    def student_forward():
        loop(0, 16, lambda i: pltpu.make_async_copy(w_pad, wland.at[i], w_r.at[i]).wait())
        wz[...] = jnp.zeros_like(wz)
        bias = jnp.zeros((1, 1024), F32)
        for a in range(4):
            rows = [wland[4 * a + b].astype(F32) for b in range(4)]
            for r in rows:
                bias = bias + r[28:29]
            wz[pl.ds(off + a * 112, 112), :] = jnp.concatenate([r[:28] for r in rows], axis=0).astype(BF)
        brow[...] = bias
        local[4].wait()

        def fetch(j):
            @pl.when(j != m)
            def _():
                rcopy(xland.at[j], xland.at[j], x_s.at[0], x_r.at[j], g, sib).wait_recv()

            xt[j] = jnp.transpose(xland[j])

        def one(i, j, dst):
            fetch(j)
            for n in range(4):
                cols = slice(n * 256, (n + 1) * 256)
                o = jnp.dot(xland[j], wz[:, cols], preferred_element_type=F32) + brow[:, cols]
                dst[i, :, cols] = o.astype(BF)

        def theirs(i):
            xx = lax.rem(x + i, 4)
            one(xx, (1 - core) * 4 + xx, osib)
            os_send(xx, True)

        loop(0, 4, theirs)
        loop(0, 4, lambda i: one(i, core * 4 + i, osend))

    def output_sums():
        def one(i):
            xx = lax.rem(x + i, 4)
            rcopy(oswap.at[xx], oswap.at[xx], os_s.at[0], os_r.at[xx], g, sib).wait_recv()
            osend[xx] = (osend[xx].astype(F32) + oswap[xx].astype(F32)).astype(BF)

            @pl.when(i < 4)
            def _():
                o_send(i, True)

        loop(1, 5, one)
        oland[x] = osend[x]

    local[3].wait()
    pcopy.wait_recv()

    def chunk(i):
        z = lax.rem(cz + 1 + i // 2, 4)
        own = lax.rem(i, 2) == 1
        c = z * 2 + lax.rem(ch + 1 + i, 2)

        @pl.when(i == 2)
        def _():
            student_forward()

        @pl.when(i == 4)
        def _():
            output_sums()

        attend(core, c, qo.at[c], qs.at[c], keys, values, S, mx, acc, att)
        for n in range(4):
            cols = slice(n * 256, (n + 1) * 256)
            p = jnp.dot(att[:, :512], proj_o[:, cols], preferred_element_type=F32)
            p = p + jnp.dot(att[:, 512:], proj_s[:, cols], preferred_element_type=F32)
            tsend[c, :, cols] = p.astype(BF)

        @pl.when(i < 6)
        def _():
            ta_send(c, True)

        @pl.when(jnp.logical_not(own))
        def _():
            tb_send(z, True)

        @pl.when(own)
        def _():
            rcopy(tb.at[z], tb.at[z], tb_s.at[0], tb_r.at[z], g, sib).wait_recv()
            tbsum[z] = (tsend[c, :, B].astype(F32) + tb[z].astype(F32)).astype(BF)

            @pl.when(i < 6)
            def _():
                tb2_send(z, True)

        @pl.when(i == 6)
        def _():
            total = tsend[c, :, A].astype(F32)
            for k in range(1, 4):
                zz = lax.rem(cz + k, 4)
                ta_wait(1 - ch, zz)
                total = total + ta[1 - ch, zz].astype(F32)
            ta2[0] = total.astype(BF)
            ta2_send().start()

    loop(0, 8, chunk)
    total = tsend[chip, :, A].astype(F32)
    for k in range(1, 4):
        zz = lax.rem(cz + k, 4)
        ta_wait(ch, zz)
        total = total + ta[ch, zz].astype(F32)
    ta2_send().wait_recv()
    total = total + ta2[1].astype(F32)
    tsum[:, :, A] = total.astype(BF).reshape(8, 16, 512)
    total = tbsum[cz].astype(F32)
    for k in range(1, 4):
        zz = lax.rem(cz + k, 4)
        rcopy(tb2.at[zz], tb2.at[zz], tb2_s.at[0], tb2_r.at[zz], g, sib).wait_recv()
        total = total + tb2[zz].astype(F32)
    tsum[:, :, B] = total.astype(BF).reshape(8, 16, 512)

    def p_send(i, start):
        j = lax.rem(g + i, 8)
        copy = rcopy(tsum.at[j], pland.at[g], p_s.at[j], p_r.at[g], j, t)
        if start:
            copy.start()
        else:
            copy.wait_send()

    loop(1, 8, lambda i: p_send(i, True))
    pland[g] = tsum[g]

    def o_wait(i):
        j = lax.rem(x + i, 4)
        rcopy(oland.at[j], oland.at[j], o_s.at[0], o_r.at[j], g, sib).wait_recv()

    loop(1, 4, o_wait)

    def p_wait(i):
        j = lax.rem(g + i, 8)
        rcopy(pland.at[j], pland.at[j], p_s.at[0], p_r.at[j], g, sib).wait_recv()

    loop(1, 8, p_wait)
    keep = jnp.where(ids_in[...] < TEXT_IDS, 1.0, 0.0).astype(F32)
    keep = jnp.transpose(jnp.broadcast_to(keep, (128, 128)))
    for k in range(8):
        rows = slice(k * 16, (k + 1) * 16)
        o = oland[0, rows, :].astype(F32)
        for j in range(1, 4):
            o = o + oland[j, rows, :].astype(F32)
        paired = pland[own_in[k]].astype(F32)
        kk = jnp.concatenate([keep[rows]] * 8, axis=1)
        eland[m, rows, :] = (kk * (o - paired)).astype(BF)

    def e_send(i, start):
        xx = lax.rem(x + i, 4)
        copy = rcopy(eland.at[m], eland.at[m], e_s.at[i], e_r.at[m], yl * 4 + xx, t)
        if start:
            copy.start()
        else:
            copy.wait_send()

    def e_relay(i, start):
        j = core * 4 + lax.rem(x + i, 4)
        copy = rcopy(eland.at[j], eland.at[j], re_s.at[i], e_r.at[j], g, sib)
        if start:
            copy.start()
        else:
            copy.wait_send()

    def e_wait(j):
        rcopy(eland.at[j], eland.at[j], e_s.at[0], e_r.at[j], g, sib).wait_recv()

    loop(1, 4, lambda i: e_send(i, True))
    e_relay(0, True)

    def e_pass(i):
        e_wait(core * 4 + lax.rem(x + i, 4))
        e_relay(i, True)

    loop(1, 4, e_pass)
    loop(0, 4, lambda i: e_wait((1 - core) * 4 + i))

    def i_send(i, start):
        j = lax.rem(m + i, 8)
        dg, dt = member(j)
        copy = rcopy(igsend.at[j], igland.at[m], i_s.at[j], i_r.at[m], dg, dt)
        if start:
            copy.start()
        else:
            copy.wait_send()

    def input_grad(i):
        j = lax.rem(m + i, 8)
        igsend[j] = lax.dot_general(eland[j], wz[...], (((1,), (1,)), ((), ())),
                                    preferred_element_type=F32).astype(BF)

        @pl.when(i < 8)
        def _():
            i_send(i, True)

    esum = []
    lsum = []
    for n in range(4):
        cols = slice(n * 256, (n + 1) * 256)
        total = jnp.zeros((512, 256), F32)
        eb = jnp.zeros((8, 256), F32)
        lb = jnp.zeros((8, 256), F32)
        for j in range(8):
            e = eland[j, :, cols]
            total = total + jnp.dot(xt[j], e, preferred_element_type=F32)
            ef = e.astype(F32)
            for r in range(16):
                er = ef[r * 8:(r + 1) * 8]
                eb = eb + er
                lb = lb + er * er
        wg[:, cols] = total
        esum.append(jnp.sum(eb, axis=0, keepdims=True))
        lsum.append(jnp.sum(lb, axis=0, keepdims=True))
    esum = jnp.concatenate(esum, axis=1)
    lsum = jnp.concatenate(lsum, axis=1)
    ehi = esum.astype(BF).astype(F32)
    lhi = lsum.astype(BF).astype(F32)
    extra = [ehi, esum - ehi, lhi, lsum - lhi]

    def g_send(i, start):
        here = (c_is_yl) & (i == t)

        if start:
            @pl.when(here)
            def _():
                pltpu.make_async_copy(wsend.at[i], wgland.at[src16], g_r.at[src16]).start()

        @pl.when(jnp.logical_not(here))
        def _():
            copy = rcopy(wsend.at[i], wgland.at[src16], g_s.at[i], g_r.at[src16], core * 4 + x, i)
            if start:
                copy.start()
            else:
                copy.wait_send()

    c_is_yl = core == yl
    row = lax.broadcasted_iota(jnp.int32, (32, 1024), 0)
    for i in range(16):
        v = wg[pl.ds(off + (28 * i) // 8 * 8, 32), :]
        if (28 * i) % 8:
            v = pltpu.roll(v, 28, 0)
        for r in range(4):
            v = jnp.where(row == 28 + r, extra[r], v)
        wsend[i] = v.astype(BF)
    loop(0, 16, lambda i: g_send(lax.rem(t + i, 16), True))
    loop(1, 9, input_grad)
    ig_own = pltpu.make_async_copy(igsend.at[m], igland.at[m], i_r.at[m])
    ig_own.start()

    loop(0, 16, lambda i: pltpu.make_async_copy(wsend.at[i], wgland.at[i], g_r.at[i]).wait())
    ig_own.wait()

    def i_wait(i):
        j = lax.rem(m + i, 8)
        rcopy(igland.at[j], igland.at[j], i_s.at[0], i_r.at[j], g, sib).wait_recv()

    loop(1, 8, i_wait)

    loop(1, 8, lambda i: kv_send(i, False))
    qcopy.wait_send()
    pcopy.wait_send()
    loop(0, 8, lambda i: kv_relay(i * 2 + core, False))
    loop(0, 16, lambda i: w_send(i, False))
    loop(1, 8, lambda i: x_send(i, False))
    loop(0, 4, lambda i: os_send(i, False))
    loop(1, 4, lambda i: o_send(i, False))
    loop(2, 8, lambda i: ta_send(lax.rem(cz * 2 + i, 8), False))
    loop(0, 4, lambda i: tb_send(i, False))
    loop(1, 4, lambda i: tb2_send(lax.rem(cz + i, 4), False))
    ta2_send().wait_send()
    loop(1, 8, lambda i: p_send(i, False))
    loop(1, 4, lambda i: e_send(i, False))
    loop(0, 4, lambda i: e_relay(i, False))
    loop(0, 16, lambda i: g_send(i, False))
    loop(1, 8, lambda i: i_send(i, False))


def finish(wgland, igland, wg_out, bias_out, loss_out, ig_out):
    d = lax.axis_index("grp") * 16 + lax.axis_index("tp")
    total = wgland[0].astype(F32)
    for i in range(1, 16):
        total = total + wgland[i].astype(F32)
    wg_out[...] = total[:28]
    small = total[24:32]
    loss_out[...] = jnp.sum(small[6:8], axis=(0, 1), keepdims=True) / 32768.0
    both = jnp.broadcast_to(small[4:5] + small[5:6], (8, 1024))
    both = pltpu.roll(both, lax.rem(1024 - d * 8, 1024), 1)
    bias_out[...] = both[0:1, 0:8]
    for b in range(4):
        ig_out[:, b * 896:b * 896 + 384] = igland[2 * b, :, :384]
        ig_out[:, b * 896 + 384:b * 896 + 512] = igland[2 * b, :, 384:] + igland[2 * b + 1, :, :128]
        ig_out[:, b * 896 + 512:(b + 1) * 896] = igland[2 * b + 1, :, 128:]


def on_device(queries, keys_values, projector, ownership, token_ids, student_input, student_weight, student_bias):
    hbm = pl.BlockSpec(memory_space=pl.ANY)
    vmem = pl.BlockSpec(memory_space=pltpu.VMEM)
    smem = pl.BlockSpec(memory_space=pltpu.SMEM)
    dma = pltpu.SemaphoreType.DMA
    V = pltpu.VMEM
    wgland, igland = pl.pallas_call(
        kernel,
        out_shape=(jax.ShapeDtypeStruct((16, 32, 1024), BF), jax.ShapeDtypeStruct((8, 128, 512), BF)),
        in_specs=[hbm, hbm, hbm, smem, vmem, hbm, vmem, vmem],
        out_specs=(hbm, hbm),
        scratch_shapes=[
            V((8, 128, 512), BF), V((8, 128, 512), BF), V((2048, 128), BF), V((2048, 128), BF),
            V((1024, 2048), F32), V((1024, 128), F32), V((1024, 256), F32), V((128, 1024), BF),
            V((512, 1024), BF), V((512, 1024), BF), V((8, 128, 1024), BF),
            V((2, 4, 128, 512), BF), V((2, 128, 512), BF), V((4, 128, 512), BF), V((4, 128, 512), BF),
            V((4, 128, 512), BF), V((8, 16, 1024), BF), V((8, 16, 1024), BF),
            V((8, 128, 512), BF), V((8, 512, 128), BF), V((32, 1024), BF), V((16, 32, 1024), BF),
            V((512, 1024), BF), V((1, 1024), F32),
            V((4, 128, 1024), BF), V((4, 128, 1024), BF), V((4, 128, 1024), BF), V((4, 128, 1024), BF),
            V((8, 128, 1024), BF), V((512, 1024), F32), V((16, 32, 1024), BF), V((8, 128, 512), BF),
            dma((5,)), dma((2,)), dma((2,)), dma((8,)), dma((16,)), dma((8,)), dma((16,)), dma((8,)), dma((8,)),
            dma((16,)), dma((16,)), dma((8,)), dma((8,)), dma((4,)), dma((4,)), dma((4,)), dma((4,)),
            dma((8,)), dma((8,)), dma((4,)), dma((4,)), dma((1,)), dma((1,)), dma((4,)), dma((4,)),
            dma((8,)), dma((8,)), dma((4,)), dma((8,)), dma((4,)), dma((16,)), dma((16,)),
            dma((8,)), dma((8,)),
        ],
        compiler_params=pltpu.CompilerParams(
            collective_id=0, has_side_effects=True, vmem_limit_bytes=60 * 2 ** 20),
        cost_estimate=pl.CostEstimate(flops=9 * 10 ** 9, bytes_accessed=8 * 10 ** 6, transcendentals=9 * 10 ** 6),
    )(queries.reshape(8, 2, 128, 512), keys_values[0], projector, ownership, token_ids.reshape(1, 128),
      student_input, student_weight, student_bias.reshape(1, 8))
    wg, bias, loss, ig = pl.pallas_call(
        finish,
        out_shape=(jax.ShapeDtypeStruct((28, 1024), F32), jax.ShapeDtypeStruct((1, 8), F32),
                   jax.ShapeDtypeStruct((1, 1), F32), jax.ShapeDtypeStruct((128, 3584), BF)),
        in_specs=[vmem, vmem],
        out_specs=(vmem, vmem, vmem, vmem),
        compiler_params=pltpu.CompilerParams(vmem_limit_bytes=32 * 2 ** 20),
    )(wgland, igland)
    return loss.reshape(()), wg, bias.reshape(8), ig


def solution(mesh):
    return jax.shard_map(
        on_device,
        mesh=mesh,
        in_specs=(
            P("grp", None, "tp"), P("grp", "tp", None), P("tp", None), P(), P(("grp", "tp")),
            P(("grp", "tp"), None), P(("grp", "tp"), None), P(("grp", "tp")),
        ),
        out_specs=(P(), P(("grp", "tp"), None), P(("grp", "tp")), P(("grp", "tp"), None)),
        check_vma=False,
    )
```

```python
import functools

import jax
import jax.numpy as jnp
from jax import lax
from jax.experimental import pallas as pl
from jax.experimental.pallas import tpu as pltpu
from jax.sharding import PartitionSpec as P

MESH = pl.DeviceIdType.MESH
TEXT_IDS = 151643
SCALE = 128 ** -0.5 * 1.4426950408889634
BF = jnp.bfloat16
F32 = jnp.float32


def rcopy(src, dst, send_sem, recv_sem, grp, tp):
    return pltpu.make_async_remote_copy(
        src_ref=src, dst_ref=dst, send_sem=send_sem, recv_sem=recv_sem,
        device_id=(grp, tp), device_id_type=MESH)


def loop(first, last, body):
    lax.fori_loop(first, last, lambda i, carry: (body(i), carry)[1], 0)


def attend(core, c, qo, qs, keys, values, S, mx, acc, out, between):
    q = jnp.concatenate([r[:, h * 128:(h + 1) * 128] for r in (qo, qs) for h in range(4)], axis=0)

    def score(j, T, masked):
        at = pl.ds(pl.multiple_of(j * 256, 256), T)
        if masked:
            row = lax.broadcasted_iota(jnp.int32, (128, T), 0) + core * 128
            keep = row >= lax.broadcasted_iota(jnp.int32, (128, T), 1)
        s_all = lax.dot_general(q, keys[at, :], (((1,), (1,)), ((), ())), preferred_element_type=F32)
        for h in range(8):
            hr = slice(h * 128, (h + 1) * 128)
            s = s_all[hr]
            if masked:
                s = jnp.where(keep, s, -1e30)
            S[hr, at] = s
            m = mx[hr, :]
            for w in range(T // 128):
                m = jnp.maximum(m, s[:, w * 128:(w + 1) * 128])
            if masked:
                m = jnp.broadcast_to(jnp.max(m, axis=1, keepdims=True) * SCALE, (128, 128))
            mx[hr, :] = m

    mx[...] = jnp.full_like(mx, -1e30)
    loop(0, c // 2, lambda j: score(2 * j, 512, False))
    loop(0, lax.rem(c, 2), lambda j: score(c - 1, 256, False))
    score(c, 256, True)
    acc[...] = jnp.zeros_like(acc)
    between()

    def weigh(off, W):
        vt = values[pl.ds(off, W), :]
        vt = jnp.concatenate([vt, jnp.ones_like(vt)], axis=1)
        ps = []
        for h in range(8):
            hr = slice(h * 128, (h + 1) * 128)
            m = mx[hr, :]
            ps.append(jnp.concatenate(
                [jnp.exp2(S[hr, pl.ds(pl.multiple_of(off + w * 128, 128), 128)] * SCALE - m).astype(BF)
                 for w in range(W // 128)], axis=1))
        acc[...] += jnp.dot(jnp.concatenate(ps, axis=0), vt, preferred_element_type=F32)

    n = c + 1
    loop(0, n // 4, lambda j: weigh(pl.multiple_of(j * 1024, 1024), 1024))
    loop(0, lax.rem(n // 2, 2), lambda j: weigh(pl.multiple_of(n // 4 * 1024, 512), 512))
    loop(0, lax.rem(n, 2), lambda j: weigh(pl.multiple_of((n - 1) * 256, 256), 256))
    for h in range(8):
        a = acc[h * 128:(h + 1) * 128, :]
        out[:, h * 128:(h + 1) * 128] = (a[:, :128] / a[:, 128:]).astype(BF)


def kernel(q_in, kv_in, proj_in, own_in, ids_in, x_in, w_in, b_in,
           wgland, igland,
           qo, qs, keys, values, S, mx, acc, att, proj_o, proj_s, tsend, ta, ta2, tb, tbsum, tb2, tsum, pland,
           xland, xt, w_pad, wland, wz, wz2, brow, osib, oswap, osend, oland, eland, wg, extra, wsend, igsend,
           l_sem, qp_s, qp_r, k_s, k_r, v_s, v_r, rk_s, rv_s, w_s, w_r, x_s, x_r, os_s, os_r, o_s, o_r,
           ta_s, ta_r, tb_s, tb_r, ta2_s, ta2_r, tb2_s, tb2_r, p_s, p_r, e_s, e_r, f_s, f_r, re_s, re_r, g_s, g_r, i_s, i_r, w2_s, w2_r, round2, round3):
    g = lax.axis_index("grp")
    t = lax.axis_index("tp")
    x, yl = lax.rem(g, 4), g // 4
    core, chip = lax.rem(t, 2), t // 2
    sib = chip * 2 + 1 - core
    m = core * 4 + x
    src16 = chip * 2 + yl

    def member(i):
        return yl * 4 + lax.rem(i, 4), chip * 2 + i // 4

    def plane(i):
        return lax.rem(i, 2) * 4 + x, (i // 2) * 2 + yl

    own_kv = pl.ds(pl.multiple_of(t * 128, 128), 128)
    kcol = pl.ds(pl.multiple_of(chip * 128, 128), 128)
    vcol = pl.ds(pl.multiple_of(1024 + chip * 128, 128), 128)

    def window(i):
        return pl.ds(pl.multiple_of((i // 2) * 896 + lax.rem(i, 2) * 384, 128), 512)

    local = [
        pltpu.make_async_copy(kv_in.at[:, kcol], keys.at[own_kv, :], l_sem.at[0]),
        pltpu.make_async_copy(kv_in.at[:, vcol], values.at[own_kv, :], l_sem.at[1]),
        pltpu.make_async_copy(q_in.at[:, core], qo, l_sem.at[2]),
        pltpu.make_async_copy(proj_in, proj_o, l_sem.at[3]),
        pltpu.make_async_copy(x_in.at[:, window(m)], xland.at[m], l_sem.at[4]),
    ]
    for copy in local:
        copy.start()

    lane = lax.broadcasted_iota(jnp.int32, (4, 1024), 1) - (g * 16 + t) * 8
    first = lax.broadcasted_iota(jnp.int32, (4, 1024), 0) == 0
    b_row = jnp.zeros((4, 1024), F32)
    for r in range(8):
        b_row = jnp.where(first & (lane == r), jnp.broadcast_to(b_in[:, r:r + 1].astype(F32), (4, 1024)), b_row)
    w_pad[...] = jnp.concatenate([w_in[...].astype(F32), b_row], axis=0).astype(BF)

    barrier = pltpu.get_barrier_semaphore()

    def greet(sem):
        def tell(grp, tp):
            pl.semaphore_signal(sem, inc=1, device_id=(grp, tp), device_id_type=MESH)

        loop(1, 8, lambda i: tell(g, lax.rem(chip + i, 8) * 2 + core))
        tell(g, sib)
        loop(1, 4, lambda i: tell(yl * 4 + lax.rem(x + i, 4), t))
        tell((1 - yl) * 4 + x, t)

    greet(barrier)
    pl.semaphore_wait(barrier, 12)

    def kv_cols(q):
        return (pl.ds(pl.multiple_of(q * 128, 128), 128),
                pl.ds(pl.multiple_of(1024 + q * 128, 128), 128))

    def k_send(i, start):
        q = lax.rem(chip + i, 8)
        a = rcopy(kv_in.at[:, kv_cols(q)[0]], keys.at[own_kv, :], k_s.at[q], k_r.at[t], g, q * 2 + core)
        if start:
            a.start()
        else:
            a.wait_send()

    def v_send(i, start):
        q = lax.rem(chip + i, 8)
        a = rcopy(kv_in.at[:, kv_cols(q)[1]], values.at[own_kv, :], v_s.at[q], v_r.at[t], g, q * 2 + core)
        if start:
            a.start()
        else:
            a.wait_send()

    loop(1, 8, lambda i: k_send(i, True))
    qcopy = rcopy(q_in.at[:, 1 - core], qs, qp_s.at[0], qp_r.at[0], g, sib)
    pcopy = rcopy(proj_in, proj_s, qp_s.at[1], qp_r.at[1], g, sib)
    qcopy.start()
    loop(1, 8, lambda i: v_send(i, True))
    greet(round2)

    def rows_of(src):
        return pl.ds(pl.multiple_of(src * 128, 128), 128)

    def k_relay(src):
        rows = rows_of(src)
        return rcopy(keys.at[rows, :], keys.at[rows, :], rk_s.at[src // 2], k_r.at[src], g, sib)

    def v_relay(src):
        rows = rows_of(src)
        return rcopy(values.at[rows, :], values.at[rows, :], rv_s.at[src // 2], v_r.at[src], g, sib)

    def k_pass(i):
        src = lax.rem(chip + 8 - i, 8) * 2 + core
        k_relay(src).wait_recv()
        k_relay(src).start()

    def v_pass(i):
        src = lax.rem(chip + 8 - i, 8) * 2 + core
        v_relay(src).wait_recv()
        v_relay(src).start()

    local[0].wait()
    k_relay(t).start()
    local[1].wait()
    v_relay(t).start()
    loop(1, 8, k_pass)
    pl.semaphore_wait(round2, 12)
    pl.semaphore_signal(round3, inc=1, device_id=(g, sib), device_id_type=MESH)

    def w_send(i, start):
        i = lax.rem(src16 + i, 16)
        dg, dt = plane(i)
        here = (i == src16) & (core == yl)

        if start:
            @pl.when(here)
            def _():
                pltpu.make_async_copy(w_pad, wland.at[t], w_r.at[t]).start()

        @pl.when(jnp.logical_not(here))
        def _():
            copy = rcopy(w_pad, wland.at[t], w_s.at[i], w_r.at[t], dg, dt)
            if start:
                copy.start()
            else:
                copy.wait_send()

    def x_send(i, start):
        j = lax.rem(m + i, 8)
        dg, dt = member(j)
        copy = rcopy(x_in.at[:, window(j)], xland.at[m], x_s.at[j], x_r.at[m], dg, dt)
        if start:
            copy.start()
        else:
            copy.wait_send()

    loop(1, 8, lambda i: x_send(i, True))
    loop(1, 8, v_pass)
    pcopy.start()
    pl.semaphore_wait(round3, 1)
    loop(0, 16, lambda i: w_send(i, True))
    loop(0, 8, lambda i: k_relay(i * 2 + 1 - core).wait_recv())
    local[2].wait()
    qcopy.wait_recv()

    cz, ch = chip // 2, lax.rem(chip, 2)
    A, B = pl.ds(0, 512), pl.ds(512, 512)

    def ta_send(c, start):
        copy = rcopy(tsend.at[c, :, A], ta.at[lax.rem(c, 2), cz], ta_s.at[c], ta_r.at[lax.rem(c, 2) * 4 + cz],
                     g, (c // 2 * 2 + ch) * 2 + core)
        if start:
            copy.start()
        else:
            copy.wait_send()

    def ta_wait(h, z):
        rcopy(ta.at[h, z], ta.at[h, z], ta_s.at[0], ta_r.at[h * 4 + z], g, sib).wait_recv()

    def ta2_send():
        return rcopy(ta2.at[0], ta2.at[1], ta2_s.at[0], ta2_r.at[0], g, (cz * 2 + 1 - ch) * 2 + core)

    def tb_send(z, start):
        copy = rcopy(tsend.at[z * 2 + 1 - ch, :, B], tb.at[z], tb_s.at[z], tb_r.at[z],
                     g, (cz * 2 + 1 - ch) * 2 + core)
        if start:
            copy.start()
        else:
            copy.wait_send()

    def tb2_send(z, start):
        copy = rcopy(tbsum.at[z], tb2.at[cz], tb2_s.at[z], tb2_r.at[cz], g, (z * 2 + ch) * 2 + core)
        if start:
            copy.start()
        else:
            copy.wait_send()

    def os_send(i, start):
        copy = rcopy(osib.at[i], oswap.at[i], os_s.at[i], os_r.at[i], g, sib)
        if start:
            copy.start()
        else:
            copy.wait_send()

    def o_send(i, start):
        xx = lax.rem(x + i, 4)
        copy = rcopy(osend.at[xx], oland.at[x], o_s.at[xx], o_r.at[x], yl * 4 + xx, t)
        if start:
            copy.start()
        else:
            copy.wait_send()

    off = pl.multiple_of(lax.rem(x, 2) * 64, 64)

    def student_forward():
        loop(0, 16, lambda i: pltpu.make_async_copy(w_pad, wland.at[i], w_r.at[i]).wait())
        wz[...] = jnp.zeros_like(wz)
        bias = jnp.zeros((1, 1024), F32)
        for a in range(4):
            rows = [wland[4 * a + b].astype(F32) for b in range(4)]
            for r in rows:
                bias = bias + r[28:29]
            wz[pl.ds(off + a * 112, 112), :] = jnp.concatenate([r[:28] for r in rows], axis=0).astype(BF)
        brow[...] = bias
        local[4].wait()

        def fetch(j):
            @pl.when(j != m)
            def _():
                rcopy(xland.at[j], xland.at[j], x_s.at[0], x_r.at[j], g, sib).wait_recv()

            xt[j] = jnp.transpose(xland[j])

        def one(i, j, dst):
            fetch(j)
            for n in range(4):
                cols = slice(n * 256, (n + 1) * 256)
                o = jnp.dot(xland[j], wz[:, cols], preferred_element_type=F32) + brow[:, cols]
                dst[i, :, cols] = o.astype(BF)

        def theirs(i):
            xx = lax.rem(x + i, 4)
            one(xx, (1 - core) * 4 + xx, osib)
            os_send(xx, True)

        loop(0, 4, theirs)
        loop(0, 4, lambda i: one(i, core * 4 + i, osend))

    def output_sums():
        def one(i):
            xx = lax.rem(x + i, 4)
            rcopy(oswap.at[xx], oswap.at[xx], os_s.at[0], os_r.at[xx], g, sib).wait_recv()
            osend[xx] = (osend[xx].astype(F32) + oswap[xx].astype(F32)).astype(BF)

            @pl.when(i < 4)
            def _():
                o_send(i, True)

        loop(1, 5, one)
        oland[x] = osend[x]
        w2_send().start()

    def w2_send():
        return rcopy(wz, wz2, w2_s.at[0], w2_r.at[0], yl * 4 + lax.rem(x + 2, 4), t)

    def first_chunk(i):
        @pl.when(i == 0)
        def _():
            loop(0, 8, lambda k: v_relay(k * 2 + 1 - core).wait_recv())
            local[3].wait()
            pcopy.wait_recv()


    def chunk(i):
        z = lax.rem(cz + 1 + i // 2, 4)
        own = lax.rem(i, 2) == 1
        c = z * 2 + lax.rem(ch + 1 + i, 2)

        @pl.when(i == 2)
        def _():
            student_forward()

        @pl.when(i == 4)
        def _():
            output_sums()

        attend(core, c, qo.at[c], qs.at[c], keys, values, S, mx, acc, att, lambda: first_chunk(i))
        for n in range(4):
            cols = slice(n * 256, (n + 1) * 256)
            p = jnp.dot(att[:, :512], proj_o[:, cols], preferred_element_type=F32)
            p = p + jnp.dot(att[:, 512:], proj_s[:, cols], preferred_element_type=F32)
            tsend[c, :, cols] = p.astype(BF)

        @pl.when(i < 6)
        def _():
            ta_send(c, True)

        @pl.when(jnp.logical_not(own))
        def _():
            tb_send(z, True)

        @pl.when((i > 0) & jnp.logical_not(own))
        def _():
            zz = lax.rem(cz + i // 2, 4)
            rcopy(tb.at[zz], tb.at[zz], tb_s.at[0], tb_r.at[zz], g, sib).wait_recv()
            tbsum[zz] = (tsend[zz * 2 + ch, :, B].astype(F32) + tb[zz].astype(F32)).astype(BF)
            tb2_send(zz, True)

        @pl.when(i == 6)
        def _():
            total = tsend[c, :, A].astype(F32)
            for k in range(1, 4):
                zz = lax.rem(cz + k, 4)
                ta_wait(1 - ch, zz)
                total = total + ta[1 - ch, zz].astype(F32)
            ta2[0] = total.astype(BF)
            ta2_send().start()

    loop(0, 8, chunk)
    total = tsend[chip, :, A].astype(F32)
    for k in range(1, 4):
        zz = lax.rem(cz + k, 4)
        ta_wait(ch, zz)
        total = total + ta[ch, zz].astype(F32)
    ta2_send().wait_recv()
    total = total + ta2[1].astype(F32)
    tsum[:, :, A] = total.astype(BF).reshape(8, 16, 512)
    rcopy(tb.at[cz], tb.at[cz], tb_s.at[0], tb_r.at[cz], g, sib).wait_recv()
    total = tsend[chip, :, B].astype(F32) + tb[cz].astype(F32)
    for k in range(1, 4):
        zz = lax.rem(cz + k, 4)
        rcopy(tb2.at[zz], tb2.at[zz], tb2_s.at[0], tb2_r.at[zz], g, sib).wait_recv()
        total = total + tb2[zz].astype(F32)
    tsum[:, :, B] = total.astype(BF).reshape(8, 16, 512)

    def p_send(i, start):
        j = lax.rem(g + i, 8)
        copy = rcopy(tsum.at[j], pland.at[g], p_s.at[j], p_r.at[g], j, t)
        if start:
            copy.start()
        else:
            copy.wait_send()

    loop(1, 8, lambda i: p_send(i, True))
    pland[g] = tsum[g]

    def o_wait(i):
        j = lax.rem(x + i, 4)
        rcopy(oland.at[j], oland.at[j], o_s.at[0], o_r.at[j], g, sib).wait_recv()

    loop(1, 4, o_wait)

    def p_wait(i):
        j = lax.rem(g + i, 8)
        rcopy(pland.at[j], pland.at[j], p_s.at[0], p_r.at[j], g, sib).wait_recv()

    loop(1, 8, p_wait)
    keep = jnp.where(ids_in[...] < TEXT_IDS, 1.0, 0.0).astype(F32)
    keep = jnp.transpose(jnp.broadcast_to(keep, (128, 128)))
    for k in range(8):
        rows = slice(k * 16, (k + 1) * 16)
        o = oland[0, rows, :].astype(F32)
        for j in range(1, 4):
            o = o + oland[j, rows, :].astype(F32)
        paired = pland[own_in[k]].astype(F32)
        kk = jnp.concatenate([keep[rows]] * 8, axis=1)
        eland[m, rows, :] = (kk * (o - paired)).astype(BF)

    def cols_of(n):
        return pl.ds(n * 512, 512)

    def e_next(dx, k, n):
        here = eland.at[m, :, cols_of(n)]
        return rcopy(here, here, e_s.at[k * 2 + n], e_r.at[k * 2 + n], yl * 4 + lax.rem(x + dx, 4), t)

    def e_far(dx, k, n):
        here = eland.at[core * 4 + lax.rem(x + 4 - dx, 4), pl.ds(k * 64, 64), cols_of(n)]
        return rcopy(here, here, f_s.at[k * 2 + n], f_r.at[k * 2 + n], yl * 4 + lax.rem(x + dx, 4), t)

    def e_relay(dx, n):
        xx = lax.rem(x + dx, 4)
        here = eland.at[core * 4 + xx, :, cols_of(n)]
        return rcopy(here, here, re_s.at[xx * 2 + n], re_r.at[xx * 2 + n], g, sib)

    for n in range(2):
        e_next(1, 0, n).start()
        e_next(3, 1, n).start()
        e_relay(0, n).start()

    row = lax.broadcasted_iota(jnp.int32, (32, 512), 0)

    def g_send(i, n, start):
        here = (core == yl) & (i == t)
        src, dst = wsend.at[i, :, cols_of(n)], wgland.at[src16, :, cols_of(n)]

        if start:
            @pl.when(here)
            def _():
                pltpu.make_async_copy(src, dst, g_r.at[n * 16 + src16]).start()

        @pl.when(jnp.logical_not(here))
        def _():
            copy = rcopy(src, dst, g_s.at[n * 16 + i], g_r.at[n * 16 + src16], core * 4 + x, i)
            if start:
                copy.start()
            else:
                copy.wait_send()

    for n in range(2):
        e_next(1, 0, n).wait_recv()
        e_far(1, 0, n).start()
        e_relay(3, n).start()
        e_next(3, 1, n).wait_recv()
        e_far(3, 1, n).start()
        e_relay(1, n).start()
        e_far(1, 0, n).wait_recv()
        e_far(3, 1, n).wait_recv()
        e_relay(2, n).start()
        for k in range(4):
            e_relay(k, n).wait_recv()

        for u in range(2):
            cols = slice(n * 512 + u * 256, n * 512 + (u + 1) * 256)
            total = jnp.zeros((512, 256), F32)
            eb = jnp.zeros((8, 256), F32)
            lb = jnp.zeros((8, 256), F32)
            for j in range(8):
                e = eland[j, :, cols]
                total = total + jnp.dot(xt[j], e, preferred_element_type=F32)
                ef = e.astype(F32)
                for r in range(16):
                    er = ef[r * 8:(r + 1) * 8]
                    eb = eb + er
                    lb = lb + er * er
            wg[:, cols] = total
            esum = jnp.sum(eb, axis=0, keepdims=True)
            lsum = jnp.sum(lb, axis=0, keepdims=True)
            ehi = esum.astype(BF).astype(F32)
            lhi = lsum.astype(BF).astype(F32)
            for r, v in enumerate([ehi, esum - ehi, lhi, lsum - lhi]):
                extra[r:r + 1, cols] = v
        cols = slice(n * 512, (n + 1) * 512)
        for i in range(16):
            v = wg[pl.ds(off + (28 * i) // 8 * 8, 32), cols]
            if (28 * i) % 8:
                v = pltpu.roll(v, 28, 0)
            for r in range(4):
                v = jnp.where(row == 28 + r, extra[r:r + 1, cols], v)
            wsend[i, :, cols] = v.astype(BF)
        loop(0, 16, lambda i: g_send(lax.rem(t + i, 16), n, True))

    m2 = core * 4 + lax.rem(x + 2, 4)

    def i_send(k, j, slot, start):
        dg, dt = member(j)
        copy = rcopy(igsend.at[k], igland.at[slot], i_s.at[k], i_r.at[slot], dg, dt)
        if start:
            copy.start()
        else:
            copy.wait_send()

    pairs = [(1, wz, m), (3, wz, m), (0, wz, m), (0, wz2, m2)]
    ig_own = [pltpu.make_async_copy(igsend.at[4], igland.at[m], i_r.at[m]),
              pltpu.make_async_copy(igsend.at[6], igland.at[m2], i_r.at[m2])]
    for k, (dx, w, slot) in enumerate(pairs):
        xx = lax.rem(x + dx, 4)
        mine, other = core * 4 + xx, (1 - core) * 4 + xx
        if k == 3:
            w2_send().wait_recv()
        e = jnp.concatenate([eland[mine], eland[other]], axis=0)
        ig = lax.dot_general(e, w[...], (((1,), (1,)), ((), ())), preferred_element_type=F32).astype(BF)
        igsend[2 * k] = ig[:128]
        igsend[2 * k + 1] = ig[128:]
        if dx:
            i_send(2 * k, mine, slot, True)
        else:
            ig_own[k - 2].start()
        i_send(2 * k + 1, other, slot, True)

    def g_wait(i):
        for n in range(2):
            here = wgland.at[i, :, cols_of(n)]
            pltpu.make_async_copy(wsend.at[i, :, cols_of(n)], here, g_r.at[n * 16 + i]).wait()

    loop(0, 16, g_wait)
    for copy in ig_own:
        copy.wait()

    def i_wait(i):
        @pl.when((i != m) & (i != m2))
        def _():
            rcopy(igland.at[i], igland.at[i], i_s.at[0], i_r.at[i], g, sib).wait_recv()

    loop(0, 8, i_wait)
    loop(1, 8, lambda i: k_send(i, False))
    loop(1, 8, lambda i: v_send(i, False))
    qcopy.wait_send()
    pcopy.wait_send()
    loop(0, 8, lambda i: k_relay(i * 2 + core).wait_send())
    loop(0, 8, lambda i: v_relay(i * 2 + core).wait_send())
    w2_send().wait_send()
    loop(0, 16, lambda i: w_send(i, False))
    loop(1, 8, lambda i: x_send(i, False))
    loop(0, 4, lambda i: os_send(i, False))
    loop(1, 4, lambda i: o_send(i, False))
    loop(2, 8, lambda i: ta_send(lax.rem(cz * 2 + i, 8), False))
    loop(0, 4, lambda i: tb_send(i, False))
    loop(1, 4, lambda i: tb2_send(lax.rem(cz + i, 4), False))
    ta2_send().wait_send()
    loop(1, 8, lambda i: p_send(i, False))
    for n in range(2):
        for k, dx in ((0, 1), (1, 3)):
            e_next(dx, k, n).wait_send()
            e_far(dx, k, n).wait_send()
        for dx in range(4):
            e_relay(dx, n).wait_send()
        loop(0, 16, lambda i: g_send(i, n, False))
    for k, (dx, w, slot) in enumerate(pairs):
        xx = lax.rem(x + dx, 4)
        if dx:
            i_send(2 * k, core * 4 + xx, slot, False)
        i_send(2 * k + 1, (1 - core) * 4 + xx, slot, False)


def finish(wgland, igland, wg_out, bias_out, loss_out, ig_out):
    d = lax.axis_index("grp") * 16 + lax.axis_index("tp")
    total = wgland[0].astype(F32)
    for i in range(1, 16):
        total = total + wgland[i].astype(F32)
    wg_out[...] = total[:28]
    small = total[24:32]
    loss_out[...] = jnp.sum(small[6:8], axis=(0, 1), keepdims=True) / 32768.0
    both = jnp.broadcast_to(small[4:5] + small[5:6], (8, 1024))
    both = pltpu.roll(both, lax.rem(1024 - d * 8, 1024), 1)
    bias_out[...] = both[0:1, 0:8]
    for b in range(4):
        ig_out[:, b * 896:b * 896 + 384] = igland[2 * b, :, :384]
        ig_out[:, b * 896 + 384:b * 896 + 512] = igland[2 * b, :, 384:] + igland[2 * b + 1, :, :128]
        ig_out[:, b * 896 + 512:(b + 1) * 896] = igland[2 * b + 1, :, 128:]


def on_device(queries, keys_values, projector, ownership, token_ids, student_input, student_weight, student_bias):
    hbm = pl.BlockSpec(memory_space=pl.ANY)
    vmem = pl.BlockSpec(memory_space=pltpu.VMEM)
    smem = pl.BlockSpec(memory_space=pltpu.SMEM)
    dma = pltpu.SemaphoreType.DMA
    V = pltpu.VMEM
    wgland, igland = pl.pallas_call(
        kernel,
        out_shape=(jax.ShapeDtypeStruct((16, 32, 1024), BF), jax.ShapeDtypeStruct((8, 128, 512), BF)),
        in_specs=[hbm, hbm, hbm, smem, vmem, hbm, vmem, vmem],
        out_specs=(hbm, hbm),
        scratch_shapes=[
            V((8, 128, 512), BF), V((8, 128, 512), BF), V((2048, 128), BF), V((2048, 128), BF),
            V((1024, 2048), F32), V((1024, 128), F32), V((1024, 256), F32), V((128, 1024), BF),
            V((512, 1024), BF), V((512, 1024), BF), V((8, 128, 1024), BF),
            V((2, 4, 128, 512), BF), V((2, 128, 512), BF), V((4, 128, 512), BF), V((4, 128, 512), BF),
            V((4, 128, 512), BF), V((8, 16, 1024), BF), V((8, 16, 1024), BF),
            V((8, 128, 512), BF), V((8, 512, 128), BF), V((32, 1024), BF), V((16, 32, 1024), BF),
            V((512, 1024), BF), V((512, 1024), BF), V((1, 1024), F32),
            V((4, 128, 1024), BF), V((4, 128, 1024), BF), V((4, 128, 1024), BF), V((4, 128, 1024), BF),
            V((8, 128, 1024), BF), V((512, 1024), F32), V((8, 1024), F32), V((16, 32, 1024), BF), V((8, 128, 512), BF),
            dma((5,)), dma((2,)), dma((2,)), dma((8,)), dma((16,)), dma((8,)), dma((16,)), dma((8,)), dma((8,)),
            dma((16,)), dma((16,)), dma((8,)), dma((8,)), dma((4,)), dma((4,)), dma((4,)), dma((4,)),
            dma((8,)), dma((8,)), dma((4,)), dma((4,)), dma((1,)), dma((1,)), dma((4,)), dma((4,)),
            dma((8,)), dma((8,)), dma((4,)), dma((4,)), dma((4,)), dma((4,)), dma((8,)), dma((8,)),
            dma((32,)), dma((32,)), dma((8,)), dma((8,)), dma((1,)), dma((1,)),
            pltpu.SemaphoreType.REGULAR, pltpu.SemaphoreType.REGULAR,
        ],
        compiler_params=pltpu.CompilerParams(
            collective_id=0, has_side_effects=True, vmem_limit_bytes=60 * 2 ** 20),
        cost_estimate=pl.CostEstimate(flops=9 * 10 ** 9, bytes_accessed=8 * 10 ** 6, transcendentals=9 * 10 ** 6),
    )(queries.reshape(8, 2, 128, 512), keys_values[0], projector, ownership, token_ids.reshape(1, 128),
      student_input, student_weight, student_bias.reshape(1, 8))
    wg, bias, loss, ig = pl.pallas_call(
        finish,
        out_shape=(jax.ShapeDtypeStruct((28, 1024), F32), jax.ShapeDtypeStruct((1, 8), F32),
                   jax.ShapeDtypeStruct((1, 1), F32), jax.ShapeDtypeStruct((128, 3584), BF)),
        in_specs=[vmem, vmem],
        out_specs=(vmem, vmem, vmem, vmem),
        compiler_params=pltpu.CompilerParams(vmem_limit_bytes=32 * 2 ** 20),
    )(wgland, igland)
    return loss.reshape(()), wg, bias.reshape(8), ig


def solution(mesh):
    return jax.shard_map(
        on_device,
        mesh=mesh,
        in_specs=(
            P("grp", None, "tp"), P("grp", "tp", None), P("tp", None), P(), P(("grp", "tp")),
            P(("grp", "tp"), None), P(("grp", "tp"), None), P(("grp", "tp")),
        ),
        out_specs=(P(), P(("grp", "tp"), None), P(("grp", "tp")), P(("grp", "tp"), None)),
        check_vma=False,
    )
```

```python
import functools

import jax
import jax.numpy as jnp
from jax import lax
from jax.experimental import pallas as pl
from jax.experimental.pallas import tpu as pltpu
from jax.sharding import PartitionSpec as P

MESH = pl.DeviceIdType.MESH
TEXT_IDS = 151643
SCALE = 128 ** -0.5 * 1.4426950408889634
BF = jnp.bfloat16
F32 = jnp.float32


def rcopy(src, dst, send_sem, recv_sem, grp, tp):
    return pltpu.make_async_remote_copy(
        src_ref=src, dst_ref=dst, send_sem=send_sem, recv_sem=recv_sem,
        device_id=(grp, tp), device_id_type=MESH)


def loop(first, last, body):
    lax.fori_loop(first, last, lambda i, carry: (body(i), carry)[1], 0)


def attend(core, c, qo, qs, keys, values, S, mx, acc, out, between):
    q = jnp.concatenate([r[:, h * 128:(h + 1) * 128] for r in (qo, qs) for h in range(4)], axis=0)

    def score(j, T, masked):
        at = pl.ds(pl.multiple_of(j * 256, 256), T)
        if masked:
            row = lax.broadcasted_iota(jnp.int32, (128, T), 0) + core * 128
            keep = row >= lax.broadcasted_iota(jnp.int32, (128, T), 1)
        s_all = lax.dot_general(q, keys[at, :], (((1,), (1,)), ((), ())), preferred_element_type=F32)
        for h in range(8):
            hr = slice(h * 128, (h + 1) * 128)
            s = s_all[hr]
            if masked:
                s = jnp.where(keep, s, -1e30)
            S[hr, at] = s
            m = mx[hr, :]
            for w in range(T // 128):
                m = jnp.maximum(m, s[:, w * 128:(w + 1) * 128])
            if masked:
                m = jnp.broadcast_to(jnp.max(m, axis=1, keepdims=True) * SCALE, (128, 128))
            mx[hr, :] = m

    mx[...] = jnp.full_like(mx, -1e30)
    loop(0, c // 2, lambda j: score(2 * j, 512, False))
    loop(0, lax.rem(c, 2), lambda j: score(c - 1, 256, False))
    score(c, 256, True)
    acc[...] = jnp.zeros_like(acc)
    between()

    def weigh(off, W):
        vt = values[pl.ds(off, W), :]
        vt = jnp.concatenate([vt, jnp.ones_like(vt)], axis=1)
        ps = []
        for h in range(8):
            hr = slice(h * 128, (h + 1) * 128)
            m = mx[hr, :]
            ps.append(jnp.concatenate(
                [jnp.exp2(S[hr, pl.ds(pl.multiple_of(off + w * 128, 128), 128)] * SCALE - m).astype(BF)
                 for w in range(W // 128)], axis=1))
        acc[...] += jnp.dot(jnp.concatenate(ps, axis=0), vt, preferred_element_type=F32)

    n = c + 1
    loop(0, n // 4, lambda j: weigh(pl.multiple_of(j * 1024, 1024), 1024))
    loop(0, lax.rem(n // 2, 2), lambda j: weigh(pl.multiple_of(n // 4 * 1024, 512), 512))
    loop(0, lax.rem(n, 2), lambda j: weigh(pl.multiple_of((n - 1) * 256, 256), 256))
    for h in range(8):
        a = acc[h * 128:(h + 1) * 128, :]
        out[:, h * 128:(h + 1) * 128] = (a[:, :128] / a[:, 128:]).astype(BF)


def kernel(q_in, kv_in, proj_in, own_in, ids_in, x_in, w_in, b_in,
           wgland, igland,
           qo, qs, keys, values, S, mx, acc, att, proj_o, proj_s, tsend, ta, ta2, tb, tbsum, tb2, tsum, pland,
           xland, xt, w_pad, wland, wz, brow, osib, oswap, osend, oland, eland, wg, wsend, igsend,
           l_sem, qp_s, qp_r, k_s, k_r, v_s, v_r, rk_s, rv_s, w_s, w_r, x_s, x_r, os_s, os_r, o_s, o_r,
           ta_s, ta_r, tb_s, tb_r, ta2_s, ta2_r, tb2_s, tb2_r, p_s, p_r, e_s, e_r, re_s, re_r, g_s, g_r, i_s, i_r, round2, round3):
    g = lax.axis_index("grp")
    t = lax.axis_index("tp")
    x, yl = lax.rem(g, 4), g // 4
    core, chip = lax.rem(t, 2), t // 2
    sib = chip * 2 + 1 - core
    m = core * 4 + x
    src16 = chip * 2 + yl

    def member(i):
        return yl * 4 + lax.rem(i, 4), chip * 2 + i // 4

    def plane(i):
        return lax.rem(i, 2) * 4 + x, (i // 2) * 2 + yl

    own_kv = pl.ds(pl.multiple_of(t * 128, 128), 128)
    kcol = pl.ds(pl.multiple_of(chip * 128, 128), 128)
    vcol = pl.ds(pl.multiple_of(1024 + chip * 128, 128), 128)

    def window(i):
        return pl.ds(pl.multiple_of((i // 2) * 896 + lax.rem(i, 2) * 384, 128), 512)

    local = [
        pltpu.make_async_copy(kv_in.at[:, kcol], keys.at[own_kv, :], l_sem.at[0]),
        pltpu.make_async_copy(kv_in.at[:, vcol], values.at[own_kv, :], l_sem.at[1]),
        pltpu.make_async_copy(q_in.at[:, core], qo, l_sem.at[2]),
        pltpu.make_async_copy(proj_in, proj_o, l_sem.at[3]),
        pltpu.make_async_copy(x_in.at[:, window(m)], xland.at[m], l_sem.at[4]),
    ]
    for copy in local:
        copy.start()

    lane = lax.broadcasted_iota(jnp.int32, (4, 1024), 1) - (g * 16 + t) * 8
    first = lax.broadcasted_iota(jnp.int32, (4, 1024), 0) == 0
    b_row = jnp.zeros((4, 1024), F32)
    for r in range(8):
        b_row = jnp.where(first & (lane == r), jnp.broadcast_to(b_in[:, r:r + 1].astype(F32), (4, 1024)), b_row)
    w_pad[...] = jnp.concatenate([w_in[...].astype(F32), b_row], axis=0).astype(BF)

    barrier = pltpu.get_barrier_semaphore()

    def greet(sem):
        def tell(grp, tp):
            pl.semaphore_signal(sem, inc=1, device_id=(grp, tp), device_id_type=MESH)

        loop(1, 8, lambda i: tell(g, lax.rem(chip + i, 8) * 2 + core))
        tell(g, sib)
        loop(1, 4, lambda i: tell(yl * 4 + lax.rem(x + i, 4), t))
        tell((1 - yl) * 4 + x, t)

    greet(barrier)
    pl.semaphore_wait(barrier, 12)

    def kv_cols(q):
        return (pl.ds(pl.multiple_of(q * 128, 128), 128),
                pl.ds(pl.multiple_of(1024 + q * 128, 128), 128))

    def k_send(i, start):
        q = lax.rem(chip + i * (1 + 6 * core), 8)
        a = rcopy(kv_in.at[:, kv_cols(q)[0]], keys.at[own_kv, :], k_s.at[q], k_r.at[t], g, q * 2 + core)
        if start:
            a.start()
        else:
            a.wait_send()

    def v_send(i, start):
        q = lax.rem(chip + i * (1 + 6 * core), 8)
        a = rcopy(kv_in.at[:, kv_cols(q)[1]], values.at[own_kv, :], v_s.at[q], v_r.at[t], g, q * 2 + core)
        if start:
            a.start()
        else:
            a.wait_send()

    loop(1, 8, lambda i: k_send(i, True))
    qcopy = rcopy(q_in.at[:, 1 - core], qs, qp_s.at[0], qp_r.at[0], g, sib)
    pcopy = rcopy(proj_in, proj_s, qp_s.at[1], qp_r.at[1], g, sib)
    qcopy.start()
    loop(1, 8, lambda i: v_send(i, True))
    greet(round2)

    def rows_of(src):
        return pl.ds(pl.multiple_of(src * 128, 128), 128)

    def k_relay(src):
        rows = rows_of(src)
        return rcopy(keys.at[rows, :], keys.at[rows, :], rk_s.at[src // 2], k_r.at[src], g, sib)

    def v_relay(src):
        rows = rows_of(src)
        return rcopy(values.at[rows, :], values.at[rows, :], rv_s.at[src // 2], v_r.at[src], g, sib)

    def k_pass(i):
        src = lax.rem(chip + i * (7 - 6 * core), 8) * 2 + core
        k_relay(src).wait_recv()
        k_relay(src).start()

    def v_pass(i):
        src = lax.rem(chip + i * (7 - 6 * core), 8) * 2 + core
        v_relay(src).wait_recv()
        v_relay(src).start()

    local[0].wait()
    k_relay(t).start()
    local[1].wait()
    v_relay(t).start()
    loop(1, 8, k_pass)
    pl.semaphore_wait(round2, 12)
    pl.semaphore_signal(round3, inc=1, device_id=(g, sib), device_id_type=MESH)

    def w_send(i, start):
        i = lax.rem(src16 + i, 16)
        dg, dt = plane(i)
        here = (i == src16) & (core == yl)

        if start:
            @pl.when(here)
            def _():
                pltpu.make_async_copy(w_pad, wland.at[t], w_r.at[t]).start()

        @pl.when(jnp.logical_not(here))
        def _():
            copy = rcopy(w_pad, wland.at[t], w_s.at[i], w_r.at[t], dg, dt)
            if start:
                copy.start()
            else:
                copy.wait_send()

    def x_send(i, start):
        j = lax.rem(m + i, 8)
        dg, dt = member(j)
        copy = rcopy(x_in.at[:, window(j)], xland.at[m], x_s.at[j], x_r.at[m], dg, dt)
        if start:
            copy.start()
        else:
            copy.wait_send()

    loop(1, 8, lambda i: x_send(i, True))
    loop(1, 8, v_pass)
    pcopy.start()
    pl.semaphore_wait(round3, 1)
    loop(0, 16, lambda i: w_send(i, True))
    loop(0, 8, lambda i: k_relay(i * 2 + 1 - core).wait_recv())
    local[2].wait()
    qcopy.wait_recv()

    cz, ch = chip // 2, lax.rem(chip, 2)
    A, B = pl.ds(0, 512), pl.ds(512, 512)

    def ta_send(c, start):
        copy = rcopy(tsend.at[c, :, A], ta.at[lax.rem(c, 2), cz], ta_s.at[c], ta_r.at[lax.rem(c, 2) * 4 + cz],
                     g, (c // 2 * 2 + ch) * 2 + core)
        if start:
            copy.start()
        else:
            copy.wait_send()

    def ta_wait(h, z):
        rcopy(ta.at[h, z], ta.at[h, z], ta_s.at[0], ta_r.at[h * 4 + z], g, sib).wait_recv()

    def ta2_send():
        return rcopy(ta2.at[0], ta2.at[1], ta2_s.at[0], ta2_r.at[0], g, (cz * 2 + 1 - ch) * 2 + core)

    def tb_send(z, start):
        copy = rcopy(tsend.at[z * 2 + 1 - ch, :, B], tb.at[z], tb_s.at[z], tb_r.at[z],
                     g, (cz * 2 + 1 - ch) * 2 + core)
        if start:
            copy.start()
        else:
            copy.wait_send()

    def tb2_send(z, start):
        copy = rcopy(tbsum.at[z], tb2.at[cz], tb2_s.at[z], tb2_r.at[cz], g, (z * 2 + ch) * 2 + core)
        if start:
            copy.start()
        else:
            copy.wait_send()

    def os_send(i, start):
        copy = rcopy(osib.at[i], oswap.at[i], os_s.at[i], os_r.at[i], g, sib)
        if start:
            copy.start()
        else:
            copy.wait_send()

    def o_send(i, start):
        xx = lax.rem(x + i, 4)
        copy = rcopy(osend.at[xx], oland.at[x], o_s.at[xx], o_r.at[x], yl * 4 + xx, t)
        if start:
            copy.start()
        else:
            copy.wait_send()

    off = pl.multiple_of(lax.rem(x, 2) * 64, 64)

    def student_forward():
        loop(0, 16, lambda i: pltpu.make_async_copy(w_pad, wland.at[i], w_r.at[i]).wait())
        wz[...] = jnp.zeros_like(wz)
        bias = jnp.zeros((1, 1024), F32)
        for a in range(4):
            rows = [wland[4 * a + b].astype(F32) for b in range(4)]
            for r in rows:
                bias = bias + r[28:29]
            wz[pl.ds(off + a * 112, 112), :] = jnp.concatenate([r[:28] for r in rows], axis=0).astype(BF)
        brow[...] = bias
        local[4].wait()

        def fetch(j):
            @pl.when(j != m)
            def _():
                rcopy(xland.at[j], xland.at[j], x_s.at[0], x_r.at[j], g, sib).wait_recv()


        def one(i, j, dst):
            fetch(j)
            for n in range(4):
                cols = slice(n * 256, (n + 1) * 256)
                o = jnp.dot(xland[j], wz[:, cols], preferred_element_type=F32) + brow[:, cols]
                dst[i, :, cols] = o.astype(BF)

        def theirs(i):
            xx = lax.rem(x + i, 4)
            one(xx, (1 - core) * 4 + xx, osib)
            os_send(xx, True)

        loop(0, 4, theirs)
        loop(0, 4, lambda i: one(i, core * 4 + i, osend))

    def output_sums():
        def one(i):
            xx = lax.rem(x + i, 4)
            rcopy(oswap.at[xx], oswap.at[xx], os_s.at[0], os_r.at[xx], g, sib).wait_recv()
            osend[xx] = (osend[xx].astype(F32) + oswap[xx].astype(F32)).astype(BF)

            @pl.when(i < 4)
            def _():
                o_send(i, True)

        loop(1, 5, one)
        oland[x] = osend[x]

    def first_chunk(i):
        @pl.when(i == 0)
        def _():
            loop(0, 8, lambda k: v_relay(k * 2 + 1 - core).wait_recv())
            local[3].wait()
            pcopy.wait_recv()


    def chunk(i):
        k = jnp.where(i < 3, i + 1, jnp.where(i < 5, i - 2, jnp.where(i == 6, 3, 0)))
        other = (i < 3) | (i == 5)
        z = lax.rem(cz + k * (1 + 2 * core), 4)
        c = z * 2 + lax.rem(ch + jnp.where(other, 1, 0), 2)

        @pl.when(i == 4)
        def _():
            student_forward()

        @pl.when(i == 6)
        def _():
            output_sums()

        attend(core, c, qo.at[c], qs.at[c], keys, values, S, mx, acc, att, lambda: first_chunk(i))
        for n in range(4):
            cols = slice(n * 256, (n + 1) * 256)
            p = jnp.dot(att[:, :512], proj_o[:, cols], preferred_element_type=F32)
            p = p + jnp.dot(att[:, 512:], proj_s[:, cols], preferred_element_type=F32)
            tsend[c, :, cols] = p.astype(BF)

        @pl.when(k > 0)
        def _():
            ta_send(c, True)

        @pl.when(other)
        def _():
            tb_send(z, True)

        @pl.when(jnp.logical_not(other) & (k > 0))
        def _():
            rcopy(tb.at[z], tb.at[z], tb_s.at[0], tb_r.at[z], g, sib).wait_recv()
            tbsum[z] = (tsend[c, :, B].astype(F32) + tb[z].astype(F32)).astype(BF)
            tb2_send(z, True)

        @pl.when(i == 5)
        def _():
            total = tsend[c, :, A].astype(F32)
            for k in range(1, 4):
                zz = lax.rem(cz + k, 4)
                ta_wait(1 - ch, zz)
                total = total + ta[1 - ch, zz].astype(F32)
            ta2[0] = total.astype(BF)
            ta2_send().start()

    loop(0, 8, chunk)
    for j in range(8):
        xt[:, j * 128:(j + 1) * 128] = jnp.transpose(xland[j])
    total = tsend[chip, :, A].astype(F32)
    for k in range(1, 4):
        zz = lax.rem(cz + k, 4)
        ta_wait(ch, zz)
        total = total + ta[ch, zz].astype(F32)
    ta2_send().wait_recv()
    total = total + ta2[1].astype(F32)
    tsum[:, :, A] = total.astype(BF).reshape(8, 16, 512)
    rcopy(tb.at[cz], tb.at[cz], tb_s.at[0], tb_r.at[cz], g, sib).wait_recv()
    total = tsend[chip, :, B].astype(F32) + tb[cz].astype(F32)
    for k in range(1, 4):
        zz = lax.rem(cz + k, 4)
        rcopy(tb2.at[zz], tb2.at[zz], tb2_s.at[0], tb2_r.at[zz], g, sib).wait_recv()
        total = total + tb2[zz].astype(F32)
    tsum[:, :, B] = total.astype(BF).reshape(8, 16, 512)

    def p_send(i, start):
        j = lax.rem(g + i, 8)
        copy = rcopy(tsum.at[j], pland.at[g], p_s.at[j], p_r.at[g], j, t)
        if start:
            copy.start()
        else:
            copy.wait_send()

    loop(1, 8, lambda i: p_send(i, True))
    pland[g] = tsum[g]

    def o_wait(i):
        j = lax.rem(x + i, 4)
        rcopy(oland.at[j], oland.at[j], o_s.at[0], o_r.at[j], g, sib).wait_recv()

    loop(1, 4, o_wait)

    def p_wait(i):
        j = lax.rem(g + i, 8)
        rcopy(pland.at[j], pland.at[j], p_s.at[0], p_r.at[j], g, sib).wait_recv()

    loop(1, 8, p_wait)
    keep = jnp.where(ids_in[...] < TEXT_IDS, 1.0, 0.0).astype(F32)
    keep = jnp.transpose(jnp.broadcast_to(keep, (128, 128)))
    keep = jnp.concatenate([keep, keep], axis=1)

    def errors(n):
        cols = slice(n * 256, (n + 1) * 256)
        for k in range(8):
            rows = slice(k * 16, (k + 1) * 16)
            o = oland[0, rows, cols].astype(F32)
            for j in range(1, 4):
                o = o + oland[j, rows, cols].astype(F32)
            eland[m, rows, cols] = (keep[rows] * (o - pland[own_in[k], :, cols].astype(F32))).astype(BF)

    def cols_of(n):
        return pl.ds(n * 256, 256)

    def e_send(dx, n):
        here = eland.at[m, :, cols_of(n)]
        return rcopy(here, here, e_s.at[dx * 4 + n], e_r.at[dx * 4 + n], yl * 4 + lax.rem(x + dx, 4), t)

    def e_relay(dx, n):
        xx = lax.rem(x + dx, 4)
        here = eland.at[core * 4 + xx, :, cols_of(n)]
        return rcopy(here, here, re_s.at[xx * 4 + n], re_r.at[xx * 4 + n], g, sib)

    def e_begin(n):
        errors(n)
        for dx in (2, 1, 3):
            e_send(dx, n).start()
        e_relay(0, n).start()

    def e_pass(n):
        for dx in (1, 3, 2):
            e_send(dx, n).wait_recv()
            e_relay(4 - dx, n).start()

    row = lax.broadcasted_iota(jnp.int32, (32, 256), 0)

    def g_send(i, n, start):
        here = (core == yl) & (i == t)
        src, dst = wsend.at[i, :, cols_of(n)], wgland.at[src16, :, cols_of(n)]

        if start:
            @pl.when(here)
            def _():
                pltpu.make_async_copy(src, dst, g_r.at[n * 16 + src16]).start()

        @pl.when(jnp.logical_not(here))
        def _():
            copy = rcopy(src, dst, g_s.at[n * 16 + i], g_r.at[n * 16 + src16], core * 4 + x, i)
            if start:
                copy.start()
            else:
                copy.wait_send()

    def weight_grad(n):
        if n < 3:
            for k in range(4):
                e_relay(k, n).wait_recv()
        cols = slice(n * 256, (n + 1) * 256)
        eb = jnp.zeros((8, 256), F32)
        lb = jnp.zeros((8, 256), F32)
        for j in range(8):
            ef = eland[j, :, cols].astype(F32)
            for r in range(16):
                er = ef[r * 8:(r + 1) * 8]
                eb = eb + er
                lb = lb + er * er
        wg[...] = jnp.dot(xt[...], eland[:, :, cols].reshape(1024, 256), preferred_element_type=F32)
        esum = jnp.sum(eb, axis=0, keepdims=True)
        lsum = jnp.sum(lb, axis=0, keepdims=True)
        ehi = esum.astype(BF).astype(F32)
        lhi = lsum.astype(BF).astype(F32)
        for i in range(16):
            v = wg[pl.ds(off + (28 * i) // 8 * 8, 32), :]
            if (28 * i) % 8:
                v = pltpu.roll(v, 28, 0)
            for r, e in enumerate([ehi, esum - ehi, lhi, lsum - lhi]):
                v = jnp.where(row == 28 + r, e, v)
            wsend[i, :, cols] = v.astype(BF)
        loop(0, 16, lambda i: g_send(lax.rem(t + i, 16), n, True))

    for n in range(4):
        e_begin(n)
    for n in range(3):
        e_pass(n)
        weight_grad(n)
    e_pass(3)
    for k in range(4):
        e_relay(k, 3).wait_recv()

    def i_send(k, j, slot, start):
        dg, dt = member(j)
        copy = rcopy(igsend.at[k], igland.at[slot], i_s.at[k], i_r.at[slot], dg, dt)
        if start:
            copy.start()
        else:
            copy.wait_send()

    pairs = [(2, wz, m), (1, wz, m), (3, wz, m), (0, wz, m)]
    ig_own = [pltpu.make_async_copy(igsend.at[6], igland.at[m], i_r.at[m])]
    for k, (dx, w, slot) in enumerate(pairs):
        if k == 3:
            weight_grad(3)
        xx = lax.rem(x + dx, 4)
        mine, other = core * 4 + xx, (1 - core) * 4 + xx
        e = jnp.concatenate([eland[mine], eland[other]], axis=0)
        ig = lax.dot_general(e, w[...], (((1,), (1,)), ((), ())), preferred_element_type=F32).astype(BF)
        igsend[2 * k] = ig[:128]
        igsend[2 * k + 1] = ig[128:]
        if dx:
            i_send(2 * k, mine, slot, True)
        else:
            ig_own[0].start()
        i_send(2 * k + 1, other, slot, True)

    def g_wait(i):
        for n in range(4):
            here = wgland.at[i, :, cols_of(n)]
            pltpu.make_async_copy(wsend.at[i, :, cols_of(n)], here, g_r.at[n * 16 + i]).wait()

    loop(0, 16, g_wait)
    for copy in ig_own:
        copy.wait()

    def i_wait(i):
        @pl.when(i != m)
        def _():
            rcopy(igland.at[i], igland.at[i], i_s.at[0], i_r.at[i], g, sib).wait_recv()

    loop(0, 8, i_wait)
    loop(1, 8, lambda i: k_send(i, False))
    loop(1, 8, lambda i: v_send(i, False))
    qcopy.wait_send()
    pcopy.wait_send()
    loop(0, 8, lambda i: k_relay(i * 2 + core).wait_send())
    loop(0, 8, lambda i: v_relay(i * 2 + core).wait_send())
    loop(0, 16, lambda i: w_send(i, False))
    loop(1, 8, lambda i: x_send(i, False))
    loop(0, 4, lambda i: os_send(i, False))
    loop(1, 4, lambda i: o_send(i, False))
    loop(2, 8, lambda i: ta_send(lax.rem(cz * 2 + i, 8), False))
    loop(0, 4, lambda i: tb_send(i, False))
    loop(1, 4, lambda i: tb2_send(lax.rem(cz + i, 4), False))
    ta2_send().wait_send()
    loop(1, 8, lambda i: p_send(i, False))
    for n in range(4):
        for dx in (1, 2, 3):
            e_send(dx, n).wait_send()
        for dx in range(4):
            e_relay(dx, n).wait_send()
        loop(0, 16, lambda i: g_send(i, n, False))
    for k, (dx, w, slot) in enumerate(pairs):
        xx = lax.rem(x + dx, 4)
        if dx:
            i_send(2 * k, core * 4 + xx, slot, False)
        i_send(2 * k + 1, (1 - core) * 4 + xx, slot, False)


def finish(wg_in, ig_in, wg_out, bias_out, loss_out, ig_out, wgland, igland, sem):
    d = lax.axis_index("grp") * 16 + lax.axis_index("tp")
    wg_copy = pltpu.make_async_copy(wg_in, wgland, sem.at[0])
    ig_copy = pltpu.make_async_copy(ig_in, igland, sem.at[1])
    wg_copy.start()
    ig_copy.start()
    wg_copy.wait()
    total = wgland[0].astype(F32)
    for i in range(1, 16):
        total = total + wgland[i].astype(F32)
    wg_out[...] = total[:28]
    small = total[24:32]
    loss_out[...] = jnp.sum(small[6:8], axis=(0, 1), keepdims=True) / 32768.0
    both = jnp.broadcast_to(small[4:5] + small[5:6], (8, 1024))
    both = pltpu.roll(both, lax.rem(1024 - d * 8, 1024), 1)
    bias_out[...] = both[0:1, 0:8]
    ig_copy.wait()
    for b in range(4):
        ig_out[:, b * 896:b * 896 + 384] = igland[2 * b, :, :384]
        ig_out[:, b * 896 + 384:b * 896 + 512] = igland[2 * b, :, 384:] + igland[2 * b + 1, :, :128]
        ig_out[:, b * 896 + 512:(b + 1) * 896] = igland[2 * b + 1, :, 128:]


def on_device(queries, keys_values, projector, ownership, token_ids, student_input, student_weight, student_bias):
    hbm = pl.BlockSpec(memory_space=pl.ANY)
    vmem = pl.BlockSpec(memory_space=pltpu.VMEM)
    smem = pl.BlockSpec(memory_space=pltpu.SMEM)
    dma = pltpu.SemaphoreType.DMA
    V = pltpu.VMEM
    wgland, igland = pl.pallas_call(
        kernel,
        out_shape=(jax.ShapeDtypeStruct((16, 32, 1024), BF), jax.ShapeDtypeStruct((8, 128, 512), BF)),
        in_specs=[hbm, hbm, hbm, smem, vmem, hbm, vmem, vmem],
        out_specs=(hbm, hbm),
        scratch_shapes=[
            V((8, 128, 512), BF), V((8, 128, 512), BF), V((2048, 128), BF), V((2048, 128), BF),
            V((1024, 2048), F32), V((1024, 128), F32), V((1024, 256), F32), V((128, 1024), BF),
            V((512, 1024), BF), V((512, 1024), BF), V((8, 128, 1024), BF),
            V((2, 4, 128, 512), BF), V((2, 128, 512), BF), V((4, 128, 512), BF), V((4, 128, 512), BF),
            V((4, 128, 512), BF), V((8, 16, 1024), BF), V((8, 16, 1024), BF),
            V((8, 128, 512), BF), V((512, 1024), BF), V((32, 1024), BF), V((16, 32, 1024), BF),
            V((512, 1024), BF), V((1, 1024), F32),
            V((4, 128, 1024), BF), V((4, 128, 1024), BF), V((4, 128, 1024), BF), V((4, 128, 1024), BF),
            V((8, 128, 1024), BF), V((512, 256), F32), V((16, 32, 1024), BF), V((8, 128, 512), BF),
            dma((5,)), dma((2,)), dma((2,)), dma((8,)), dma((16,)), dma((8,)), dma((16,)), dma((8,)), dma((8,)),
            dma((16,)), dma((16,)), dma((8,)), dma((8,)), dma((4,)), dma((4,)), dma((4,)), dma((4,)),
            dma((8,)), dma((8,)), dma((4,)), dma((4,)), dma((1,)), dma((1,)), dma((4,)), dma((4,)),
            dma((8,)), dma((8,)), dma((16,)), dma((16,)), dma((16,)), dma((16,)),
            dma((64,)), dma((64,)), dma((8,)), dma((8,)),
            pltpu.SemaphoreType.REGULAR, pltpu.SemaphoreType.REGULAR,
        ],
        compiler_params=pltpu.CompilerParams(
            collective_id=0, has_side_effects=True, vmem_limit_bytes=60 * 2 ** 20),
        cost_estimate=pl.CostEstimate(flops=9 * 10 ** 9, bytes_accessed=8 * 10 ** 6, transcendentals=9 * 10 ** 6),
    )(queries.reshape(8, 2, 128, 512), keys_values[0], projector, ownership, token_ids.reshape(1, 128),
      student_input, student_weight, student_bias.reshape(1, 8))
    wg, bias, loss, ig = pl.pallas_call(
        finish,
        out_shape=(jax.ShapeDtypeStruct((28, 1024), F32), jax.ShapeDtypeStruct((1, 8), F32),
                   jax.ShapeDtypeStruct((1, 1), F32), jax.ShapeDtypeStruct((128, 3584), BF)),
        in_specs=[hbm, hbm],
        out_specs=(vmem, vmem, vmem, vmem),
        scratch_shapes=[V((16, 32, 1024), BF), V((8, 128, 512), BF), dma((2,))],
        compiler_params=pltpu.CompilerParams(vmem_limit_bytes=32 * 2 ** 20),
    )(wgland, igland)
    return loss.reshape(()), wg, bias.reshape(8), ig


def solution(mesh):
    return jax.shard_map(
        on_device,
        mesh=mesh,
        in_specs=(
            P("grp", None, "tp"), P("grp", "tp", None), P("tp", None), P(), P(("grp", "tp")),
            P(("grp", "tp"), None), P(("grp", "tp"), None), P(("grp", "tp")),
        ),
        out_specs=(P(), P(("grp", "tp"), None), P(("grp", "tp")), P(("grp", "tp"), None)),
        check_vma=False,
    )
```

```python
import functools

import jax
import jax.numpy as jnp
from jax import lax
from jax.experimental import pallas as pl
from jax.experimental.pallas import tpu as pltpu
from jax.sharding import PartitionSpec as P

MESH = pl.DeviceIdType.MESH
TEXT_IDS = 151643
SCALE = 128 ** -0.5 * 1.4426950408889634
BF = jnp.bfloat16
F32 = jnp.float32


def rcopy(src, dst, send_sem, recv_sem, grp, tp):
    return pltpu.make_async_remote_copy(
        src_ref=src, dst_ref=dst, send_sem=send_sem, recv_sem=recv_sem,
        device_id=(grp, tp), device_id_type=MESH)


def loop(first, last, body):
    lax.fori_loop(first, last, lambda i, carry: (body(i), carry)[1], 0)


def attend(core, c, qo, qs, keys, values, S, mx, acc, out):
    L = 256 * (c + 1)
    q = jnp.concatenate([r[:, h * 128:(h + 1) * 128] for r in (qo, qs) for h in range(4)], axis=0)
    row = lax.broadcasted_iota(jnp.int32, (128, 256), 0) + core * 128
    keep = row >= lax.broadcasted_iota(jnp.int32, (128, 256), 1)
    for a in range(0, L, 512):
        b = min(a + 512, L)
        s_all = lax.dot_general(q, keys[a:b, :], (((1,), (1,)), ((), ())), preferred_element_type=F32)
        for h in range(8):
            hr = slice(h * 128, (h + 1) * 128)
            s = s_all[hr]
            if b == L:
                last = jnp.where(keep, s[:, b - a - 256:], -1e30)
                s = last if b - a == 256 else jnp.concatenate([s[:, :256], last], axis=1)
            S[hr, a:b] = s
            m = s[:, :128]
            for w in range(128, b - a, 128):
                m = jnp.maximum(m, s[:, w:w + 128])
            if a:
                m = jnp.maximum(mx[hr, :], m)
            if b == L:
                m = jnp.broadcast_to(jnp.max(m, axis=1, keepdims=True) * SCALE, (128, 128))
            mx[hr, :] = m
    for a in range(0, L, 1024):
        b = min(a + 1024, L)
        vt = values[a:b, :]
        vt = jnp.concatenate([vt, jnp.ones_like(vt)], axis=1)
        ps = []
        for h in range(8):
            hr = slice(h * 128, (h + 1) * 128)
            m = mx[hr, :]
            ps.append(jnp.concatenate(
                [jnp.exp2(S[hr, w:w + 128] * SCALE - m).astype(BF) for w in range(a, b, 128)], axis=1))
        o = jnp.dot(jnp.concatenate(ps, axis=0), vt, preferred_element_type=F32)
        if a:
            o = o + acc[...]
        if b < L:
            acc[...] = o
    for h in range(8):
        r = o[h * 128:(h + 1) * 128]
        out[:, h * 128:(h + 1) * 128] = (r[:, :128] / r[:, 128:]).astype(BF)


def kernel(q_in, kv_in, proj_in, own_in, ids_in, x_in, w_in, b_in,
           wgland, igland,
           qo, qs, keys, values, S, mx, acc, att, proj_o, proj_s, tsend, ta, ta2, tb, tbsum, tb2, tsum, pland,
           xland, xt, w_pad, wland, wz, brow, osib, oswap, osend, oland, eland, wg, wsend, igsend,
           l_sem, qp_s, qp_r, k_s, k_r, v_s, v_r, rk_s, rv_s, w_s, w_r, x_s, x_r, os_s, os_r, o_s, o_r,
           ta_s, ta_r, tb_s, tb_r, ta2_s, ta2_r, tb2_s, tb2_r, p_s, p_r, e_s, e_r, re_s, re_r, g_s, g_r, i_s, i_r, round2, round3):
    g = lax.axis_index("grp")
    t = lax.axis_index("tp")
    x, yl = lax.rem(g, 4), g // 4
    core, chip = lax.rem(t, 2), t // 2
    sib = chip * 2 + 1 - core
    m = core * 4 + x
    src16 = chip * 2 + yl

    def member(i):
        return yl * 4 + lax.rem(i, 4), chip * 2 + i // 4

    def plane(i):
        return lax.rem(i, 2) * 4 + x, (i // 2) * 2 + yl

    own_kv = pl.ds(pl.multiple_of(t * 128, 128), 128)
    kcol = pl.ds(pl.multiple_of(chip * 128, 128), 128)
    vcol = pl.ds(pl.multiple_of(1024 + chip * 128, 128), 128)

    def window(i):
        return pl.ds(pl.multiple_of((i // 2) * 896 + lax.rem(i, 2) * 384, 128), 512)

    local = [
        pltpu.make_async_copy(kv_in.at[:, kcol], keys.at[own_kv, :], l_sem.at[0]),
        pltpu.make_async_copy(kv_in.at[:, vcol], values.at[own_kv, :], l_sem.at[1]),
        pltpu.make_async_copy(q_in.at[:, core], qo, l_sem.at[2]),
        pltpu.make_async_copy(proj_in, proj_o, l_sem.at[3]),
        pltpu.make_async_copy(x_in.at[:, window(m)], xland.at[m], l_sem.at[4]),
    ]
    for copy in local:
        copy.start()

    lane = lax.broadcasted_iota(jnp.int32, (4, 1024), 1) - (g * 16 + t) * 8
    first = lax.broadcasted_iota(jnp.int32, (4, 1024), 0) == 0
    b_row = jnp.zeros((4, 1024), F32)
    for r in range(8):
        b_row = jnp.where(first & (lane == r), jnp.broadcast_to(b_in[:, r:r + 1].astype(F32), (4, 1024)), b_row)
    w_pad[...] = jnp.concatenate([w_in[...].astype(F32), b_row], axis=0).astype(BF)

    barrier = pltpu.get_barrier_semaphore()

    def greet(sem):
        def tell(grp, tp):
            pl.semaphore_signal(sem, inc=1, device_id=(grp, tp), device_id_type=MESH)

        loop(1, 8, lambda i: tell(g, lax.rem(chip + i, 8) * 2 + core))
        tell(g, sib)
        loop(1, 4, lambda i: tell(yl * 4 + lax.rem(x + i, 4), t))
        tell((1 - yl) * 4 + x, t)

    greet(barrier)
    pl.semaphore_wait(barrier, 12)

    def kv_cols(q):
        return (pl.ds(pl.multiple_of(q * 128, 128), 128),
                pl.ds(pl.multiple_of(1024 + q * 128, 128), 128))

    def k_send(i, start):
        q = lax.rem(chip + i * (1 + 6 * core), 8)
        a = rcopy(kv_in.at[:, kv_cols(q)[0]], keys.at[own_kv, :], k_s.at[q], k_r.at[t], g, q * 2 + core)
        if start:
            a.start()
        else:
            a.wait_send()

    def v_send(i, start):
        q = lax.rem(chip + i * (1 + 6 * core), 8)
        a = rcopy(kv_in.at[:, kv_cols(q)[1]], values.at[own_kv, :], v_s.at[q], v_r.at[t], g, q * 2 + core)
        if start:
            a.start()
        else:
            a.wait_send()

    loop(1, 8, lambda i: k_send(i, True))
    qcopy = rcopy(q_in.at[:, 1 - core], qs, qp_s.at[0], qp_r.at[0], g, sib)
    pcopy = rcopy(proj_in, proj_s, qp_s.at[1], qp_r.at[1], g, sib)
    qcopy.start()
    loop(1, 8, lambda i: v_send(i, True))
    greet(round2)

    def rows_of(src):
        return pl.ds(pl.multiple_of(src * 128, 128), 128)

    def k_relay(src):
        rows = rows_of(src)
        return rcopy(keys.at[rows, :], keys.at[rows, :], rk_s.at[src // 2], k_r.at[src], g, sib)

    def v_relay(src):
        rows = rows_of(src)
        return rcopy(values.at[rows, :], values.at[rows, :], rv_s.at[src // 2], v_r.at[src], g, sib)

    def k_pass(i):
        src = lax.rem(chip + i * (7 - 6 * core), 8) * 2 + core
        k_relay(src).wait_recv()
        k_relay(src).start()

    def v_pass(i):
        src = lax.rem(chip + i * (7 - 6 * core), 8) * 2 + core
        v_relay(src).wait_recv()
        v_relay(src).start()

    local[0].wait()
    k_relay(t).start()
    local[1].wait()
    v_relay(t).start()
    loop(1, 8, k_pass)
    pl.semaphore_wait(round2, 12)
    pl.semaphore_signal(round3, inc=1, device_id=(g, sib), device_id_type=MESH)

    def w_send(i, start):
        i = lax.rem(src16 + i, 16)
        dg, dt = plane(i)
        here = (i == src16) & (core == yl)

        if start:
            @pl.when(here)
            def _():
                pltpu.make_async_copy(w_pad, wland.at[t], w_r.at[t]).start()

        @pl.when(jnp.logical_not(here))
        def _():
            copy = rcopy(w_pad, wland.at[t], w_s.at[i], w_r.at[t], dg, dt)
            if start:
                copy.start()
            else:
                copy.wait_send()

    def x_send(i, start):
        j = lax.rem(m + i, 8)
        dg, dt = member(j)
        copy = rcopy(x_in.at[:, window(j)], xland.at[m], x_s.at[j], x_r.at[m], dg, dt)
        if start:
            copy.start()
        else:
            copy.wait_send()

    loop(1, 8, lambda i: x_send(i, True))
    loop(1, 8, v_pass)
    pcopy.start()
    pl.semaphore_wait(round3, 1)
    loop(0, 16, lambda i: w_send(i, True))
    loop(0, 8, lambda i: k_relay(i * 2 + 1 - core).wait_recv())
    local[2].wait()
    qcopy.wait_recv()

    cz, ch = chip // 2, lax.rem(chip, 2)
    A, B = pl.ds(0, 512), pl.ds(512, 512)

    def ta_send(c, start):
        copy = rcopy(tsend.at[c, :, A], ta.at[lax.rem(c, 2), cz], ta_s.at[c], ta_r.at[lax.rem(c, 2) * 4 + cz],
                     g, (c // 2 * 2 + ch) * 2 + core)
        if start:
            copy.start()
        else:
            copy.wait_send()

    def ta_wait(h, z):
        rcopy(ta.at[h, z], ta.at[h, z], ta_s.at[0], ta_r.at[h * 4 + z], g, sib).wait_recv()

    def ta2_send():
        return rcopy(ta2.at[0], ta2.at[1], ta2_s.at[0], ta2_r.at[0], g, (cz * 2 + 1 - ch) * 2 + core)

    def tb_send(z, start):
        copy = rcopy(tsend.at[z * 2 + 1 - ch, :, B], tb.at[z], tb_s.at[z], tb_r.at[z],
                     g, (cz * 2 + 1 - ch) * 2 + core)
        if start:
            copy.start()
        else:
            copy.wait_send()

    def tb2_send(z, start):
        copy = rcopy(tbsum.at[z], tb2.at[cz], tb2_s.at[z], tb2_r.at[cz], g, (z * 2 + ch) * 2 + core)
        if start:
            copy.start()
        else:
            copy.wait_send()

    def os_send(i, start):
        copy = rcopy(osib.at[i], oswap.at[i], os_s.at[i], os_r.at[i], g, sib)
        if start:
            copy.start()
        else:
            copy.wait_send()

    def o_send(i, start):
        xx = lax.rem(x + i, 4)
        copy = rcopy(osend.at[xx], oland.at[x], o_s.at[xx], o_r.at[x], yl * 4 + xx, t)
        if start:
            copy.start()
        else:
            copy.wait_send()

    off = pl.multiple_of(lax.rem(x, 2) * 64, 64)

    def student_forward():
        loop(0, 16, lambda i: pltpu.make_async_copy(w_pad, wland.at[i], w_r.at[i]).wait())
        wz[...] = jnp.zeros_like(wz)
        bias = jnp.zeros((1, 1024), F32)
        for a in range(4):
            rows = [wland[4 * a + b].astype(F32) for b in range(4)]
            for r in rows:
                bias = bias + r[28:29]
            wz[pl.ds(off + a * 112, 112), :] = jnp.concatenate([r[:28] for r in rows], axis=0).astype(BF)
        brow[...] = bias
        local[4].wait()

        def fetch(j):
            @pl.when(j != m)
            def _():
                rcopy(xland.at[j], xland.at[j], x_s.at[0], x_r.at[j], g, sib).wait_recv()

        def forward(half, dst):
            first = half * 4
            loop(0, 4, lambda i: fetch(first + i))
            rows = xland[pl.ds(first, 4)].reshape(512, 512)
            for n in range(4):
                cols = slice(n * 256, (n + 1) * 256)
                o = jnp.dot(rows, wz[:, cols], preferred_element_type=F32) + brow[:, cols]
                dst[:, :, cols] = o.astype(BF).reshape(4, 128, 256)

        forward(1 - core, osib)
        loop(0, 4, lambda i: os_send(i, True))
        forward(core, osend)

    def output_sums():
        def one(i):
            xx = lax.rem(x + i, 4)
            rcopy(oswap.at[xx], oswap.at[xx], os_s.at[0], os_r.at[xx], g, sib).wait_recv()
            osend[xx] = (osend[xx].astype(F32) + oswap[xx].astype(F32)).astype(BF)

            @pl.when(i < 4)
            def _():
                o_send(i, True)

        loop(1, 5, one)
        oland[x] = osend[x]

    def first_chunk(i):
        @pl.when(i == 0)
        def _():
            loop(0, 8, lambda k: v_relay(k * 2 + 1 - core).wait_recv())
            local[3].wait()
            pcopy.wait_recv()


    def chunk(i):
        k = jnp.where(i < 3, i + 1, jnp.where(i < 5, i - 2, jnp.where(i == 6, 3, 0)))
        other = (i < 3) | (i == 5)
        z = lax.rem(cz + k * (1 + 2 * core), 4)
        c = z * 2 + lax.rem(ch + jnp.where(other, 1, 0), 2)

        @pl.when(i == 3)
        def _():
            student_forward()

        @pl.when(i == 5)
        def _():
            output_sums()

        first_chunk(i)

        def at(n):
            return lambda: attend(core, n, qo.at[n], qs.at[n], keys, values, S, mx, acc, att)

        lax.switch(c, [at(n) for n in range(8)])
        for n in range(4):
            cols = slice(n * 256, (n + 1) * 256)
            p = jnp.dot(att[:, :512], proj_o[:, cols], preferred_element_type=F32)
            p = p + jnp.dot(att[:, 512:], proj_s[:, cols], preferred_element_type=F32)
            tsend[c, :, cols] = p.astype(BF)

        @pl.when(k > 0)
        def _():
            ta_send(c, True)

        @pl.when(other)
        def _():
            tb_send(z, True)

        @pl.when(jnp.logical_not(other) & (k > 0))
        def _():
            rcopy(tb.at[z], tb.at[z], tb_s.at[0], tb_r.at[z], g, sib).wait_recv()
            tbsum[z] = (tsend[c, :, B].astype(F32) + tb[z].astype(F32)).astype(BF)
            tb2_send(z, True)

        @pl.when(i == 5)
        def _():
            total = tsend[c, :, A].astype(F32)
            for k in range(1, 4):
                zz = lax.rem(cz + k, 4)
                ta_wait(1 - ch, zz)
                total = total + ta[1 - ch, zz].astype(F32)
            ta2[0] = total.astype(BF)
            ta2_send().start()

    loop(0, 8, chunk)
    for j in range(8):
        xt[:, j * 128:(j + 1) * 128] = jnp.transpose(xland[j])
    total = tsend[chip, :, A].astype(F32)
    for k in range(1, 4):
        zz = lax.rem(cz + k, 4)
        ta_wait(ch, zz)
        total = total + ta[ch, zz].astype(F32)
    ta2_send().wait_recv()
    total = total + ta2[1].astype(F32)
    tsum[:, :, A] = total.astype(BF).reshape(8, 16, 512)
    rcopy(tb.at[cz], tb.at[cz], tb_s.at[0], tb_r.at[cz], g, sib).wait_recv()
    total = tsend[chip, :, B].astype(F32) + tb[cz].astype(F32)
    for k in range(1, 4):
        zz = lax.rem(cz + k, 4)
        rcopy(tb2.at[zz], tb2.at[zz], tb2_s.at[0], tb2_r.at[zz], g, sib).wait_recv()
        total = total + tb2[zz].astype(F32)
    tsum[:, :, B] = total.astype(BF).reshape(8, 16, 512)

    def p_send(i, start):
        j = lax.rem(g + i, 8)
        copy = rcopy(tsum.at[j], pland.at[g], p_s.at[j], p_r.at[g], j, t)
        if start:
            copy.start()
        else:
            copy.wait_send()

    loop(1, 8, lambda i: p_send(i, True))
    pland[g] = tsum[g]

    def o_wait(i):
        j = lax.rem(x + i, 4)
        rcopy(oland.at[j], oland.at[j], o_s.at[0], o_r.at[j], g, sib).wait_recv()

    loop(1, 4, o_wait)

    def p_wait(i):
        j = lax.rem(g + i, 8)
        rcopy(pland.at[j], pland.at[j], p_s.at[0], p_r.at[j], g, sib).wait_recv()

    loop(1, 8, p_wait)
    keep = jnp.where(ids_in[...] < TEXT_IDS, 1.0, 0.0).astype(F32)
    keep = jnp.transpose(jnp.broadcast_to(keep, (128, 128)))
    keep = jnp.concatenate([keep, keep], axis=1)

    def errors(n):
        cols = slice(n * 256, (n + 1) * 256)
        for k in range(8):
            rows = slice(k * 16, (k + 1) * 16)
            o = oland[0, rows, cols].astype(F32)
            for j in range(1, 4):
                o = o + oland[j, rows, cols].astype(F32)
            eland[m, rows, cols] = (keep[rows] * (o - pland[own_in[k], :, cols].astype(F32))).astype(BF)

    def cols_of(n):
        return pl.ds(n * 256, 256)

    def e_send(dx, n):
        here = eland.at[m, :, cols_of(n)]
        return rcopy(here, here, e_s.at[dx * 4 + n], e_r.at[dx * 4 + n], yl * 4 + lax.rem(x + dx, 4), t)

    def e_relay(dx, n):
        xx = lax.rem(x + dx, 4)
        here = eland.at[core * 4 + xx, :, cols_of(n)]
        return rcopy(here, here, re_s.at[xx * 4 + n], re_r.at[xx * 4 + n], g, sib)

    def e_begin(n):
        errors(n)
        for dx in (2, 1, 3):
            e_send(dx, n).start()
        e_relay(0, n).start()

    def e_pass(n):
        for dx in (1, 3, 2):
            e_send(dx, n).wait_recv()
            e_relay(4 - dx, n).start()

    row = lax.broadcasted_iota(jnp.int32, (32, 256), 0)

    def g_send(i, n, start):
        here = (core == yl) & (i == t)
        src, dst = wsend.at[i, :, cols_of(n)], wgland.at[src16, :, cols_of(n)]

        if start:
            @pl.when(here)
            def _():
                pltpu.make_async_copy(src, dst, g_r.at[n * 16 + src16]).start()

        @pl.when(jnp.logical_not(here))
        def _():
            copy = rcopy(src, dst, g_s.at[n * 16 + i], g_r.at[n * 16 + src16], core * 4 + x, i)
            if start:
                copy.start()
            else:
                copy.wait_send()

    def weight_grad(n):
        if n < 3:
            for k in range(4):
                e_relay(k, n).wait_recv()
        cols = slice(n * 256, (n + 1) * 256)
        eb = jnp.zeros((8, 256), F32)
        lb = jnp.zeros((8, 256), F32)
        for j in range(8):
            ef = eland[j, :, cols].astype(F32)
            for r in range(16):
                er = ef[r * 8:(r + 1) * 8]
                eb = eb + er
                lb = lb + er * er
        wg[...] = jnp.dot(xt[...], eland[:, :, cols].reshape(1024, 256), preferred_element_type=F32)
        esum = jnp.sum(eb, axis=0, keepdims=True)
        lsum = jnp.sum(lb, axis=0, keepdims=True)
        ehi = esum.astype(BF).astype(F32)
        lhi = lsum.astype(BF).astype(F32)
        for i in range(16):
            v = wg[pl.ds(off + (28 * i) // 8 * 8, 32), :]
            if (28 * i) % 8:
                v = pltpu.roll(v, 28, 0)
            for r, e in enumerate([ehi, esum - ehi, lhi, lsum - lhi]):
                v = jnp.where(row == 28 + r, e, v)
            wsend[i, :, cols] = v.astype(BF)
        loop(0, 16, lambda i: g_send(lax.rem(t + i, 16), n, True))

    for n in range(4):
        e_begin(n)
    for n in range(3):
        e_pass(n)
        weight_grad(n)
    e_pass(3)
    for k in range(4):
        e_relay(k, 3).wait_recv()

    def i_send(k, j, slot, start):
        dg, dt = member(j)
        copy = rcopy(igsend.at[k], igland.at[slot], i_s.at[k], i_r.at[slot], dg, dt)
        if start:
            copy.start()
        else:
            copy.wait_send()

    pairs = [(2, wz, m), (1, wz, m), (3, wz, m), (0, wz, m)]
    ig_own = [pltpu.make_async_copy(igsend.at[6], igland.at[m], i_r.at[m])]
    for k, (dx, w, slot) in enumerate(pairs):
        if k == 3:
            weight_grad(3)
        xx = lax.rem(x + dx, 4)
        mine, other = core * 4 + xx, (1 - core) * 4 + xx
        e = jnp.concatenate([eland[mine], eland[other]], axis=0)
        ig = lax.dot_general(e, w[...], (((1,), (1,)), ((), ())), preferred_element_type=F32).astype(BF)
        igsend[2 * k] = ig[:128]
        igsend[2 * k + 1] = ig[128:]
        if dx:
            i_send(2 * k, mine, slot, True)
        else:
            ig_own[0].start()
        i_send(2 * k + 1, other, slot, True)

    def g_wait(i):
        for n in range(4):
            here = wgland.at[i, :, cols_of(n)]
            pltpu.make_async_copy(wsend.at[i, :, cols_of(n)], here, g_r.at[n * 16 + i]).wait()

    loop(0, 16, g_wait)
    for copy in ig_own:
        copy.wait()

    def i_wait(i):
        @pl.when(i != m)
        def _():
            rcopy(igland.at[i], igland.at[i], i_s.at[0], i_r.at[i], g, sib).wait_recv()

    loop(0, 8, i_wait)
    loop(1, 8, lambda i: k_send(i, False))
    loop(1, 8, lambda i: v_send(i, False))
    qcopy.wait_send()
    pcopy.wait_send()
    loop(0, 8, lambda i: k_relay(i * 2 + core).wait_send())
    loop(0, 8, lambda i: v_relay(i * 2 + core).wait_send())
    loop(0, 16, lambda i: w_send(i, False))
    loop(1, 8, lambda i: x_send(i, False))
    loop(0, 4, lambda i: os_send(i, False))
    loop(1, 4, lambda i: o_send(i, False))
    loop(2, 8, lambda i: ta_send(lax.rem(cz * 2 + i, 8), False))
    loop(0, 4, lambda i: tb_send(i, False))
    loop(1, 4, lambda i: tb2_send(lax.rem(cz + i, 4), False))
    ta2_send().wait_send()
    loop(1, 8, lambda i: p_send(i, False))
    for n in range(4):
        for dx in (1, 2, 3):
            e_send(dx, n).wait_send()
        for dx in range(4):
            e_relay(dx, n).wait_send()
        loop(0, 16, lambda i: g_send(i, n, False))
    for k, (dx, w, slot) in enumerate(pairs):
        xx = lax.rem(x + dx, 4)
        if dx:
            i_send(2 * k, core * 4 + xx, slot, False)
        i_send(2 * k + 1, (1 - core) * 4 + xx, slot, False)


def finish(wg_in, ig_in, wg_out, bias_out, loss_out, ig_out, wgland, igland, sem):
    d = lax.axis_index("grp") * 16 + lax.axis_index("tp")
    wg_copy = pltpu.make_async_copy(wg_in, wgland, sem.at[0])
    ig_copy = pltpu.make_async_copy(ig_in, igland, sem.at[1])
    wg_copy.start()
    ig_copy.start()
    wg_copy.wait()
    total = wgland[0].astype(F32)
    for i in range(1, 16):
        total = total + wgland[i].astype(F32)
    wg_out[...] = total[:28]
    small = total[24:32]
    loss_out[...] = jnp.sum(small[6:8], axis=(0, 1), keepdims=True) / 32768.0
    both = jnp.broadcast_to(small[4:5] + small[5:6], (8, 1024))
    both = pltpu.roll(both, lax.rem(1024 - d * 8, 1024), 1)
    bias_out[...] = both[0:1, 0:8]
    ig_copy.wait()
    for b in range(4):
        ig_out[:, b * 896:b * 896 + 384] = igland[2 * b, :, :384]
        ig_out[:, b * 896 + 384:b * 896 + 512] = igland[2 * b, :, 384:] + igland[2 * b + 1, :, :128]
        ig_out[:, b * 896 + 512:(b + 1) * 896] = igland[2 * b + 1, :, 128:]


def on_device(queries, keys_values, projector, ownership, token_ids, student_input, student_weight, student_bias):
    hbm = pl.BlockSpec(memory_space=pl.ANY)
    vmem = pl.BlockSpec(memory_space=pltpu.VMEM)
    smem = pl.BlockSpec(memory_space=pltpu.SMEM)
    dma = pltpu.SemaphoreType.DMA
    V = pltpu.VMEM
    wgland, igland = pl.pallas_call(
        kernel,
        out_shape=(jax.ShapeDtypeStruct((16, 32, 1024), BF), jax.ShapeDtypeStruct((8, 128, 512), BF)),
        in_specs=[hbm, hbm, hbm, smem, vmem, hbm, vmem, vmem],
        out_specs=(hbm, hbm),
        scratch_shapes=[
            V((8, 128, 512), BF), V((8, 128, 512), BF), V((2048, 128), BF), V((2048, 128), BF),
            V((1024, 2048), F32), V((1024, 128), F32), V((1024, 256), F32), V((128, 1024), BF),
            V((512, 1024), BF), V((512, 1024), BF), V((8, 128, 1024), BF),
            V((2, 4, 128, 512), BF), V((2, 128, 512), BF), V((4, 128, 512), BF), V((4, 128, 512), BF),
            V((4, 128, 512), BF), V((8, 16, 1024), BF), V((8, 16, 1024), BF),
            V((8, 128, 512), BF), V((512, 1024), BF), V((32, 1024), BF), V((16, 32, 1024), BF),
            V((512, 1024), BF), V((1, 1024), F32),
            V((4, 128, 1024), BF), V((4, 128, 1024), BF), V((4, 128, 1024), BF), V((4, 128, 1024), BF),
            V((8, 128, 1024), BF), V((512, 256), F32), V((16, 32, 1024), BF), V((8, 128, 512), BF),
            dma((5,)), dma((2,)), dma((2,)), dma((8,)), dma((16,)), dma((8,)), dma((16,)), dma((8,)), dma((8,)),
            dma((16,)), dma((16,)), dma((8,)), dma((8,)), dma((4,)), dma((4,)), dma((4,)), dma((4,)),
            dma((8,)), dma((8,)), dma((4,)), dma((4,)), dma((1,)), dma((1,)), dma((4,)), dma((4,)),
            dma((8,)), dma((8,)), dma((16,)), dma((16,)), dma((16,)), dma((16,)),
            dma((64,)), dma((64,)), dma((8,)), dma((8,)),
            pltpu.SemaphoreType.REGULAR, pltpu.SemaphoreType.REGULAR,
        ],
        compiler_params=pltpu.CompilerParams(
            collective_id=0, has_side_effects=True, vmem_limit_bytes=60 * 2 ** 20),
        cost_estimate=pl.CostEstimate(flops=9 * 10 ** 9, bytes_accessed=8 * 10 ** 6, transcendentals=9 * 10 ** 6),
    )(queries.reshape(8, 2, 128, 512), keys_values[0], projector, ownership, token_ids.reshape(1, 128),
      student_input, student_weight, student_bias.reshape(1, 8))
    wg, bias, loss, ig = pl.pallas_call(
        finish,
        out_shape=(jax.ShapeDtypeStruct((28, 1024), F32), jax.ShapeDtypeStruct((1, 8), F32),
                   jax.ShapeDtypeStruct((1, 1), F32), jax.ShapeDtypeStruct((128, 3584), BF)),
        in_specs=[hbm, hbm],
        out_specs=(vmem, vmem, vmem, vmem),
        scratch_shapes=[V((16, 32, 1024), BF), V((8, 128, 512), BF), dma((2,))],
        compiler_params=pltpu.CompilerParams(vmem_limit_bytes=60 * 2 ** 20),
    )(wgland, igland)
    return loss.reshape(()), wg, bias.reshape(8), ig


def solution(mesh):
    return jax.shard_map(
        on_device,
        mesh=mesh,
        in_specs=(
            P("grp", None, "tp"), P("grp", "tp", None), P("tp", None), P(), P(("grp", "tp")),
            P(("grp", "tp"), None), P(("grp", "tp"), None), P(("grp", "tp")),
        ),
        out_specs=(P(), P(("grp", "tp"), None), P(("grp", "tp")), P(("grp", "tp"), None)),
        check_vma=False,
    )
```

```python
import functools

import jax
import jax.numpy as jnp
from jax import lax
from jax.experimental import pallas as pl
from jax.experimental.pallas import tpu as pltpu
from jax.sharding import PartitionSpec as P

MESH = pl.DeviceIdType.MESH
TEXT_IDS = 151643
SCALE = 128 ** -0.5 * 1.4426950408889634
BF = jnp.bfloat16
F32 = jnp.float32


def rcopy(src, dst, send_sem, recv_sem, grp, tp):
    return pltpu.make_async_remote_copy(
        src_ref=src, dst_ref=dst, send_sem=send_sem, recv_sem=recv_sem,
        device_id=(grp, tp), device_id_type=MESH)


def loop(first, last, body):
    lax.fori_loop(first, last, lambda i, carry: (body(i), carry)[1], 0)


def attend(core, c, qo, qs, keys, values, S, mx, acc, out):
    L = 256 * (c + 1)
    q = jnp.concatenate([r[:, h * 128:(h + 1) * 128] for r in (qo, qs) for h in range(4)], axis=0)
    row = lax.broadcasted_iota(jnp.int32, (128, 256), 0) + core * 128
    keep = row >= lax.broadcasted_iota(jnp.int32, (128, 256), 1)
    for a in range(0, L, 512):
        b = min(a + 512, L)
        s_all = lax.dot_general(q, keys[a:b, :], (((1,), (1,)), ((), ())), preferred_element_type=F32)
        for h in range(8):
            hr = slice(h * 128, (h + 1) * 128)
            s = s_all[hr]
            if b == L:
                last = jnp.where(keep, s[:, b - a - 256:], -1e30)
                s = last if b - a == 256 else jnp.concatenate([s[:, :256], last], axis=1)
            S[hr, a:b] = s
            m = s[:, :128]
            for w in range(128, b - a, 128):
                m = jnp.maximum(m, s[:, w:w + 128])
            if a:
                m = jnp.maximum(mx[hr, :], m)
            if b == L:
                m = jnp.broadcast_to(jnp.max(m, axis=1, keepdims=True) * SCALE, (128, 128))
            mx[hr, :] = m
    for a in range(0, L, 1024):
        b = min(a + 1024, L)
        vt = values[a:b, :]
        vt = jnp.concatenate([vt, jnp.ones_like(vt)], axis=1)
        ps = []
        for h in range(8):
            hr = slice(h * 128, (h + 1) * 128)
            m = mx[hr, :]
            ps.append(jnp.concatenate(
                [jnp.exp2(S[hr, w:w + 128] * SCALE - m).astype(BF) for w in range(a, b, 128)], axis=1))
        o = jnp.dot(jnp.concatenate(ps, axis=0), vt, preferred_element_type=F32)
        if a:
            o = o + acc[...]
        if b < L:
            acc[...] = o
    for h in range(8):
        r = o[h * 128:(h + 1) * 128]
        out[:, h * 128:(h + 1) * 128] = (r[:, :128] / r[:, 128:]).astype(BF)


def kernel(q_in, kv_in, proj_in, own_in, ids_in, x_in, w_in, b_in,
           wgland, igland,
           qo, qs, keys, values, S, mx, acc, att, proj_o, proj_s, tsend, ta, ta2, tb, tbsum, tb2, tsum, pland,
           xland, xt, w_pad, wland, wz, brow, osib, oswap, osend, oland, eland, wg, wsend, igsend,
           l_sem, qp_s, qp_r, k_s, k_r, v_s, v_r, rk_s, rv_s, w_s, w_r, x_s, x_r, os_s, os_r, o_s, o_r,
           ta_s, ta_r, tb_s, tb_r, ta2_s, ta2_r, tb2_s, tb2_r, p_s, p_r, e_s, e_r, re_s, re_r, g_s, g_r, i_s, i_r, round2, round3):
    g = lax.axis_index("grp")
    t = lax.axis_index("tp")
    x, yl = lax.rem(g, 4), g // 4
    core, chip = lax.rem(t, 2), t // 2
    sib = chip * 2 + 1 - core
    m = core * 4 + x
    src16 = chip * 2 + yl

    def member(i):
        return yl * 4 + lax.rem(i, 4), chip * 2 + i // 4

    own_kv = pl.ds(pl.multiple_of(t * 128, 128), 128)
    kcol = pl.ds(pl.multiple_of(chip * 128, 128), 128)
    vcol = pl.ds(pl.multiple_of(1024 + chip * 128, 128), 128)

    def window(i):
        return pl.ds(pl.multiple_of((i // 2) * 896 + lax.rem(i, 2) * 384, 128), 512)

    local = [
        pltpu.make_async_copy(kv_in.at[:, kcol], keys.at[own_kv, :], l_sem.at[0]),
        pltpu.make_async_copy(kv_in.at[:, vcol], values.at[own_kv, :], l_sem.at[1]),
        pltpu.make_async_copy(q_in.at[:, core], qo, l_sem.at[2]),
        pltpu.make_async_copy(proj_in, proj_o, l_sem.at[3]),
        pltpu.make_async_copy(x_in.at[:, window(m)], xland.at[m], l_sem.at[4]),
    ]
    for copy in local:
        copy.start()

    lane = lax.broadcasted_iota(jnp.int32, (4, 1024), 1) - (g * 16 + t) * 8
    first = lax.broadcasted_iota(jnp.int32, (4, 1024), 0) == 0
    b_row = jnp.zeros((4, 1024), F32)
    for r in range(8):
        b_row = jnp.where(first & (lane == r), jnp.broadcast_to(b_in[:, r:r + 1].astype(F32), (4, 1024)), b_row)
    w_pad[...] = jnp.concatenate([w_in[...].astype(F32), b_row], axis=0).astype(BF)

    barrier = pltpu.get_barrier_semaphore()

    def greet(sem):
        def tell(grp, tp):
            pl.semaphore_signal(sem, inc=1, device_id=(grp, tp), device_id_type=MESH)

        loop(1, 8, lambda i: tell(g, lax.rem(chip + i, 8) * 2 + core))
        tell(g, sib)
        loop(1, 4, lambda i: tell(yl * 4 + lax.rem(x + i, 4), t))
        tell((1 - yl) * 4 + x, t)

    greet(barrier)
    pl.semaphore_wait(barrier, 12)

    def kv_cols(q):
        return (pl.ds(pl.multiple_of(q * 128, 128), 128),
                pl.ds(pl.multiple_of(1024 + q * 128, 128), 128))

    def k_send(i, start):
        q = lax.rem(chip + i * (1 + 6 * core), 8)
        a = rcopy(kv_in.at[:, kv_cols(q)[0]], keys.at[own_kv, :], k_s.at[q], k_r.at[t], g, q * 2 + core)
        if start:
            a.start()
        else:
            a.wait_send()

    def v_send(i, start):
        q = lax.rem(chip + i * (1 + 6 * core), 8)
        a = rcopy(kv_in.at[:, kv_cols(q)[1]], values.at[own_kv, :], v_s.at[q], v_r.at[t], g, q * 2 + core)
        if start:
            a.start()
        else:
            a.wait_send()

    loop(1, 8, lambda i: k_send(i, True))
    qcopy = rcopy(q_in.at[:, 1 - core], qs, qp_s.at[0], qp_r.at[0], g, sib)
    pcopy = rcopy(proj_in, proj_s, qp_s.at[1], qp_r.at[1], g, sib)
    qcopy.start()
    loop(1, 8, lambda i: v_send(i, True))
    greet(round2)

    def rows_of(src):
        return pl.ds(pl.multiple_of(src * 128, 128), 128)

    def k_relay(src):
        rows = rows_of(src)
        return rcopy(keys.at[rows, :], keys.at[rows, :], rk_s.at[src // 2], k_r.at[src], g, sib)

    def v_relay(src):
        rows = rows_of(src)
        return rcopy(values.at[rows, :], values.at[rows, :], rv_s.at[src // 2], v_r.at[src], g, sib)

    def k_pass(i):
        src = lax.rem(chip + i * (7 - 6 * core), 8) * 2 + core
        k_relay(src).wait_recv()
        k_relay(src).start()

    def v_pass(i):
        src = lax.rem(chip + i * (7 - 6 * core), 8) * 2 + core
        v_relay(src).wait_recv()
        v_relay(src).start()

    local[0].wait()
    k_relay(t).start()
    local[1].wait()
    v_relay(t).start()
    loop(1, 8, k_pass)
    pl.semaphore_wait(round2, 12)
    pl.semaphore_signal(round3, inc=1, device_id=(g, sib), device_id_type=MESH)

    cz, ch, y = chip // 2, lax.rem(chip, 2), lax.rem(chip, 2) * 2 + yl

    def w_first(i, start):
        zz, yy = lax.rem(cz + i * (1 - core), 4), lax.rem(y + i * core, 4)
        here = (i == 0) & (core == yl)
        if start:
            @pl.when(here)
            def _():
                pltpu.make_async_copy(w_pad, wland.at[t], w_r.at[t]).start()

        @pl.when(jnp.logical_not(here))
        def _():
            copy = rcopy(w_pad, wland.at[t], w_s.at[i], w_r.at[t],
                         lax.rem(yy, 2) * 4 + x, zz * 4 + yy // 2 * 2 + yl)
            if start:
                copy.start()
            else:
                copy.wait_send()

    def w_wait(i):
        pltpu.make_async_copy(w_pad, wland.at[i], w_r.at[i]).wait()

    def w_along_y(i, start):
        slot = i * 4 + ch * 2
        if start:
            w_wait(slot)
        for k in range(1, 4):
            yy = lax.rem(y + k, 4)
            copy = rcopy(wland.at[slot], wland.at[slot], w_s.at[4 + i * 3 + k - 1], w_r.at[slot],
                         lax.rem(yy, 2) * 4 + x, cz * 4 + yy // 2 * 2 + core)
            if start:
                copy.start()
            else:
                copy.wait_send()

    def w_along_z(i, start):
        slot = cz * 4 + i * 2 + 1
        if start:
            w_wait(slot)
        for k in range(1, 4):
            zz = lax.rem(cz + k, 4)
            copy = rcopy(wland.at[slot], wland.at[slot], w_s.at[16 + i * 3 + k - 1], w_r.at[slot],
                         g, zz * 4 + ch * 2 + core)
            if start:
                copy.start()
            else:
                copy.wait_send()

    def w_second(start):
        @pl.when(core == yl)
        def _():
            loop(0, 4, lambda i: w_along_y(i, start))

        loop(0, 2, lambda i: w_along_z(i, start))

    def w_late(i):
        early_y = (lax.rem(i, 2) == 0) & (core == yl) & (lax.rem(i // 2, 2) == ch)
        early_z = (lax.rem(i, 2) == 1) & (i // 4 == cz)

        @pl.when(jnp.logical_not(early_y | early_z))
        def _():
            w_wait(i)

    def x_send(i, start):
        j = lax.rem(m + i, 8)
        dg, dt = member(j)
        copy = rcopy(x_in.at[:, window(j)], xland.at[m], x_s.at[j], x_r.at[m], dg, dt)
        if start:
            copy.start()
        else:
            copy.wait_send()

    pl.semaphore_wait(round3, 1)
    loop(0, 4, lambda i: w_first(i, True))
    loop(1, 8, lambda i: x_send(i, True))
    loop(1, 8, v_pass)
    pcopy.start()
    w_second(True)
    loop(0, 8, lambda i: k_relay(i * 2 + 1 - core).wait_recv())
    local[2].wait()
    qcopy.wait_recv()

    A, B = pl.ds(0, 512), pl.ds(512, 512)

    def ta_send(c, start):
        copy = rcopy(tsend.at[c, :, A], ta.at[lax.rem(c, 2), cz], ta_s.at[c], ta_r.at[lax.rem(c, 2) * 4 + cz],
                     g, (c // 2 * 2 + ch) * 2 + core)
        if start:
            copy.start()
        else:
            copy.wait_send()

    def ta_wait(h, z):
        rcopy(ta.at[h, z], ta.at[h, z], ta_s.at[0], ta_r.at[h * 4 + z], g, sib).wait_recv()

    def ta2_send():
        return rcopy(ta2.at[0], ta2.at[1], ta2_s.at[0], ta2_r.at[0], g, (cz * 2 + 1 - ch) * 2 + core)

    def tb_send(z, start):
        copy = rcopy(tsend.at[z * 2 + 1 - ch, :, B], tb.at[z], tb_s.at[z], tb_r.at[z],
                     g, (cz * 2 + 1 - ch) * 2 + core)
        if start:
            copy.start()
        else:
            copy.wait_send()

    def tb2_send(z, start):
        copy = rcopy(tbsum.at[z], tb2.at[cz], tb2_s.at[z], tb2_r.at[cz], g, (z * 2 + ch) * 2 + core)
        if start:
            copy.start()
        else:
            copy.wait_send()

    def os_send(i, start):
        copy = rcopy(osib.at[i], oswap.at[i], os_s.at[i], os_r.at[i], g, sib)
        if start:
            copy.start()
        else:
            copy.wait_send()

    def o_send(i, start):
        xx = lax.rem(x + i, 4)
        copy = rcopy(osend.at[xx], oland.at[x], o_s.at[xx], o_r.at[x], yl * 4 + xx, t)
        if start:
            copy.start()
        else:
            copy.wait_send()

    off = pl.multiple_of(lax.rem(x, 2) * 64, 64)

    def student_forward():
        loop(0, 16, w_late)
        wz[...] = jnp.zeros_like(wz)
        bias = jnp.zeros((1, 1024), F32)
        for a in range(4):
            rows = [wland[4 * a + b].astype(F32) for b in range(4)]
            for r in rows:
                bias = bias + r[28:29]
            wz[pl.ds(off + a * 112, 112), :] = jnp.concatenate([r[:28] for r in rows], axis=0).astype(BF)
        brow[...] = bias
        local[4].wait()

        def fetch(j):
            @pl.when(j != m)
            def _():
                rcopy(xland.at[j], xland.at[j], x_s.at[0], x_r.at[j], g, sib).wait_recv()

        def forward(half, dst):
            first = half * 4
            loop(0, 4, lambda i: fetch(first + i))
            rows = xland[pl.ds(first, 4)].reshape(512, 512)
            for n in range(4):
                cols = slice(n * 256, (n + 1) * 256)
                o = jnp.dot(rows, wz[:, cols], preferred_element_type=F32) + brow[:, cols]
                dst[:, :, cols] = o.astype(BF).reshape(4, 128, 256)

        forward(1 - core, osib)
        loop(0, 4, lambda i: os_send(i, True))
        forward(core, osend)

    def output_sums():
        def one(i):
            xx = lax.rem(x + i, 4)
            rcopy(oswap.at[xx], oswap.at[xx], os_s.at[0], os_r.at[xx], g, sib).wait_recv()
            osend[xx] = (osend[xx].astype(F32) + oswap[xx].astype(F32)).astype(BF)

            @pl.when(i < 4)
            def _():
                o_send(i, True)

        loop(1, 5, one)
        oland[x] = osend[x]

    def first_chunk(i):
        @pl.when(i == 0)
        def _():
            loop(0, 8, lambda k: v_relay(k * 2 + 1 - core).wait_recv())
            local[3].wait()
            pcopy.wait_recv()


    def chunk(i):
        k = jnp.where(i < 3, i + 1, jnp.where(i < 5, i - 2, jnp.where(i == 6, 3, 0)))
        other = (i < 3) | (i == 5)
        z = lax.rem(cz + k * (1 + 2 * core), 4)
        c = z * 2 + lax.rem(ch + jnp.where(other, 1, 0), 2)

        @pl.when(i == 3)
        def _():
            student_forward()

        @pl.when(i == 4)
        def _():
            output_sums()

        first_chunk(i)

        def at(n):
            return lambda: attend(core, n, qo.at[n], qs.at[n], keys, values, S, mx, acc, att)

        lax.switch(c, [at(n) for n in range(8)])
        for n in range(4):
            cols = slice(n * 256, (n + 1) * 256)
            p = jnp.dot(att[:, :512], proj_o[:, cols], preferred_element_type=F32)
            p = p + jnp.dot(att[:, 512:], proj_s[:, cols], preferred_element_type=F32)
            tsend[c, :, cols] = p.astype(BF)

        @pl.when(k > 0)
        def _():
            ta_send(c, True)

        @pl.when(other)
        def _():
            tb_send(z, True)

        @pl.when(jnp.logical_not(other) & (k > 0))
        def _():
            rcopy(tb.at[z], tb.at[z], tb_s.at[0], tb_r.at[z], g, sib).wait_recv()
            tbsum[z] = (tsend[c, :, B].astype(F32) + tb[z].astype(F32)).astype(BF)
            tb2_send(z, True)

        @pl.when(i == 5)
        def _():
            total = tsend[c, :, A].astype(F32)
            for k in range(1, 4):
                zz = lax.rem(cz + k, 4)
                ta_wait(1 - ch, zz)
                total = total + ta[1 - ch, zz].astype(F32)
            ta2[0] = total.astype(BF)
            ta2_send().start()

    loop(0, 8, chunk)
    for j in range(8):
        xt[:, j * 128:(j + 1) * 128] = jnp.transpose(xland[j])
    total = tsend[chip, :, A].astype(F32)
    for k in range(1, 4):
        zz = lax.rem(cz + k, 4)
        ta_wait(ch, zz)
        total = total + ta[ch, zz].astype(F32)
    ta2_send().wait_recv()
    total = total + ta2[1].astype(F32)
    tsum[:, :, A] = total.astype(BF).reshape(8, 16, 512)
    rcopy(tb.at[cz], tb.at[cz], tb_s.at[0], tb_r.at[cz], g, sib).wait_recv()
    total = tsend[chip, :, B].astype(F32) + tb[cz].astype(F32)
    for k in range(1, 4):
        zz = lax.rem(cz + k, 4)
        rcopy(tb2.at[zz], tb2.at[zz], tb2_s.at[0], tb2_r.at[zz], g, sib).wait_recv()
        total = total + tb2[zz].astype(F32)
    tsum[:, :, B] = total.astype(BF).reshape(8, 16, 512)

    def p_send(i, start):
        j = lax.rem(g + i, 8)
        copy = rcopy(tsum.at[j], pland.at[g], p_s.at[j], p_r.at[g], j, t)
        if start:
            copy.start()
        else:
            copy.wait_send()

    loop(1, 8, lambda i: p_send(i, True))
    pland[g] = tsum[g]

    def o_wait(i):
        j = lax.rem(x + i, 4)
        rcopy(oland.at[j], oland.at[j], o_s.at[0], o_r.at[j], g, sib).wait_recv()

    loop(1, 4, o_wait)

    def p_wait(i):
        j = lax.rem(g + i, 8)
        rcopy(pland.at[j], pland.at[j], p_s.at[0], p_r.at[j], g, sib).wait_recv()

    loop(1, 8, p_wait)
    keep = jnp.where(ids_in[...] < TEXT_IDS, 1.0, 0.0).astype(F32)
    keep = jnp.transpose(jnp.broadcast_to(keep, (128, 128)))
    keep = jnp.concatenate([keep, keep], axis=1)

    def errors(n):
        cols = slice(n * 256, (n + 1) * 256)
        for k in range(8):
            rows = slice(k * 16, (k + 1) * 16)
            o = oland[0, rows, cols].astype(F32)
            for j in range(1, 4):
                o = o + oland[j, rows, cols].astype(F32)
            eland[m, rows, cols] = (keep[rows] * (o - pland[own_in[k], :, cols].astype(F32))).astype(BF)

    def cols_of(n):
        return pl.ds(n * 256, 256)

    def e_send(dx, n):
        here = eland.at[m, :, cols_of(n)]
        return rcopy(here, here, e_s.at[dx * 4 + n], e_r.at[dx * 4 + n], yl * 4 + lax.rem(x + dx, 4), t)

    def e_relay(dx, n):
        xx = lax.rem(x + dx, 4)
        here = eland.at[core * 4 + xx, :, cols_of(n)]
        return rcopy(here, here, re_s.at[xx * 4 + n], re_r.at[xx * 4 + n], g, sib)

    def e_begin(n):
        errors(n)
        for dx in (2, 1, 3):
            e_send(dx, n).start()
        e_relay(0, n).start()

    def e_pass(n):
        for dx in (1, 3, 2):
            e_send(dx, n).wait_recv()
            e_relay(4 - dx, n).start()

    row = lax.broadcasted_iota(jnp.int32, (32, 256), 0)

    def g_send(i, n, start):
        here = (core == yl) & (i == t)
        src, dst = wsend.at[i, :, cols_of(n)], wgland.at[src16, :, cols_of(n)]

        if start:
            @pl.when(here)
            def _():
                pltpu.make_async_copy(src, dst, g_r.at[n * 16 + src16]).start()

        @pl.when(jnp.logical_not(here))
        def _():
            copy = rcopy(src, dst, g_s.at[n * 16 + i], g_r.at[n * 16 + src16], core * 4 + x, i)
            if start:
                copy.start()
            else:
                copy.wait_send()

    def weight_grad(n):
        if n < 3:
            for k in range(4):
                e_relay(k, n).wait_recv()
        cols = slice(n * 256, (n + 1) * 256)
        eb = jnp.zeros((8, 256), F32)
        lb = jnp.zeros((8, 256), F32)
        for j in range(8):
            ef = eland[j, :, cols].astype(F32)
            for r in range(16):
                er = ef[r * 8:(r + 1) * 8]
                eb = eb + er
                lb = lb + er * er
        wg[...] = jnp.dot(xt[...], eland[:, :, cols].reshape(1024, 256), preferred_element_type=F32)
        esum = jnp.sum(eb, axis=0, keepdims=True)
        lsum = jnp.sum(lb, axis=0, keepdims=True)
        ehi = esum.astype(BF).astype(F32)
        lhi = lsum.astype(BF).astype(F32)
        for i in range(16):
            v = wg[pl.ds(off + (28 * i) // 8 * 8, 32), :]
            if (28 * i) % 8:
                v = pltpu.roll(v, 28, 0)
            for r, e in enumerate([ehi, esum - ehi, lhi, lsum - lhi]):
                v = jnp.where(row == 28 + r, e, v)
            wsend[i, :, cols] = v.astype(BF)
        loop(0, 16, lambda i: g_send(lax.rem(t + i, 16), n, True))

    for n in range(4):
        e_begin(n)
    for n in range(3):
        e_pass(n)
        weight_grad(n)
    e_pass(3)
    for k in range(4):
        e_relay(k, 3).wait_recv()

    def i_send(k, j, slot, start):
        dg, dt = member(j)
        copy = rcopy(igsend.at[k], igland.at[slot], i_s.at[k], i_r.at[slot], dg, dt)
        if start:
            copy.start()
        else:
            copy.wait_send()

    pairs = [(2, wz, m), (1, wz, m), (3, wz, m), (0, wz, m)]
    ig_own = [pltpu.make_async_copy(igsend.at[6], igland.at[m], i_r.at[m])]
    for k, (dx, w, slot) in enumerate(pairs):
        if k == 3:
            weight_grad(3)
        xx = lax.rem(x + dx, 4)
        mine, other = core * 4 + xx, (1 - core) * 4 + xx
        e = jnp.concatenate([eland[mine], eland[other]], axis=0)
        ig = lax.dot_general(e, w[...], (((1,), (1,)), ((), ())), preferred_element_type=F32).astype(BF)
        igsend[2 * k] = ig[:128]
        igsend[2 * k + 1] = ig[128:]
        if dx:
            i_send(2 * k, mine, slot, True)
        else:
            ig_own[0].start()
        i_send(2 * k + 1, other, slot, True)

    def g_wait(i):
        for n in range(4):
            here = wgland.at[i, :, cols_of(n)]
            pltpu.make_async_copy(wsend.at[i, :, cols_of(n)], here, g_r.at[n * 16 + i]).wait()

    loop(0, 16, g_wait)
    for copy in ig_own:
        copy.wait()

    def i_wait(i):
        @pl.when(i != m)
        def _():
            rcopy(igland.at[i], igland.at[i], i_s.at[0], i_r.at[i], g, sib).wait_recv()

    loop(0, 8, i_wait)
    loop(1, 8, lambda i: k_send(i, False))
    loop(1, 8, lambda i: v_send(i, False))
    qcopy.wait_send()
    pcopy.wait_send()
    loop(0, 8, lambda i: k_relay(i * 2 + core).wait_send())
    loop(0, 8, lambda i: v_relay(i * 2 + core).wait_send())
    loop(0, 4, lambda i: w_first(i, False))
    w_second(False)
    loop(1, 8, lambda i: x_send(i, False))
    loop(0, 4, lambda i: os_send(i, False))
    loop(1, 4, lambda i: o_send(i, False))
    loop(2, 8, lambda i: ta_send(lax.rem(cz * 2 + i, 8), False))
    loop(0, 4, lambda i: tb_send(i, False))
    loop(1, 4, lambda i: tb2_send(lax.rem(cz + i, 4), False))
    ta2_send().wait_send()
    loop(1, 8, lambda i: p_send(i, False))
    for n in range(4):
        for dx in (1, 2, 3):
            e_send(dx, n).wait_send()
        for dx in range(4):
            e_relay(dx, n).wait_send()
        loop(0, 16, lambda i: g_send(i, n, False))
    for k, (dx, w, slot) in enumerate(pairs):
        xx = lax.rem(x + dx, 4)
        if dx:
            i_send(2 * k, core * 4 + xx, slot, False)
        i_send(2 * k + 1, (1 - core) * 4 + xx, slot, False)


def finish(wg_in, ig_in, wg_out, bias_out, loss_out, ig_out, wgland, igland, sem):
    d = lax.axis_index("grp") * 16 + lax.axis_index("tp")
    wg_copy = pltpu.make_async_copy(wg_in, wgland, sem.at[0])
    ig_copy = pltpu.make_async_copy(ig_in, igland, sem.at[1])
    wg_copy.start()
    ig_copy.start()
    wg_copy.wait()
    total = wgland[0].astype(F32)
    for i in range(1, 16):
        total = total + wgland[i].astype(F32)
    wg_out[...] = total[:28]
    small = total[24:32]
    loss_out[...] = jnp.sum(small[6:8], axis=(0, 1), keepdims=True) / 32768.0
    both = jnp.broadcast_to(small[4:5] + small[5:6], (8, 1024))
    both = pltpu.roll(both, lax.rem(1024 - d * 8, 1024), 1)
    bias_out[...] = both[0:1, 0:8]
    ig_copy.wait()
    for b in range(4):
        ig_out[:, b * 896:b * 896 + 384] = igland[2 * b, :, :384]
        ig_out[:, b * 896 + 384:b * 896 + 512] = igland[2 * b, :, 384:] + igland[2 * b + 1, :, :128]
        ig_out[:, b * 896 + 512:(b + 1) * 896] = igland[2 * b + 1, :, 128:]


def on_device(queries, keys_values, projector, ownership, token_ids, student_input, student_weight, student_bias):
    hbm = pl.BlockSpec(memory_space=pl.ANY)
    vmem = pl.BlockSpec(memory_space=pltpu.VMEM)
    smem = pl.BlockSpec(memory_space=pltpu.SMEM)
    dma = pltpu.SemaphoreType.DMA
    V = pltpu.VMEM
    wgland, igland = pl.pallas_call(
        kernel,
        out_shape=(jax.ShapeDtypeStruct((16, 32, 1024), BF), jax.ShapeDtypeStruct((8, 128, 512), BF)),
        in_specs=[hbm, hbm, hbm, smem, vmem, hbm, vmem, vmem],
        out_specs=(hbm, hbm),
        scratch_shapes=[
            V((8, 128, 512), BF), V((8, 128, 512), BF), V((2048, 128), BF), V((2048, 128), BF),
            V((1024, 2048), F32), V((1024, 128), F32), V((1024, 256), F32), V((128, 1024), BF),
            V((512, 1024), BF), V((512, 1024), BF), V((8, 128, 1024), BF),
            V((2, 4, 128, 512), BF), V((2, 128, 512), BF), V((4, 128, 512), BF), V((4, 128, 512), BF),
            V((4, 128, 512), BF), V((8, 16, 1024), BF), V((8, 16, 1024), BF),
            V((8, 128, 512), BF), V((512, 1024), BF), V((32, 1024), BF), V((16, 32, 1024), BF),
            V((512, 1024), BF), V((1, 1024), F32),
            V((4, 128, 1024), BF), V((4, 128, 1024), BF), V((4, 128, 1024), BF), V((4, 128, 1024), BF),
            V((8, 128, 1024), BF), V((512, 256), F32), V((16, 32, 1024), BF), V((8, 128, 512), BF),
            dma((5,)), dma((2,)), dma((2,)), dma((8,)), dma((16,)), dma((8,)), dma((16,)), dma((8,)), dma((8,)),
            dma((22,)), dma((16,)), dma((8,)), dma((8,)), dma((4,)), dma((4,)), dma((4,)), dma((4,)),
            dma((8,)), dma((8,)), dma((4,)), dma((4,)), dma((1,)), dma((1,)), dma((4,)), dma((4,)),
            dma((8,)), dma((8,)), dma((16,)), dma((16,)), dma((16,)), dma((16,)),
            dma((64,)), dma((64,)), dma((8,)), dma((8,)),
            pltpu.SemaphoreType.REGULAR, pltpu.SemaphoreType.REGULAR,
        ],
        compiler_params=pltpu.CompilerParams(
            collective_id=0, has_side_effects=True, vmem_limit_bytes=60 * 2 ** 20),
        cost_estimate=pl.CostEstimate(flops=9 * 10 ** 9, bytes_accessed=8 * 10 ** 6, transcendentals=9 * 10 ** 6),
    )(queries.reshape(8, 2, 128, 512), keys_values[0], projector, ownership, token_ids.reshape(1, 128),
      student_input, student_weight, student_bias.reshape(1, 8))
    wg, bias, loss, ig = pl.pallas_call(
        finish,
        out_shape=(jax.ShapeDtypeStruct((28, 1024), F32), jax.ShapeDtypeStruct((1, 8), F32),
                   jax.ShapeDtypeStruct((1, 1), F32), jax.ShapeDtypeStruct((128, 3584), BF)),
        in_specs=[hbm, hbm],
        out_specs=(vmem, vmem, vmem, vmem),
        scratch_shapes=[V((16, 32, 1024), BF), V((8, 128, 512), BF), dma((2,))],
        compiler_params=pltpu.CompilerParams(vmem_limit_bytes=60 * 2 ** 20),
    )(wgland, igland)
    return loss.reshape(()), wg, bias.reshape(8), ig


def solution(mesh):
    return jax.shard_map(
        on_device,
        mesh=mesh,
        in_specs=(
            P("grp", None, "tp"), P("grp", "tp", None), P("tp", None), P(), P(("grp", "tp")),
            P(("grp", "tp"), None), P(("grp", "tp"), None), P(("grp", "tp")),
        ),
        out_specs=(P(), P(("grp", "tp"), None), P(("grp", "tp")), P(("grp", "tp"), None)),
        check_vma=False,
    )
```

```python
import functools

import jax
import jax.numpy as jnp
from jax import lax
from jax.experimental import pallas as pl
from jax.experimental.pallas import tpu as pltpu
from jax.sharding import PartitionSpec as P

MESH = pl.DeviceIdType.MESH
TEXT_IDS = 151643
SCALE = 128 ** -0.5 * 1.4426950408889634
BF = jnp.bfloat16
F32 = jnp.float32


def rcopy(src, dst, send_sem, recv_sem, grp, tp):
    return pltpu.make_async_remote_copy(
        src_ref=src, dst_ref=dst, send_sem=send_sem, recv_sem=recv_sem,
        device_id=(grp, tp), device_id_type=MESH)


def loop(first, last, body):
    lax.fori_loop(first, last, lambda i, carry: (body(i), carry)[1], 0)


def attend(core, c, qo, qs, keys, values, S, mx, acc, out):
    L = 256 * (c + 1)
    q = jnp.concatenate([r[:, h * 128:(h + 1) * 128] for r in (qo, qs) for h in range(4)], axis=0)
    row = lax.broadcasted_iota(jnp.int32, (128, 256), 0) + core * 128
    keep = row >= lax.broadcasted_iota(jnp.int32, (128, 256), 1)
    for a in range(0, L, 512):
        b = min(a + 512, L)
        s_all = lax.dot_general(q, keys[a:b, :], (((1,), (1,)), ((), ())), preferred_element_type=F32)
        for h in range(8):
            hr = slice(h * 128, (h + 1) * 128)
            s = s_all[hr]
            if b == L:
                last = jnp.where(keep, s[:, b - a - 256:], -1e30)
                s = last if b - a == 256 else jnp.concatenate([s[:, :256], last], axis=1)
            S[hr, a:b] = s
            m = s[:, :128]
            for w in range(128, b - a, 128):
                m = jnp.maximum(m, s[:, w:w + 128])
            if a:
                m = jnp.maximum(mx[hr, :], m)
            if b == L:
                m = jnp.broadcast_to(jnp.max(m, axis=1, keepdims=True) * SCALE, (128, 128))
            mx[hr, :] = m
    for a in range(0, L, 1024):
        b = min(a + 1024, L)
        vt = values[a:b, :]
        vt = jnp.concatenate([vt, jnp.ones_like(vt)], axis=1)
        ps = []
        for h in range(8):
            hr = slice(h * 128, (h + 1) * 128)
            m = mx[hr, :]
            ps.append(jnp.concatenate(
                [jnp.exp2(S[hr, w:w + 128] * SCALE - m).astype(BF) for w in range(a, b, 128)], axis=1))
        o = jnp.dot(jnp.concatenate(ps, axis=0), vt, preferred_element_type=F32)
        if a:
            o = o + acc[...]
        if b < L:
            acc[...] = o
    for h in range(8):
        r = o[h * 128:(h + 1) * 128]
        out[:, h * 128:(h + 1) * 128] = (r[:, :128] / r[:, 128:]).astype(BF)


def kernel(q_in, kv_in, proj_in, own_in, ids_in, x_in, w_in, b_in,
           wgland, igland,
           qo, qs, keys, values, S, mx, acc, att, proj_o, proj_s, tsend, ta, ta2, tb, tbsum, tb2, tsum, pland,
           xland, xt, w_pad, wland, wz, brow, osib, oswap, osend, oland, eland, wg, wsend, igsend,
           l_sem, qp_s, qp_r, k_s, k_r, v_s, v_r, rk_s, rv_s, w_s, w_r, x_s, x_r, os_s, os_r, o_s, o_r,
           ta_s, ta_r, tb_s, tb_r, ta2_s, ta2_r, tb2_s, tb2_r, p_s, p_r, e_s, e_r, re_s, re_r, g_s, g_r, i_s, i_r, round2, round3):
    g = lax.axis_index("grp")
    t = lax.axis_index("tp")
    x, yl = lax.rem(g, 4), g // 4
    core, chip = lax.rem(t, 2), t // 2
    sib = chip * 2 + 1 - core
    m = core * 4 + x
    src16 = chip * 2 + yl

    def member(i):
        return yl * 4 + lax.rem(i, 4), chip * 2 + i // 4

    own_kv = pl.ds(pl.multiple_of(t * 128, 128), 128)
    kcol = pl.ds(pl.multiple_of(chip * 128, 128), 128)
    vcol = pl.ds(pl.multiple_of(1024 + chip * 128, 128), 128)

    def window(i):
        return pl.ds(pl.multiple_of((i // 2) * 896 + lax.rem(i, 2) * 384, 128), 512)

    local = [
        pltpu.make_async_copy(kv_in.at[:, kcol], keys.at[own_kv, :], l_sem.at[0]),
        pltpu.make_async_copy(kv_in.at[:, vcol], values.at[own_kv, :], l_sem.at[1]),
        pltpu.make_async_copy(q_in.at[:, core], qo, l_sem.at[2]),
        pltpu.make_async_copy(proj_in, proj_o, l_sem.at[3]),
        pltpu.make_async_copy(x_in.at[:, window(m)], xland.at[m], l_sem.at[4]),
    ]
    for copy in local:
        copy.start()

    lane = lax.broadcasted_iota(jnp.int32, (4, 1024), 1) - (g * 16 + t) * 8
    first = lax.broadcasted_iota(jnp.int32, (4, 1024), 0) == 0
    b_row = jnp.zeros((4, 1024), F32)
    for r in range(8):
        b_row = jnp.where(first & (lane == r), jnp.broadcast_to(b_in[:, r:r + 1].astype(F32), (4, 1024)), b_row)
    w_pad[...] = jnp.concatenate([w_in[...].astype(F32), b_row], axis=0).astype(BF)

    barrier = pltpu.get_barrier_semaphore()

    def greet(sem):
        def tell(grp, tp):
            pl.semaphore_signal(sem, inc=1, device_id=(grp, tp), device_id_type=MESH)

        loop(1, 8, lambda i: tell(g, lax.rem(chip + i, 8) * 2 + core))
        tell(g, sib)
        loop(1, 4, lambda i: tell(yl * 4 + lax.rem(x + i, 4), t))
        tell((1 - yl) * 4 + x, t)

    greet(barrier)
    pl.semaphore_wait(barrier, 12)

    def kv_cols(q):
        return (pl.ds(pl.multiple_of(q * 128, 128), 128),
                pl.ds(pl.multiple_of(1024 + q * 128, 128), 128))

    def k_send(i, start):
        q = lax.rem(chip + i * (1 + 6 * core), 8)
        a = rcopy(kv_in.at[:, kv_cols(q)[0]], keys.at[own_kv, :], k_s.at[q], k_r.at[t], g, q * 2 + core)
        if start:
            a.start()
        else:
            a.wait_send()

    def v_send(i, start):
        q = lax.rem(chip + i * (1 + 6 * core), 8)
        a = rcopy(kv_in.at[:, kv_cols(q)[1]], values.at[own_kv, :], v_s.at[q], v_r.at[t], g, q * 2 + core)
        if start:
            a.start()
        else:
            a.wait_send()

    loop(1, 8, lambda i: k_send(i, True))
    qcopy = rcopy(q_in.at[:, 1 - core], qs, qp_s.at[0], qp_r.at[0], g, sib)
    pcopy = rcopy(proj_in, proj_s, qp_s.at[1], qp_r.at[1], g, sib)
    qcopy.start()
    loop(1, 8, lambda i: v_send(i, True))
    greet(round2)

    def rows_of(src):
        return pl.ds(pl.multiple_of(src * 128, 128), 128)

    def k_relay(src):
        rows = rows_of(src)
        return rcopy(keys.at[rows, :], keys.at[rows, :], rk_s.at[src // 2], k_r.at[src], g, sib)

    def v_relay(src):
        rows = rows_of(src)
        return rcopy(values.at[rows, :], values.at[rows, :], rv_s.at[src // 2], v_r.at[src], g, sib)

    def k_pass(i):
        src = lax.rem(chip + i * (7 - 6 * core), 8) * 2 + core
        k_relay(src).wait_recv()
        k_relay(src).start()

    def v_pass(i):
        src = lax.rem(chip + i * (7 - 6 * core), 8) * 2 + core
        v_relay(src).wait_recv()
        v_relay(src).start()

    local[0].wait()
    k_relay(t).start()
    local[1].wait()
    v_relay(t).start()
    loop(1, 8, k_pass)
    pl.semaphore_wait(round2, 12)
    pl.semaphore_signal(round3, inc=1, device_id=(g, sib), device_id_type=MESH)

    cz, ch, y = chip // 2, lax.rem(chip, 2), lax.rem(chip, 2) * 2 + yl

    def w_first(i, start):
        zz, yy = lax.rem(cz + i * (1 - core), 4), lax.rem(y + i * core, 4)
        here = (i == 0) & (core == yl)
        if start:
            @pl.when(here)
            def _():
                pltpu.make_async_copy(w_pad, wland.at[t], w_r.at[t]).start()

        @pl.when(jnp.logical_not(here))
        def _():
            copy = rcopy(w_pad, wland.at[t], w_s.at[i], w_r.at[t],
                         lax.rem(yy, 2) * 4 + x, zz * 4 + yy // 2 * 2 + yl)
            if start:
                copy.start()
            else:
                copy.wait_send()

    def w_wait(i):
        pltpu.make_async_copy(w_pad, wland.at[i], w_r.at[i]).wait()

    def w_along_y(i, start):
        slot = i * 4 + ch * 2
        if start:
            w_wait(slot)
        for k in range(1, 4):
            yy = lax.rem(y + k, 4)
            copy = rcopy(wland.at[slot], wland.at[slot], w_s.at[4 + i * 3 + k - 1], w_r.at[slot],
                         lax.rem(yy, 2) * 4 + x, cz * 4 + yy // 2 * 2 + core)
            if start:
                copy.start()
            else:
                copy.wait_send()

    def w_along_z(i, start):
        slot = cz * 4 + i * 2 + 1
        if start:
            w_wait(slot)
        for k in range(1, 4):
            zz = lax.rem(cz + k, 4)
            copy = rcopy(wland.at[slot], wland.at[slot], w_s.at[16 + i * 3 + k - 1], w_r.at[slot],
                         g, zz * 4 + ch * 2 + core)
            if start:
                copy.start()
            else:
                copy.wait_send()

    def w_second(start):
        @pl.when(core == yl)
        def _():
            loop(0, 4, lambda i: w_along_y(i, start))

        loop(0, 2, lambda i: w_along_z(i, start))

    def w_late(i):
        early_y = (lax.rem(i, 2) == 0) & (core == yl) & (lax.rem(i // 2, 2) == ch)
        early_z = (lax.rem(i, 2) == 1) & (i // 4 == cz)

        @pl.when(jnp.logical_not(early_y | early_z))
        def _():
            w_wait(i)

    def x_send(i, start):
        j = lax.rem(m + i, 8)
        dg, dt = member(j)
        copy = rcopy(x_in.at[:, window(j)], xland.at[m], x_s.at[j], x_r.at[m], dg, dt)
        if start:
            copy.start()
        else:
            copy.wait_send()

    pl.semaphore_wait(round3, 1)
    loop(0, 4, lambda i: w_first(i, True))
    loop(1, 8, lambda i: x_send(i, True))
    loop(1, 8, v_pass)
    pcopy.start()
    w_second(True)
    loop(0, 8, lambda i: k_relay(i * 2 + 1 - core).wait_recv())
    local[2].wait()
    qcopy.wait_recv()

    A, B = pl.ds(0, 512), pl.ds(512, 512)

    def ta_send(c, start):
        copy = rcopy(tsend.at[c, :, A], ta.at[lax.rem(c, 2), cz], ta_s.at[c], ta_r.at[lax.rem(c, 2) * 4 + cz],
                     g, (c // 2 * 2 + ch) * 2 + core)
        if start:
            copy.start()
        else:
            copy.wait_send()

    def ta_wait(h, z):
        rcopy(ta.at[h, z], ta.at[h, z], ta_s.at[0], ta_r.at[h * 4 + z], g, sib).wait_recv()

    def ta2_send():
        return rcopy(ta2.at[0], ta2.at[1], ta2_s.at[0], ta2_r.at[0], g, (cz * 2 + 1 - ch) * 2 + core)

    def tb_send(z, start):
        copy = rcopy(tsend.at[z * 2 + 1 - ch, :, B], tb.at[z], tb_s.at[z], tb_r.at[z],
                     g, (cz * 2 + 1 - ch) * 2 + core)
        if start:
            copy.start()
        else:
            copy.wait_send()

    def tb2_send(z, start):
        copy = rcopy(tbsum.at[z], tb2.at[cz], tb2_s.at[z], tb2_r.at[cz], g, (z * 2 + ch) * 2 + core)
        if start:
            copy.start()
        else:
            copy.wait_send()

    def os_send(i, start):
        copy = rcopy(osib.at[i], oswap.at[i], os_s.at[i], os_r.at[i], g, sib)
        if start:
            copy.start()
        else:
            copy.wait_send()

    def o_send(i, start):
        xx = lax.rem(x + i, 4)
        copy = rcopy(osend.at[xx], oland.at[x], o_s.at[xx], o_r.at[x], yl * 4 + xx, t)
        if start:
            copy.start()
        else:
            copy.wait_send()

    off = pl.multiple_of(lax.rem(x, 2) * 64, 64)

    def student_forward():
        loop(0, 16, w_late)
        wz[...] = jnp.zeros_like(wz)
        bias = jnp.zeros((1, 1024), F32)
        for a in range(4):
            rows = [wland[4 * a + b].astype(F32) for b in range(4)]
            for r in rows:
                bias = bias + r[28:29]
            wz[pl.ds(off + a * 112, 112), :] = jnp.concatenate([r[:28] for r in rows], axis=0).astype(BF)
        brow[...] = bias
        local[4].wait()

        def fetch(j):
            @pl.when(j != m)
            def _():
                rcopy(xland.at[j], xland.at[j], x_s.at[0], x_r.at[j], g, sib).wait_recv()

        def forward(half, dst):
            first = half * 4
            loop(0, 4, lambda i: fetch(first + i))
            rows = xland[pl.ds(first, 4)].reshape(512, 512)
            for n in range(4):
                cols = slice(n * 256, (n + 1) * 256)
                o = jnp.dot(rows, wz[:, cols], preferred_element_type=F32) + brow[:, cols]
                dst[:, :, cols] = o.astype(BF).reshape(4, 128, 256)

        forward(1 - core, osib)
        loop(0, 4, lambda i: os_send(i, True))
        forward(core, osend)

    def output_sums():
        def one(i):
            xx = lax.rem(x + i, 4)
            rcopy(oswap.at[xx], oswap.at[xx], os_s.at[0], os_r.at[xx], g, sib).wait_recv()
            osend[xx] = (osend[xx].astype(F32) + oswap[xx].astype(F32)).astype(BF)

            @pl.when(i < 4)
            def _():
                o_send(i, True)

        loop(1, 5, one)
        oland[x] = osend[x]

    def first_chunk(i):
        @pl.when(i == 0)
        def _():
            loop(0, 8, lambda k: v_relay(k * 2 + 1 - core).wait_recv())
            local[3].wait()
            pcopy.wait_recv()


    def chunk(i):
        k = jnp.where(i < 3, i + 1, jnp.where(i < 5, i - 2, jnp.where(i == 6, 3, 0)))
        other = (i < 3) | (i == 5)
        z = lax.rem(cz + k * (1 + 2 * core), 4)
        c = z * 2 + lax.rem(ch + jnp.where(other, 1, 0), 2)

        @pl.when(i == 3)
        def _():
            student_forward()

        @pl.when(i == 4)
        def _():
            output_sums()

        first_chunk(i)

        def at(n):
            return lambda: attend(core, n, qo.at[n], qs.at[n], keys, values, S, mx, acc, att)

        lax.switch(c, [at(n) for n in range(8)])
        for n in range(4):
            cols = slice(n * 256, (n + 1) * 256)
            p = jnp.dot(att[:, :512], proj_o[:, cols], preferred_element_type=F32)
            p = p + jnp.dot(att[:, 512:], proj_s[:, cols], preferred_element_type=F32)
            tsend[c, :, cols] = p.astype(BF)

        @pl.when(k > 0)
        def _():
            ta_send(c, True)

        @pl.when(other)
        def _():
            tb_send(z, True)

        @pl.when(jnp.logical_not(other) & (k > 0))
        def _():
            rcopy(tb.at[z], tb.at[z], tb_s.at[0], tb_r.at[z], g, sib).wait_recv()
            tbsum[z] = (tsend[c, :, B].astype(F32) + tb[z].astype(F32)).astype(BF)
            tb2_send(z, True)

        @pl.when(i == 5)
        def _():
            total = tsend[c, :, A].astype(F32)
            for k in range(1, 4):
                zz = lax.rem(cz + k, 4)
                ta_wait(1 - ch, zz)
                total = total + ta[1 - ch, zz].astype(F32)
            ta2[0] = total.astype(BF)
            ta2_send().start()

    loop(0, 8, chunk)
    for j in range(8):
        xt[:, j * 128:(j + 1) * 128] = jnp.transpose(xland[j])
    total = tsend[chip, :, A].astype(F32)
    for k in range(1, 4):
        zz = lax.rem(cz + k, 4)
        ta_wait(ch, zz)
        total = total + ta[ch, zz].astype(F32)
    ta2_send().wait_recv()
    total = total + ta2[1].astype(F32)
    tsum[:, :, A] = total.astype(BF).reshape(8, 16, 512)
    rcopy(tb.at[cz], tb.at[cz], tb_s.at[0], tb_r.at[cz], g, sib).wait_recv()
    total = tsend[chip, :, B].astype(F32) + tb[cz].astype(F32)
    for k in range(1, 4):
        zz = lax.rem(cz + k, 4)
        rcopy(tb2.at[zz], tb2.at[zz], tb2_s.at[0], tb2_r.at[zz], g, sib).wait_recv()
        total = total + tb2[zz].astype(F32)
    tsum[:, :, B] = total.astype(BF).reshape(8, 16, 512)

    def p_send(i, start):
        j = lax.rem(g + i, 8)
        copy = rcopy(tsum.at[j], pland.at[g], p_s.at[j], p_r.at[g], j, t)
        if start:
            copy.start()
        else:
            copy.wait_send()

    loop(1, 8, lambda i: p_send(i, True))
    pland[g] = tsum[g]

    def o_wait(i):
        j = lax.rem(x + i, 4)
        rcopy(oland.at[j], oland.at[j], o_s.at[0], o_r.at[j], g, sib).wait_recv()

    loop(1, 4, o_wait)

    def p_wait(i):
        j = lax.rem(g + i, 8)
        rcopy(pland.at[j], pland.at[j], p_s.at[0], p_r.at[j], g, sib).wait_recv()

    loop(1, 8, p_wait)
    keep = jnp.where(ids_in[...] < TEXT_IDS, 1.0, 0.0).astype(F32)
    keep = jnp.transpose(jnp.broadcast_to(keep, (128, 128)))
    keep = jnp.concatenate([keep, keep], axis=1)

    def errors(n):
        cols = slice(n * 256, (n + 1) * 256)
        for k in range(8):
            rows = slice(k * 16, (k + 1) * 16)
            o = oland[0, rows, cols].astype(F32)
            for j in range(1, 4):
                o = o + oland[j, rows, cols].astype(F32)
            eland[m, rows, cols] = (keep[rows] * (o - pland[own_in[k], :, cols].astype(F32))).astype(BF)

    def cols_of(n):
        return pl.ds(n * 256, 256)

    def e_send(dx, n):
        here = eland.at[m, :, cols_of(n)]
        return rcopy(here, here, e_s.at[dx * 4 + n], e_r.at[dx * 4 + n], yl * 4 + lax.rem(x + dx, 4), t)

    def e_relay(dx, n):
        xx = lax.rem(x + dx, 4)
        here = eland.at[core * 4 + xx, :, cols_of(n)]
        return rcopy(here, here, re_s.at[xx * 4 + n], re_r.at[xx * 4 + n], g, sib)

    def e_begin(n):
        errors(n)
        for dx in (2, 1, 3):
            e_send(dx, n).start()
        e_relay(0, n).start()

    def e_pass(n):
        for dx in (1, 3, 2):
            e_send(dx, n).wait_recv()
            e_relay(4 - dx, n).start()

    row = lax.broadcasted_iota(jnp.int32, (32, 256), 0)

    def g_send(i, n, start):
        here = (core == yl) & (i == t)
        src, dst = wsend.at[i, :, cols_of(n)], wgland.at[src16, :, cols_of(n)]

        if start:
            @pl.when(here)
            def _():
                pltpu.make_async_copy(src, dst, g_r.at[n * 16 + src16]).start()

        @pl.when(jnp.logical_not(here))
        def _():
            copy = rcopy(src, dst, g_s.at[n * 16 + i], g_r.at[n * 16 + src16], core * 4 + x, i)
            if start:
                copy.start()
            else:
                copy.wait_send()

    def weight_grad(n):
        cols = slice(n * 256, (n + 1) * 256)
        eb = jnp.zeros((8, 256), F32)
        lb = jnp.zeros((8, 256), F32)
        for j in range(8):
            ef = eland[j, :, cols].astype(F32)
            for r in range(16):
                er = ef[r * 8:(r + 1) * 8]
                eb = eb + er
                lb = lb + er * er
        wg[...] = jnp.dot(xt[...], eland[:, :, cols].reshape(1024, 256), preferred_element_type=F32)
        esum = jnp.sum(eb, axis=0, keepdims=True)
        lsum = jnp.sum(lb, axis=0, keepdims=True)
        ehi = esum.astype(BF).astype(F32)
        lhi = lsum.astype(BF).astype(F32)
        for i in range(16):
            v = wg[pl.ds(off + (28 * i) // 8 * 8, 32), :]
            if (28 * i) % 8:
                v = pltpu.roll(v, 28, 0)
            for r, e in enumerate([ehi, esum - ehi, lhi, lsum - lhi]):
                v = jnp.where(row == 28 + r, e, v)
            wsend[i, :, cols] = v.astype(BF)
        loop(0, 16, lambda i: g_send(lax.rem(t + i, 16), n, True))

    for n in range(4):
        e_begin(n)
    def e_done(n):
        for k in range(4):
            e_relay(k, n).wait_recv()

    for n in range(2):
        e_pass(n)
        e_done(n)
        weight_grad(n)
    for n in (2, 3):
        e_pass(n)
    for n in (2, 3):
        e_done(n)

    def i_send(k, j, slot, start):
        dg, dt = member(j)
        copy = rcopy(igsend.at[k], igland.at[slot], i_s.at[k], i_r.at[slot], dg, dt)
        if start:
            copy.start()
        else:
            copy.wait_send()

    pairs = [(2, wz, m), (1, wz, m), (3, wz, m), (0, wz, m)]
    ig_own = [pltpu.make_async_copy(igsend.at[6], igland.at[m], i_r.at[m])]
    for k, (dx, w, slot) in enumerate(pairs):
        if k == 2:
            weight_grad(2)
        if k == 3:
            weight_grad(3)
        xx = lax.rem(x + dx, 4)
        mine, other = core * 4 + xx, (1 - core) * 4 + xx
        e = jnp.concatenate([eland[mine], eland[other]], axis=0)
        ig = lax.dot_general(e, w[...], (((1,), (1,)), ((), ())), preferred_element_type=F32).astype(BF)
        igsend[2 * k] = ig[:128]
        igsend[2 * k + 1] = ig[128:]
        if dx:
            i_send(2 * k, mine, slot, True)
        else:
            ig_own[0].start()
        i_send(2 * k + 1, other, slot, True)

    def g_wait(i):
        for n in range(4):
            here = wgland.at[i, :, cols_of(n)]
            pltpu.make_async_copy(wsend.at[i, :, cols_of(n)], here, g_r.at[n * 16 + i]).wait()

    loop(0, 16, g_wait)
    for copy in ig_own:
        copy.wait()

    def i_wait(i):
        @pl.when(i != m)
        def _():
            rcopy(igland.at[i], igland.at[i], i_s.at[0], i_r.at[i], g, sib).wait_recv()

    loop(0, 8, i_wait)
    loop(1, 8, lambda i: k_send(i, False))
    loop(1, 8, lambda i: v_send(i, False))
    qcopy.wait_send()
    pcopy.wait_send()
    loop(0, 8, lambda i: k_relay(i * 2 + core).wait_send())
    loop(0, 8, lambda i: v_relay(i * 2 + core).wait_send())
    loop(0, 4, lambda i: w_first(i, False))
    w_second(False)
    loop(1, 8, lambda i: x_send(i, False))
    loop(0, 4, lambda i: os_send(i, False))
    loop(1, 4, lambda i: o_send(i, False))
    loop(2, 8, lambda i: ta_send(lax.rem(cz * 2 + i, 8), False))
    loop(0, 4, lambda i: tb_send(i, False))
    loop(1, 4, lambda i: tb2_send(lax.rem(cz + i, 4), False))
    ta2_send().wait_send()
    loop(1, 8, lambda i: p_send(i, False))
    for n in range(4):
        for dx in (1, 2, 3):
            e_send(dx, n).wait_send()
        for dx in range(4):
            e_relay(dx, n).wait_send()
        loop(0, 16, lambda i: g_send(i, n, False))
    for k, (dx, w, slot) in enumerate(pairs):
        xx = lax.rem(x + dx, 4)
        if dx:
            i_send(2 * k, core * 4 + xx, slot, False)
        i_send(2 * k + 1, (1 - core) * 4 + xx, slot, False)


def finish(wg_in, ig_in, wg_out, bias_out, loss_out, ig_out, wgland, igland, sem):
    d = lax.axis_index("grp") * 16 + lax.axis_index("tp")
    wg_copy = pltpu.make_async_copy(wg_in, wgland, sem.at[0])
    ig_copy = pltpu.make_async_copy(ig_in, igland, sem.at[1])
    wg_copy.start()
    ig_copy.start()
    wg_copy.wait()
    total = wgland[0].astype(F32)
    for i in range(1, 16):
        total = total + wgland[i].astype(F32)
    wg_out[...] = total[:28]
    small = total[24:32]
    loss_out[...] = jnp.sum(small[6:8], axis=(0, 1), keepdims=True) / 32768.0
    both = jnp.broadcast_to(small[4:5] + small[5:6], (8, 1024))
    both = pltpu.roll(both, lax.rem(1024 - d * 8, 1024), 1)
    bias_out[...] = both[0:1, 0:8]
    ig_copy.wait()
    for b in range(4):
        ig_out[:, b * 896:b * 896 + 384] = igland[2 * b, :, :384]
        ig_out[:, b * 896 + 384:b * 896 + 512] = igland[2 * b, :, 384:] + igland[2 * b + 1, :, :128]
        ig_out[:, b * 896 + 512:(b + 1) * 896] = igland[2 * b + 1, :, 128:]


def on_device(queries, keys_values, projector, ownership, token_ids, student_input, student_weight, student_bias):
    hbm = pl.BlockSpec(memory_space=pl.ANY)
    vmem = pl.BlockSpec(memory_space=pltpu.VMEM)
    smem = pl.BlockSpec(memory_space=pltpu.SMEM)
    dma = pltpu.SemaphoreType.DMA
    V = pltpu.VMEM
    wgland, igland = pl.pallas_call(
        kernel,
        out_shape=(jax.ShapeDtypeStruct((16, 32, 1024), BF), jax.ShapeDtypeStruct((8, 128, 512), BF)),
        in_specs=[hbm, hbm, hbm, smem, vmem, hbm, vmem, vmem],
        out_specs=(hbm, hbm),
        scratch_shapes=[
            V((8, 128, 512), BF), V((8, 128, 512), BF), V((2048, 128), BF), V((2048, 128), BF),
            V((1024, 2048), F32), V((1024, 128), F32), V((1024, 256), F32), V((128, 1024), BF),
            V((512, 1024), BF), V((512, 1024), BF), V((8, 128, 1024), BF),
            V((2, 4, 128, 512), BF), V((2, 128, 512), BF), V((4, 128, 512), BF), V((4, 128, 512), BF),
            V((4, 128, 512), BF), V((8, 16, 1024), BF), V((8, 16, 1024), BF),
            V((8, 128, 512), BF), V((512, 1024), BF), V((32, 1024), BF), V((16, 32, 1024), BF),
            V((512, 1024), BF), V((1, 1024), F32),
            V((4, 128, 1024), BF), V((4, 128, 1024), BF), V((4, 128, 1024), BF), V((4, 128, 1024), BF),
            V((8, 128, 1024), BF), V((512, 256), F32), V((16, 32, 1024), BF), V((8, 128, 512), BF),
            dma((5,)), dma((2,)), dma((2,)), dma((8,)), dma((16,)), dma((8,)), dma((16,)), dma((8,)), dma((8,)),
            dma((22,)), dma((16,)), dma((8,)), dma((8,)), dma((4,)), dma((4,)), dma((4,)), dma((4,)),
            dma((8,)), dma((8,)), dma((4,)), dma((4,)), dma((1,)), dma((1,)), dma((4,)), dma((4,)),
            dma((8,)), dma((8,)), dma((16,)), dma((16,)), dma((16,)), dma((16,)),
            dma((64,)), dma((64,)), dma((8,)), dma((8,)),
            pltpu.SemaphoreType.REGULAR, pltpu.SemaphoreType.REGULAR,
        ],
        compiler_params=pltpu.CompilerParams(
            collective_id=0, has_side_effects=True, vmem_limit_bytes=60 * 2 ** 20),
        cost_estimate=pl.CostEstimate(flops=9 * 10 ** 9, bytes_accessed=8 * 10 ** 6, transcendentals=9 * 10 ** 6),
    )(queries.reshape(8, 2, 128, 512), keys_values[0], projector, ownership, token_ids.reshape(1, 128),
      student_input, student_weight, student_bias.reshape(1, 8))
    wg, bias, loss, ig = pl.pallas_call(
        finish,
        out_shape=(jax.ShapeDtypeStruct((28, 1024), F32), jax.ShapeDtypeStruct((1, 8), F32),
                   jax.ShapeDtypeStruct((1, 1), F32), jax.ShapeDtypeStruct((128, 3584), BF)),
        in_specs=[hbm, hbm],
        out_specs=(vmem, vmem, vmem, vmem),
        scratch_shapes=[V((16, 32, 1024), BF), V((8, 128, 512), BF), dma((2,))],
        compiler_params=pltpu.CompilerParams(vmem_limit_bytes=60 * 2 ** 20),
    )(wgland, igland)
    return loss.reshape(()), wg, bias.reshape(8), ig


def solution(mesh):
    return jax.shard_map(
        on_device,
        mesh=mesh,
        in_specs=(
            P("grp", None, "tp"), P("grp", "tp", None), P("tp", None), P(), P(("grp", "tp")),
            P(("grp", "tp"), None), P(("grp", "tp"), None), P(("grp", "tp")),
        ),
        out_specs=(P(), P(("grp", "tp"), None), P(("grp", "tp")), P(("grp", "tp"), None)),
        check_vma=False,
    )
```

```python
import functools

import jax
import jax.numpy as jnp
from jax import lax
from jax.experimental import pallas as pl
from jax.experimental.pallas import tpu as pltpu
from jax.sharding import PartitionSpec as P

MESH = pl.DeviceIdType.MESH
TEXT_IDS = 151643
SCALE = 128 ** -0.5 * 1.4426950408889634
BF = jnp.bfloat16
F32 = jnp.float32


def rcopy(src, dst, send_sem, recv_sem, grp, tp):
    return pltpu.make_async_remote_copy(
        src_ref=src, dst_ref=dst, send_sem=send_sem, recv_sem=recv_sem,
        device_id=(grp, tp), device_id_type=MESH)


def loop(first, last, body):
    lax.fori_loop(first, last, lambda i, carry: (body(i), carry)[1], 0)


def attend(core, c, qo, qs, keys, values, S, mx, acc, out):
    L = 256 * (c + 1)
    q = jnp.concatenate([r[:, h * 128:(h + 1) * 128] for r in (qo, qs) for h in range(4)], axis=0)
    row = lax.broadcasted_iota(jnp.int32, (128, 256), 0) + core * 128
    keep = row >= lax.broadcasted_iota(jnp.int32, (128, 256), 1)
    for a in range(0, L, 512):
        b = min(a + 512, L)
        s_all = lax.dot_general(q, keys[a:b, :], (((1,), (1,)), ((), ())), preferred_element_type=F32)
        for h in range(8):
            hr = slice(h * 128, (h + 1) * 128)
            s = s_all[hr]
            if b == L:
                last = jnp.where(keep, s[:, b - a - 256:], -1e30)
                s = last if b - a == 256 else jnp.concatenate([s[:, :256], last], axis=1)
            S[hr, a:b] = s
            m = s[:, :128]
            for w in range(128, b - a, 128):
                m = jnp.maximum(m, s[:, w:w + 128])
            if a:
                m = jnp.maximum(mx[hr, :], m)
            if b == L:
                m = jnp.broadcast_to(jnp.max(m, axis=1, keepdims=True) * SCALE, (128, 128))
            mx[hr, :] = m
    for a in range(0, L, 1024):
        b = min(a + 1024, L)
        vt = values[a:b, :]
        vt = jnp.concatenate([vt, jnp.ones_like(vt)], axis=1)
        ps = []
        for h in range(8):
            hr = slice(h * 128, (h + 1) * 128)
            m = mx[hr, :]
            ps.append(jnp.concatenate(
                [jnp.exp2(S[hr, w:w + 128] * SCALE - m).astype(BF) for w in range(a, b, 128)], axis=1))
        o = jnp.dot(jnp.concatenate(ps, axis=0), vt, preferred_element_type=F32)
        if a:
            o = o + acc[...]
        if b < L:
            acc[...] = o
    for h in range(8):
        r = o[h * 128:(h + 1) * 128]
        out[:, h * 128:(h + 1) * 128] = (r[:, :128] / r[:, 128:]).astype(BF)


def kernel(q_in, kv_in, proj_in, own_in, ids_in, x_in, w_in, b_in,
           wgland, igland,
           qo, qs, keys, values, S, mx, acc, att, proj_o, proj_s, tsend, ta, ta2, tb, tbsum, tb2, tsum, pland,
           xland, xt, w_pad, wland, wz, brow, osib, oswap, osend, oland, eland, wg, wsend, igsend,
           l_sem, qp_s, qp_r, k_s, k_r, v_s, v_r, rk_s, rv_s, w_s, w_r, x_s, x_r, os_s, os_r, o_s, o_r,
           ta_s, ta_r, tb_s, tb_r, ta2_s, ta2_r, tb2_s, tb2_r, p_s, p_r, e_s, e_r, re_s, re_r, g_s, g_r, i_s, i_r, round2, round3):
    g = lax.axis_index("grp")
    t = lax.axis_index("tp")
    x, yl = lax.rem(g, 4), g // 4
    core, chip = lax.rem(t, 2), t // 2
    sib = chip * 2 + 1 - core
    m = core * 4 + x
    src16 = chip * 2 + yl

    def member(i):
        return yl * 4 + lax.rem(i, 4), chip * 2 + i // 4

    own_kv = pl.ds(pl.multiple_of(t * 128, 128), 128)
    kcol = pl.ds(pl.multiple_of(chip * 128, 128), 128)
    vcol = pl.ds(pl.multiple_of(1024 + chip * 128, 128), 128)

    def window(i):
        return pl.ds(pl.multiple_of((i // 2) * 896 + lax.rem(i, 2) * 384, 128), 512)

    local = [
        pltpu.make_async_copy(kv_in.at[:, kcol], keys.at[own_kv, :], l_sem.at[0]),
        pltpu.make_async_copy(kv_in.at[:, vcol], values.at[own_kv, :], l_sem.at[1]),
        pltpu.make_async_copy(q_in.at[:, core], qo, l_sem.at[2]),
        pltpu.make_async_copy(proj_in, proj_o, l_sem.at[3]),
        pltpu.make_async_copy(x_in.at[:, window(m)], xland.at[m], l_sem.at[4]),
    ]
    for copy in local:
        copy.start()

    lane = lax.broadcasted_iota(jnp.int32, (4, 1024), 1) - (g * 16 + t) * 8
    first = lax.broadcasted_iota(jnp.int32, (4, 1024), 0) == 0
    b_row = jnp.zeros((4, 1024), F32)
    for r in range(8):
        b_row = jnp.where(first & (lane == r), jnp.broadcast_to(b_in[:, r:r + 1].astype(F32), (4, 1024)), b_row)
    w_pad[...] = jnp.concatenate([w_in[...].astype(F32), b_row], axis=0).astype(BF)

    barrier = pltpu.get_barrier_semaphore()

    def greet(sem):
        def tell(grp, tp):
            pl.semaphore_signal(sem, inc=1, device_id=(grp, tp), device_id_type=MESH)

        loop(1, 8, lambda i: tell(g, lax.rem(chip + i, 8) * 2 + core))
        tell(g, sib)
        loop(1, 4, lambda i: tell(yl * 4 + lax.rem(x + i, 4), t))
        tell((1 - yl) * 4 + x, t)

    greet(barrier)
    pl.semaphore_wait(barrier, 12)

    def kv_cols(q):
        return (pl.ds(pl.multiple_of(q * 128, 128), 128),
                pl.ds(pl.multiple_of(1024 + q * 128, 128), 128))

    def k_send(i, start):
        q = lax.rem(chip + i * (1 + 6 * core), 8)
        a = rcopy(kv_in.at[:, kv_cols(q)[0]], keys.at[own_kv, :], k_s.at[q], k_r.at[t], g, q * 2 + core)
        if start:
            a.start()
        else:
            a.wait_send()

    def v_send(i, start):
        q = lax.rem(chip + i * (1 + 6 * core), 8)
        a = rcopy(kv_in.at[:, kv_cols(q)[1]], values.at[own_kv, :], v_s.at[q], v_r.at[t], g, q * 2 + core)
        if start:
            a.start()
        else:
            a.wait_send()

    loop(1, 8, lambda i: k_send(i, True))
    qcopy = rcopy(q_in.at[:, 1 - core], qs, qp_s.at[0], qp_r.at[0], g, sib)
    pcopy = rcopy(proj_in, proj_s, qp_s.at[1], qp_r.at[1], g, sib)
    qcopy.start()
    loop(1, 8, lambda i: v_send(i, True))
    greet(round2)

    def rows_of(src):
        return pl.ds(pl.multiple_of(src * 128, 128), 128)

    def k_relay(src):
        rows = rows_of(src)
        return rcopy(keys.at[rows, :], keys.at[rows, :], rk_s.at[src // 2], k_r.at[src], g, sib)

    def v_relay(src):
        rows = rows_of(src)
        return rcopy(values.at[rows, :], values.at[rows, :], rv_s.at[src // 2], v_r.at[src], g, sib)

    def k_pass(i):
        src = lax.rem(chip + i * (7 - 6 * core), 8) * 2 + core
        k_relay(src).wait_recv()
        k_relay(src).start()

    def v_pass(i):
        src = lax.rem(chip + i * (7 - 6 * core), 8) * 2 + core
        v_relay(src).wait_recv()
        v_relay(src).start()

    local[0].wait()
    k_relay(t).start()
    local[1].wait()
    v_relay(t).start()
    loop(1, 8, k_pass)
    pl.semaphore_wait(round2, 12)
    pl.semaphore_signal(round3, inc=1, device_id=(g, sib), device_id_type=MESH)

    cz, ch, y = chip // 2, lax.rem(chip, 2), lax.rem(chip, 2) * 2 + yl

    def w_first(i, start):
        zz, yy = lax.rem(cz + i * (1 - core), 4), lax.rem(y + i * core, 4)
        here = (i == 0) & (core == yl)
        if start:
            @pl.when(here)
            def _():
                pltpu.make_async_copy(w_pad, wland.at[t], w_r.at[t]).start()

        @pl.when(jnp.logical_not(here))
        def _():
            copy = rcopy(w_pad, wland.at[t], w_s.at[i], w_r.at[t],
                         lax.rem(yy, 2) * 4 + x, zz * 4 + yy // 2 * 2 + yl)
            if start:
                copy.start()
            else:
                copy.wait_send()

    def w_wait(i):
        pltpu.make_async_copy(w_pad, wland.at[i], w_r.at[i]).wait()

    def w_along_y(i, start):
        slot = i * 4 + ch * 2
        if start:
            w_wait(slot)
        for k in range(1, 4):
            yy = lax.rem(y + k, 4)
            copy = rcopy(wland.at[slot], wland.at[slot], w_s.at[4 + i * 3 + k - 1], w_r.at[slot],
                         lax.rem(yy, 2) * 4 + x, cz * 4 + yy // 2 * 2 + core)
            if start:
                copy.start()
            else:
                copy.wait_send()

    def w_along_z(i, start):
        slot = cz * 4 + i * 2 + 1
        if start:
            w_wait(slot)
        for k in range(1, 4):
            zz = lax.rem(cz + k, 4)
            copy = rcopy(wland.at[slot], wland.at[slot], w_s.at[16 + i * 3 + k - 1], w_r.at[slot],
                         g, zz * 4 + ch * 2 + core)
            if start:
                copy.start()
            else:
                copy.wait_send()

    def w_second(start):
        @pl.when(core == yl)
        def _():
            loop(0, 4, lambda i: w_along_y(i, start))

        loop(0, 2, lambda i: w_along_z(i, start))

    def w_late(i):
        early_y = (lax.rem(i, 2) == 0) & (core == yl) & (lax.rem(i // 2, 2) == ch)
        early_z = (lax.rem(i, 2) == 1) & (i // 4 == cz)

        @pl.when(jnp.logical_not(early_y | early_z))
        def _():
            w_wait(i)

    def x_send(i, start):
        j = lax.rem(m + i, 8)
        dg, dt = member(j)
        copy = rcopy(x_in.at[:, window(j)], xland.at[m], x_s.at[j], x_r.at[m], dg, dt)
        if start:
            copy.start()
        else:
            copy.wait_send()

    pl.semaphore_wait(round3, 1)
    loop(0, 4, lambda i: w_first(i, True))
    loop(1, 8, lambda i: x_send(i, True))
    loop(1, 8, v_pass)
    pcopy.start()
    w_second(True)
    loop(0, 8, lambda i: k_relay(i * 2 + 1 - core).wait_recv())
    local[2].wait()
    qcopy.wait_recv()

    A, B = pl.ds(0, 512), pl.ds(512, 512)

    def ta_send(c, start):
        copy = rcopy(tsend.at[c, :, A], ta.at[lax.rem(c, 2), cz], ta_s.at[c], ta_r.at[lax.rem(c, 2) * 4 + cz],
                     g, (c // 2 * 2 + ch) * 2 + core)
        if start:
            copy.start()
        else:
            copy.wait_send()

    def ta_wait(h, z):
        rcopy(ta.at[h, z], ta.at[h, z], ta_s.at[0], ta_r.at[h * 4 + z], g, sib).wait_recv()

    def ta2_send():
        return rcopy(ta2.at[0], ta2.at[1], ta2_s.at[0], ta2_r.at[0], g, (cz * 2 + 1 - ch) * 2 + core)

    def tb_send(z, start):
        copy = rcopy(tsend.at[z * 2 + 1 - ch, :, B], tb.at[z], tb_s.at[z], tb_r.at[z],
                     g, (cz * 2 + 1 - ch) * 2 + core)
        if start:
            copy.start()
        else:
            copy.wait_send()

    def tb2_send(z, start):
        copy = rcopy(tbsum.at[z], tb2.at[cz], tb2_s.at[z], tb2_r.at[cz], g, (z * 2 + ch) * 2 + core)
        if start:
            copy.start()
        else:
            copy.wait_send()

    def os_send(i, start):
        copy = rcopy(osib.at[i], oswap.at[i], os_s.at[i], os_r.at[i], g, sib)
        if start:
            copy.start()
        else:
            copy.wait_send()

    def o_send(i, start):
        xx = lax.rem(x + i, 4)
        copy = rcopy(osend.at[xx], oland.at[x], o_s.at[xx], o_r.at[x], yl * 4 + xx, t)
        if start:
            copy.start()
        else:
            copy.wait_send()

    off = pl.multiple_of(lax.rem(x, 2) * 64, 64)

    def student_forward():
        loop(0, 16, w_late)
        wz[...] = jnp.zeros_like(wz)
        bias = jnp.zeros((1, 1024), F32)
        for a in range(4):
            rows = [wland[4 * a + b].astype(F32) for b in range(4)]
            for r in rows:
                bias = bias + r[28:29]
            wz[pl.ds(off + a * 112, 112), :] = jnp.concatenate([r[:28] for r in rows], axis=0).astype(BF)
        brow[...] = bias
        local[4].wait()

        def fetch(j):
            @pl.when(j != m)
            def _():
                rcopy(xland.at[j], xland.at[j], x_s.at[0], x_r.at[j], g, sib).wait_recv()

        def forward(half, dst):
            first = half * 4
            loop(0, 4, lambda i: fetch(first + i))
            rows = xland[pl.ds(first, 4)].reshape(512, 512)
            for n in range(4):
                cols = slice(n * 256, (n + 1) * 256)
                o = jnp.dot(rows, wz[:, cols], preferred_element_type=F32) + brow[:, cols]
                dst[:, :, cols] = o.astype(BF).reshape(4, 128, 256)

        forward(1 - core, osib)
        loop(0, 4, lambda i: os_send(i, True))
        forward(core, osend)

    def output_sums():
        def one(i):
            xx = lax.rem(x + i, 4)
            rcopy(oswap.at[xx], oswap.at[xx], os_s.at[0], os_r.at[xx], g, sib).wait_recv()
            osend[xx] = (osend[xx].astype(F32) + oswap[xx].astype(F32)).astype(BF)

            @pl.when(i < 4)
            def _():
                o_send(i, True)

        loop(1, 5, one)
        oland[x] = osend[x]

    def first_chunk(i):
        @pl.when(i == 0)
        def _():
            loop(0, 8, lambda k: v_relay(k * 2 + 1 - core).wait_recv())
            local[3].wait()
            pcopy.wait_recv()


    def chunk(i):
        k = jnp.where(i < 3, i + 1, jnp.where(i < 5, i - 2, jnp.where(i == 6, 3, 0)))
        other = (i < 3) | (i == 5)
        z = lax.rem(cz + k * (1 + 2 * core), 4)
        c = z * 2 + lax.rem(ch + jnp.where(other, 1, 0), 2)

        @pl.when(i == 3)
        def _():
            student_forward()

        @pl.when(i == 4)
        def _():
            output_sums()

        first_chunk(i)

        def at(n):
            return lambda: attend(core, n, qo.at[n], qs.at[n], keys, values, S, mx, acc, att)

        lax.switch(c, [at(n) for n in range(8)])
        for n in range(4):
            cols = slice(n * 256, (n + 1) * 256)
            p = jnp.dot(att[:, :512], proj_o[:, cols], preferred_element_type=F32)
            p = p + jnp.dot(att[:, 512:], proj_s[:, cols], preferred_element_type=F32)
            tsend[c, :, cols] = p.astype(BF)

        @pl.when(k > 0)
        def _():
            ta_send(c, True)

        @pl.when(other)
        def _():
            tb_send(z, True)

        @pl.when(jnp.logical_not(other) & (k > 0))
        def _():
            rcopy(tb.at[z], tb.at[z], tb_s.at[0], tb_r.at[z], g, sib).wait_recv()
            tbsum[z] = (tsend[c, :, B].astype(F32) + tb[z].astype(F32)).astype(BF)
            tb2_send(z, True)

        @pl.when(i == 5)
        def _():
            total = tsend[c, :, A].astype(F32)
            for k in range(1, 4):
                zz = lax.rem(cz + k, 4)
                ta_wait(1 - ch, zz)
                total = total + ta[1 - ch, zz].astype(F32)
            ta2[0] = total.astype(BF)
            ta2_send().start()

    loop(0, 8, chunk)
    for j in range(8):
        xt[:, j * 128:(j + 1) * 128] = jnp.transpose(xland[j])
    total = tsend[chip, :, A].astype(F32)
    for k in range(1, 4):
        zz = lax.rem(cz + k, 4)
        ta_wait(ch, zz)
        total = total + ta[ch, zz].astype(F32)
    ta2_send().wait_recv()
    total = total + ta2[1].astype(F32)
    tsum[:, :, A] = total.astype(BF).reshape(8, 16, 512)
    rcopy(tb.at[cz], tb.at[cz], tb_s.at[0], tb_r.at[cz], g, sib).wait_recv()
    total = tsend[chip, :, B].astype(F32) + tb[cz].astype(F32)
    for k in range(1, 4):
        zz = lax.rem(cz + k, 4)
        rcopy(tb2.at[zz], tb2.at[zz], tb2_s.at[0], tb2_r.at[zz], g, sib).wait_recv()
        total = total + tb2[zz].astype(F32)
    tsum[:, :, B] = total.astype(BF).reshape(8, 16, 512)

    def p_send(i, start):
        j = lax.rem(g + i, 8)
        copy = rcopy(tsum.at[j], pland.at[g], p_s.at[j], p_r.at[g], j, t)
        if start:
            copy.start()
        else:
            copy.wait_send()

    loop(1, 8, lambda i: p_send(i, True))
    pland[g] = tsum[g]

    def o_wait(i):
        j = lax.rem(x + i, 4)
        rcopy(oland.at[j], oland.at[j], o_s.at[0], o_r.at[j], g, sib).wait_recv()

    loop(1, 4, o_wait)

    def p_wait(i):
        j = lax.rem(g + i, 8)
        rcopy(pland.at[j], pland.at[j], p_s.at[0], p_r.at[j], g, sib).wait_recv()

    loop(1, 8, p_wait)
    keep = jnp.where(ids_in[...] < TEXT_IDS, 1.0, 0.0).astype(F32)
    keep = jnp.transpose(jnp.broadcast_to(keep, (128, 128)))
    keep = jnp.concatenate([keep, keep], axis=1)

    def errors(n):
        cols = slice(n * 256, (n + 1) * 256)
        for k in range(8):
            rows = slice(k * 16, (k + 1) * 16)
            o = oland[0, rows, cols].astype(F32)
            for j in range(1, 4):
                o = o + oland[j, rows, cols].astype(F32)
            eland[m, rows, cols] = (keep[rows] * (o - pland[own_in[k], :, cols].astype(F32))).astype(BF)

    def cols_of(n):
        return pl.ds(n * 256, 256)

    def e_send(dx, n):
        here = eland.at[m, :, cols_of(n)]
        return rcopy(here, here, e_s.at[dx * 4 + n], e_r.at[dx * 4 + n], yl * 4 + lax.rem(x + dx, 4), t)

    def e_relay(dx, n):
        xx = lax.rem(x + dx, 4)
        here = eland.at[core * 4 + xx, :, cols_of(n)]
        return rcopy(here, here, re_s.at[xx * 4 + n], re_r.at[xx * 4 + n], g, sib)

    def e_begin(n):
        errors(n)
        for dx in (2, 1, 3):
            e_send(dx, n).start()
        e_relay(0, n).start()

    def e_pass(n):
        for dx in (1, 3, 2):
            e_send(dx, n).wait_recv()
            e_relay(4 - dx, n).start()

    row = lax.broadcasted_iota(jnp.int32, (32, 256), 0)

    def g_send(i, n, start):
        here = (core == yl) & (i == t)
        src, dst = wsend.at[i, :, cols_of(n)], wgland.at[src16, :, cols_of(n)]

        if start:
            @pl.when(here)
            def _():
                pltpu.make_async_copy(src, dst, g_r.at[n * 16 + src16]).start()

        @pl.when(jnp.logical_not(here))
        def _():
            copy = rcopy(src, dst, g_s.at[n * 16 + i], g_r.at[n * 16 + src16], core * 4 + x, i)
            if start:
                copy.start()
            else:
                copy.wait_send()

    def weight_grad(n):
        cols = slice(n * 256, (n + 1) * 256)
        eb = jnp.zeros((8, 256), F32)
        lb = jnp.zeros((8, 256), F32)
        for j in range(8):
            ef = eland[j, :, cols].astype(F32)
            for r in range(16):
                er = ef[r * 8:(r + 1) * 8]
                eb = eb + er
                lb = lb + er * er
        wg[...] = jnp.dot(xt[...], eland[:, :, cols].reshape(1024, 256), preferred_element_type=F32)
        esum = jnp.sum(eb, axis=0, keepdims=True)
        lsum = jnp.sum(lb, axis=0, keepdims=True)
        ehi = esum.astype(BF).astype(F32)
        lhi = lsum.astype(BF).astype(F32)
        for i in range(16):
            v = wg[pl.ds(off + (28 * i) // 8 * 8, 32), :]
            if (28 * i) % 8:
                v = pltpu.roll(v, 28, 0)
            for r, e in enumerate([ehi, esum - ehi, lhi, lsum - lhi]):
                v = jnp.where(row == 28 + r, e, v)
            wsend[i, :, cols] = v.astype(BF)
        loop(0, 16, lambda i: g_send(lax.rem(t + i, 16), n, True))

    for n in range(4):
        if n >= 2:
            for dx in (1, 2, 3):
                e_send(dx, n - 2).wait_send()
        e_begin(n)
    def e_done(n):
        for k in range(4):
            e_relay(k, n).wait_recv()

    for n in range(2):
        e_pass(n)
        e_done(n)
        weight_grad(n)
    for n in (2, 3):
        e_pass(n)
    for n in (2, 3):
        e_done(n)

    def i_send(k, j, slot, start):
        dg, dt = member(j)
        copy = rcopy(igsend.at[k], igland.at[slot], i_s.at[k], i_r.at[slot], dg, dt)
        if start:
            copy.start()
        else:
            copy.wait_send()

    pairs = [(2, wz, m), (1, wz, m), (3, wz, m), (0, wz, m)]
    ig_own = [pltpu.make_async_copy(igsend.at[6], igland.at[m], i_r.at[m])]
    for k, (dx, w, slot) in enumerate(pairs):
        if k == 2:
            weight_grad(2)
        if k == 3:
            weight_grad(3)
        xx = lax.rem(x + dx, 4)
        mine, other = core * 4 + xx, (1 - core) * 4 + xx
        e = jnp.concatenate([eland[mine], eland[other]], axis=0)
        ig = lax.dot_general(e, w[...], (((1,), (1,)), ((), ())), preferred_element_type=F32).astype(BF)
        igsend[2 * k] = ig[:128]
        igsend[2 * k + 1] = ig[128:]
        if dx:
            i_send(2 * k, mine, slot, True)
        else:
            ig_own[0].start()
        i_send(2 * k + 1, other, slot, True)

    def g_wait(i):
        for n in range(4):
            here = wgland.at[i, :, cols_of(n)]
            pltpu.make_async_copy(wsend.at[i, :, cols_of(n)], here, g_r.at[n * 16 + i]).wait()

    loop(0, 16, g_wait)
    for copy in ig_own:
        copy.wait()

    def i_wait(i):
        @pl.when(i != m)
        def _():
            rcopy(igland.at[i], igland.at[i], i_s.at[0], i_r.at[i], g, sib).wait_recv()

    loop(0, 8, i_wait)
    loop(1, 8, lambda i: k_send(i, False))
    loop(1, 8, lambda i: v_send(i, False))
    qcopy.wait_send()
    pcopy.wait_send()
    loop(0, 8, lambda i: k_relay(i * 2 + core).wait_send())
    loop(0, 8, lambda i: v_relay(i * 2 + core).wait_send())
    loop(0, 4, lambda i: w_first(i, False))
    w_second(False)
    loop(1, 8, lambda i: x_send(i, False))
    loop(0, 4, lambda i: os_send(i, False))
    loop(1, 4, lambda i: o_send(i, False))
    loop(2, 8, lambda i: ta_send(lax.rem(cz * 2 + i, 8), False))
    loop(0, 4, lambda i: tb_send(i, False))
    loop(1, 4, lambda i: tb2_send(lax.rem(cz + i, 4), False))
    ta2_send().wait_send()
    loop(1, 8, lambda i: p_send(i, False))
    for n in range(4):
        for dx in (1, 2, 3):
            if n >= 2:
                e_send(dx, n).wait_send()
        for dx in range(4):
            e_relay(dx, n).wait_send()
        loop(0, 16, lambda i: g_send(i, n, False))
    for k, (dx, w, slot) in enumerate(pairs):
        xx = lax.rem(x + dx, 4)
        if dx:
            i_send(2 * k, core * 4 + xx, slot, False)
        i_send(2 * k + 1, (1 - core) * 4 + xx, slot, False)


def finish(wg_in, ig_in, wg_out, bias_out, loss_out, ig_out, wgland, igland, sem):
    d = lax.axis_index("grp") * 16 + lax.axis_index("tp")
    wg_copy = pltpu.make_async_copy(wg_in, wgland, sem.at[0])
    ig_copy = pltpu.make_async_copy(ig_in, igland, sem.at[1])
    wg_copy.start()
    ig_copy.start()
    wg_copy.wait()
    total = wgland[0].astype(F32)
    for i in range(1, 16):
        total = total + wgland[i].astype(F32)
    wg_out[...] = total[:28]
    small = total[24:32]
    loss_out[...] = jnp.sum(small[6:8], axis=(0, 1), keepdims=True) / 32768.0
    both = jnp.broadcast_to(small[4:5] + small[5:6], (8, 1024))
    both = pltpu.roll(both, lax.rem(1024 - d * 8, 1024), 1)
    bias_out[...] = both[0:1, 0:8]
    ig_copy.wait()
    for b in range(4):
        ig_out[:, b * 896:b * 896 + 384] = igland[2 * b, :, :384]
        ig_out[:, b * 896 + 384:b * 896 + 512] = igland[2 * b, :, 384:] + igland[2 * b + 1, :, :128]
        ig_out[:, b * 896 + 512:(b + 1) * 896] = igland[2 * b + 1, :, 128:]


def on_device(queries, keys_values, projector, ownership, token_ids, student_input, student_weight, student_bias):
    hbm = pl.BlockSpec(memory_space=pl.ANY)
    vmem = pl.BlockSpec(memory_space=pltpu.VMEM)
    smem = pl.BlockSpec(memory_space=pltpu.SMEM)
    dma = pltpu.SemaphoreType.DMA
    V = pltpu.VMEM
    wgland, igland = pl.pallas_call(
        kernel,
        out_shape=(jax.ShapeDtypeStruct((16, 32, 1024), BF), jax.ShapeDtypeStruct((8, 128, 512), BF)),
        in_specs=[hbm, hbm, hbm, smem, vmem, hbm, vmem, vmem],
        out_specs=(hbm, hbm),
        scratch_shapes=[
            V((8, 128, 512), BF), V((8, 128, 512), BF), V((2048, 128), BF), V((2048, 128), BF),
            V((1024, 2048), F32), V((1024, 128), F32), V((1024, 256), F32), V((128, 1024), BF),
            V((512, 1024), BF), V((512, 1024), BF), V((8, 128, 1024), BF),
            V((2, 4, 128, 512), BF), V((2, 128, 512), BF), V((4, 128, 512), BF), V((4, 128, 512), BF),
            V((4, 128, 512), BF), V((8, 16, 1024), BF), V((8, 16, 1024), BF),
            V((8, 128, 512), BF), V((512, 1024), BF), V((32, 1024), BF), V((16, 32, 1024), BF),
            V((512, 1024), BF), V((1, 1024), F32),
            V((4, 128, 1024), BF), V((4, 128, 1024), BF), V((4, 128, 1024), BF), V((4, 128, 1024), BF),
            V((8, 128, 1024), BF), V((512, 256), F32), V((16, 32, 1024), BF), V((8, 128, 512), BF),
            dma((5,)), dma((2,)), dma((2,)), dma((8,)), dma((16,)), dma((8,)), dma((16,)), dma((8,)), dma((8,)),
            dma((22,)), dma((16,)), dma((8,)), dma((8,)), dma((4,)), dma((4,)), dma((4,)), dma((4,)),
            dma((8,)), dma((8,)), dma((4,)), dma((4,)), dma((1,)), dma((1,)), dma((4,)), dma((4,)),
            dma((8,)), dma((8,)), dma((16,)), dma((16,)), dma((16,)), dma((16,)),
            dma((64,)), dma((64,)), dma((8,)), dma((8,)),
            pltpu.SemaphoreType.REGULAR, pltpu.SemaphoreType.REGULAR,
        ],
        compiler_params=pltpu.CompilerParams(
            collective_id=0, has_side_effects=True, vmem_limit_bytes=60 * 2 ** 20),
        cost_estimate=pl.CostEstimate(flops=9 * 10 ** 9, bytes_accessed=8 * 10 ** 6, transcendentals=9 * 10 ** 6),
    )(queries.reshape(8, 2, 128, 512), keys_values[0], projector, ownership, token_ids.reshape(1, 128),
      student_input, student_weight, student_bias.reshape(1, 8))
    wg, bias, loss, ig = pl.pallas_call(
        finish,
        out_shape=(jax.ShapeDtypeStruct((28, 1024), F32), jax.ShapeDtypeStruct((1, 8), F32),
                   jax.ShapeDtypeStruct((1, 1), F32), jax.ShapeDtypeStruct((128, 3584), BF)),
        in_specs=[hbm, hbm],
        out_specs=(vmem, vmem, vmem, vmem),
        scratch_shapes=[V((16, 32, 1024), BF), V((8, 128, 512), BF), dma((2,))],
        compiler_params=pltpu.CompilerParams(vmem_limit_bytes=60 * 2 ** 20),
    )(wgland, igland)
    return loss.reshape(()), wg, bias.reshape(8), ig


def solution(mesh):
    return jax.shard_map(
        on_device,
        mesh=mesh,
        in_specs=(
            P("grp", None, "tp"), P("grp", "tp", None), P("tp", None), P(), P(("grp", "tp")),
            P(("grp", "tp"), None), P(("grp", "tp"), None), P(("grp", "tp")),
        ),
        out_specs=(P(), P(("grp", "tp"), None), P(("grp", "tp")), P(("grp", "tp"), None)),
        check_vma=False,
    )
```
